32 devices in a mesh: gx: 4 (over y, core), gy: 4 (over z), gz: 2 (over x).
Axes of the slice: x: 2, y: 2, z: 4, core: 2. Of those that a mesh axis runs over, the one named last changes fastest.
Arguments:
- panels: bfloat16 [4, 4, 16, 32, 1024], P(None, None, 'gz', 'gy', 'gx'), may hold values from -6 to 6
- eof_basis: bfloat16 [4, 16, 10], replicated, may hold values from -1.5 to 1.5
- control: float32 [4, 10, 32, 1024], P(None, None, 'gy', ('gx', 'gz')), may hold values from -6 to 6
- coefficients: float32 [4, 32, 1024], P(None, 'gy', ('gx', 'gz')), may hold values from -0.5 to 1.6, as said below
Outputs:
- covariance_image: float32 [4, 10, 32, 1024], P(None, None, 'gy', ('gx', 'gz'))
The draws below stay inside these ranges and needn't reach their ends.
Inputs may be any that keep to these rules, and one draw needn't show every extreme that they name: `coefficients`: kxx and kyy lie in 0.2 to 1, kxy = c sqrt(kxx kyy) with c in -0.5 to 0.5, and the inverse cell area lies in 0.6 to 1.6.
All inputs are finite; a program needn't handle non-finite values.
Results may differ from the reference program's by a relative error of at most 0.00085.
Values may be sent and summed in bfloat16 or wider, within the bound.
No kernel may reach another device: no remote copies, remote signals or barrier semaphores. Data moves between devices by JAX's collectives and lax.ppermute only.
A program may use at most 64 MiB of HBM per device.

```python
import jax
import jax.numpy as jnp
from jax import lax

F = 4
EOF = 10
M = 4
LEV = 16
STEPS = 6
NX = 1024
NY = 32


def draw_coefficients(key, part):
    keys = jax.random.split(key, 4)
    east_coeff = jax.random.uniform(keys[0], (NY, NX), jnp.float32, 0.2, 1.0)
    north_coeff = jax.random.uniform(keys[1], (NY, NX), jnp.float32, 0.2, 1.0)
    tilt = jax.random.uniform(keys[2], (NY, NX), jnp.float32, -0.5, 0.5)
    area_inv = jax.random.uniform(keys[3], (NY, NX), jnp.float32, 0.6, 1.6)
    cross = tilt * jnp.sqrt(east_coeff * north_coeff)
    return jnp.stack([east_coeff, cross, north_coeff, area_inv], axis=0)


def block_levels(rng, extent, pieces, low, high):
    def one(dim, shards_of):
        steps = jax.random.uniform(jax.random.fold_in(jax.random.fold_in(rng, 6), dim), (shards_of,), jnp.float32, low / len(pieces), high / len(pieces))
        return jnp.repeat(jnp.exp(steps), extent[dim] // shards_of).reshape((-1,) + (1,) * (len(extent) - dim - 1))

    loudness = one(*pieces[0])
    for cut in pieces[1:]:
        loudness = loudness * one(*cut)
    return loudness


def bell_draw(rng, extent, width, reach, pieces=(), dtype=jnp.bfloat16):
    entries = jax.random.normal(rng, extent, jnp.float32) * width
    if len(pieces) > 0:
        entries = block_levels(rng, extent, pieces, -0.22, 0.18) * entries
    return jnp.clip(entries, min=-reach, max=reach).astype(dtype)


def setup_inputs(seed: int = 0) -> dict:
    streams_of = jax.random.split(jax.random.key(seed), 5)
    panels = bell_draw(streams_of[0], (M, F, LEV, NY, NX), 1.0, 6.0, ((2, 2), (3, 4), (4, 4)))
    eof_basis = bell_draw(streams_of[1], (F, LEV, EOF), LEV ** -0.5, 1.5)
    control = bell_draw(streams_of[2], (F, EOF, NY, NX), 1.0, 6.0, ((2, 4), (3, 8)), jnp.float32)
    coefficients = draw_coefficients(jax.random.fold_in(streams_of[4], 71), 0)
    return dict(panels=panels, eof_basis=eof_basis, control=control, coefficients=coefficients)


time_step = 0.09

def divergence(padded, coeffs):
    east_diff = padded[:, :-1, 1:] - padded[:, :-1, :-1]
    north_diff = padded[:, 1:, :-1] - padded[:, :-1, :-1]
    flux_east = coeffs[0, :-1, :-1] * east_diff + coeffs[1, :-1, :-1] * north_diff
    flux_north = coeffs[1, :-1, :-1] * east_diff + coeffs[2, :-1, :-1] * north_diff
    return flux_east[:, 1:, 1:] - flux_east[:, 1:, :-1] + (flux_north[:, 1:, 1:] - flux_north[:, :-1, 1:])

def forward_section(padded, coeffs):
    return padded[:, 1:-1, 1:-1] + time_step * coeffs[3, 1:-1, 1:-1] * divergence(padded, coeffs)

def pad_grid(values):
    wrapped = jnp.concatenate([values[:, :, -1:], values, values[:, :, :1]], axis=2)
    return jnp.pad(wrapped, ((0, 0), (1, 1), (0, 0)))

def spread(values, coefficients):
    return forward_section(pad_grid(values), pad_grid(coefficients))

def reference(panels, eof_basis, control, coefficients):
    fields, eof_count, row_count, col_count = control.shape
    flattened = control.reshape(fields * eof_count, row_count, col_count)
    zero_state = jnp.zeros_like(flattened)
    _, backward = jax.vjp(lambda values: spread(values, coefficients), zero_state)
    adjointed = flattened
    for repeat in range(STEPS):
        adjointed = backward(adjointed)[0]
    weights = adjointed.reshape(fields, eof_count, row_count, col_count)
    basis = eof_basis.astype(jnp.float32)

    def member_term(combined, member_panel):
        projected = jnp.einsum('flyx,fle->feyx', member_panel.astype(jnp.float32), basis, precision=lax.Precision.HIGHEST)
        scores = lax.optimization_barrier(jnp.sum(projected * weights, axis=(0, 1)))
        return (combined + projected * scores, None)
    combined, _ = lax.scan(member_term, jnp.zeros(weights.shape, jnp.float32), panels)
    combined = combined / (M - 1)
    values = combined.reshape(fields * eof_count, row_count, col_count)
    for repeat in range(STEPS):
        values = spread(values, coefficients)
    return values.reshape(fields, eof_count, row_count, col_count)
```

```python
import functools

import jax
import jax.numpy as jnp
from jax import lax
from jax.experimental import pallas as pl
from jax.experimental.pallas import tpu as pltpu
from jax.sharding import PartitionSpec as P

STEPS = 6
LANES = 128
SUB = 8
RING = ("gx", "gz")

time_step = 0.09

WINDOW = SUB + 2 * STEPS
HALO = 2 * STEPS
SLOT = 32


def turn(cells, shift):
    return pltpu.roll(cells, shift % LANES, 1)


def swap_a(values, axes):
    count = lax.axis_size(axes)
    return lax.ppermute(values, axes, [(i, i ^ 1) for i in range(count)])


def swap_b(values, axes, closed):
    count = lax.axis_size(axes)
    pairs = [(i, i + 1) for i in range(1, count - 1, 2)]
    if closed:
        pairs.append((count - 1, 0))
    return lax.ppermute(values, axes, pairs + [(j, i) for i, j in pairs])


def place(w):
    return (w + 2) // SUB, (w + 2) % SUB


def lane_grid():
    return lax.broadcasted_iota(jnp.int32, (SUB, LANES), 1)


def diffuse(rows, coeff, adjoint):
    for step in range(STEPS):
        low, high = step, WINDOW - 1 - step
        moved = {}
        if adjoint:
            seen = {w: coeff(3, w) * rows[w] for w in range(low, high + 1)}
        else:
            seen = rows
        south = None
        for w in range(low, high):
            east_diff = turn(seen[w], -1) - seen[w]
            north_diff = seen[w + 1] - seen[w]
            cross = coeff(1, w)
            flux_north = cross * east_diff + coeff(2, w) * north_diff
            if w > low:
                flux_east = coeff(0, w) * east_diff + cross * north_diff
                div = flux_east - turn(flux_east, 1) + (flux_north - south)
                moved[w] = rows[w] + (div if adjoint else coeff(3, w) * div)
            south = flux_north
        rows = moved
    return rows


def tile_picker(own, from_a, from_b, odd):
    def tile(t, index):
        at = pl.ds(index * SUB, SUB)
        if t == 1:
            return own[at, :]
        first, second = (from_a, from_b) if t == 0 else (from_b, from_a)
        return jnp.where(odd, first[at, :], second[at, :])

    return tile


def row_picker(own, from_a, from_b, odd):
    def row(w, group):
        t, y = place(w)
        at = pl.ds(group * SUB * SUB + y, SUB, stride=SUB)
        if t == 1:
            return own[at, :]
        first, second = (from_a, from_b) if t == 0 else (from_b, from_a)
        return jnp.where(odd, first[at, :], second[at, :])

    return row


def pack_kernel(
    fields, eofs, members, place_ref, own, from_a, from_b, panel, *rest
):
    arrived, (out_a, out_b) = rest[:-2], rest[-2:]
    ring_odd, odd, me = place_ref[0] == 1, place_ref[1] == 1, place_ref[2]
    tile = tile_picker(own, from_a, from_b, odd)
    lane = lane_grid()
    pair = eofs // 2
    zero = jnp.zeros((SUB, LANES), jnp.float32)

    def put(at, west, east):
        out_a[at, :] = jnp.where(ring_odd, west, east)
        out_b[at, :] = jnp.where(ring_odd, east, west)

    for t in range(3):
        for j in range(pair):
            west, east = zero, zero
            for half in range(2):
                for f in range(fields):
                    cells = tile(t, f * eofs + half * pair + j)
                    start = f * SLOT + half * (SLOT // 2)
                    mask = (lane >= start) & (lane < start + HALO)
                    west = jnp.where(mask, turn(cells, start), west)
                    east = jnp.where(mask, turn(cells, start + HALO - LANES), east)
            put(pl.ds((t * pair + j) * SUB, SUB), west, east)
        west, east = zero, zero
        for k in range(4):
            cells = tile(t, fields * eofs + k)
            start = k * SLOT
            mask = (lane >= start) & (lane < start + HALO)
            west = jnp.where(mask, turn(cells, start), west)
            east = jnp.where(mask, turn(cells, start + HALO - LANES), east)
        put(pl.ds((3 * pair + t) * SUB, SUB), west, east)

    base = 3 * (pair + 1) * SUB
    depth = panel.shape[2] * SUB
    column = lax.broadcasted_iota(jnp.int32, (LANES, 2 * LANES), 0)
    target = lax.broadcasted_iota(jnp.int32, (LANES, 2 * LANES), 1)
    west_ok = (target < LANES) & (column < STEPS)
    east_ok = (target >= LANES) & (column >= LANES - STEPS)
    offset = jnp.where(
        west_ok,
        target - column,
        jnp.where(east_ok, target - LANES - column + LANES - STEPS, -1),
    )
    blocks = (panel,) + arrived
    count = len(blocks)
    for s, block in enumerate(blocks):
        total = jnp.zeros((depth, 2 * LANES), jnp.float32)
        for m in range(members):
            for f in range(fields):
                pick = (offset == f * SLOT + m * SUB).astype(jnp.bfloat16)
                total += jnp.dot(
                    block[m, f].reshape(depth, LANES), pick, preferred_element_type=jnp.float32
                )
        start = pl.multiple_of(base + lax.rem(me - s + count, count) * depth, SUB)
        put(pl.ds(start, depth), total[:, :LANES], total[:, LANES:])


def main_kernel(
    fields, eofs, members, place_ref, own, from_a, from_b, basis, panel, *rest
):
    arrived, (adj, proj, strip, coeff_main, coeff_strip, wide) = rest[:-6], rest[-6:]
    odd, me = place_ref[1] == 1, place_ref[2]
    tile = tile_picker(own, from_a, from_b, odd)
    row = row_picker(own, from_a, from_b, odd)
    lane = lane_grid()
    inner = lane & (SLOT - 1)
    shifted = (lane + STEPS) & (LANES - 1)
    zero = jnp.zeros((SUB, LANES), jnp.float32)

    blocks = (panel,) + arrived
    count = len(blocks)
    depth = panel.shape[2] * SUB
    for f in range(fields):
        total = None
        for s, block in enumerate(blocks):
            cells = jnp.concatenate(
                [block[m, f].reshape(depth, LANES) for m in range(members)], axis=1
            )
            part = jnp.dot(
                basis[lax.rem(me - s + count, count), f], cells, preferred_element_type=jnp.float32
            )
            total = part if total is None else total + part
        for m in range(members):
            proj[m, pl.ds(f * eofs * SUB, eofs * SUB), :] = total[:, m * LANES : (m + 1) * LANES]

    for k in range(4):
        for t in range(3):
            cells = tile(t, fields * eofs + k)
            if k < 3:
                cells = time_step * cells
            at = pl.ds(t * SUB, SUB)
            coeff_main[k, at, :] = cells
            west, east = zero, zero
            for f in range(fields):
                start = f * SLOT
                west = jnp.where(lane // SLOT == f, turn(cells, start + HALO), west)
                east = jnp.where(shifted // SLOT == f, turn(cells, start - STEPS - LANES + HALO), east)
            coeff_strip[0, k, at, :] = jnp.where((inner >= HALO) & (inner < 2 * HALO), west, 0.0)
            coeff_strip[1, k, at, :] = jnp.where((shifted & (SLOT - 1)) < HALO, east, 0.0)
        for w in range(WINDOW):
            wide[k, w] = jnp.broadcast_to(coeff_main[k, pl.ds(w + 2, 1), :], (SUB, LANES))

    def group(g, carry):
        rows = {w: row(w, g) for w in range(WINDOW)}
        rows = diffuse(rows, lambda k, w: wide[k, w], True)
        for y in range(SUB):
            adj[pl.ds(g * SUB * SUB + y, SUB, stride=SUB), :] = rows[y + STEPS]
        return carry

    lax.fori_loop(0, fields * eofs // SUB, group, 0)

    for t in range(3):
        for e in range(eofs):
            west, east = zero, zero
            for f in range(fields):
                cells = tile(t, f * eofs + e)
                west = jnp.where(lane // SLOT == f, turn(cells, f * SLOT + HALO), west)
                east = jnp.where(
                    shifted // SLOT == f, turn(cells, f * SLOT - STEPS - LANES + HALO), east
                )
            strip[t, pl.ds(e * SUB, SUB), :] = west
            strip[t, pl.ds((eofs + e) * SUB, SUB), :] = east
        strip[t, pl.ds(2 * eofs * SUB, 4 * SUB), :] = jnp.zeros((4 * SUB, LANES), jnp.float32)


def strip_coefficients(coeff_strip, wide_strip, eofs):
    sub = lax.broadcasted_iota(jnp.int32, (SUB, LANES), 0)
    for k in range(4):
        for w in range(WINDOW):
            west = jnp.broadcast_to(coeff_strip[0, k, pl.ds(w + 2, 1), :], (SUB, LANES))
            east = jnp.broadcast_to(coeff_strip[1, k, pl.ds(w + 2, 1), :], (SUB, LANES))
            wide_strip[k, w, pl.ds(0, SUB), :] = west
            wide_strip[k, w, pl.ds(SUB, SUB), :] = jnp.where(sub < eofs - SUB, west, east)
            wide_strip[k, w, pl.ds(2 * SUB, SUB), :] = east


def combine_kernel(
    fields, eofs, members, place_ref, got_a, got_b, basis, adj, proj, strip_own, coeff_own,
    combined, coeff_strip, strip, wide_strip, adj_strip, panel_in, proj_strip,
):
    ring_odd = place_ref[0] == 1
    lane = lane_grid()
    inner = lane & (SLOT - 1)
    pair = eofs // 2

    def got(at):
        first, second = got_a[at, :], got_b[at, :]
        return jnp.where(ring_odd, first, second), jnp.where(ring_odd, second, first)

    west_mask = inner < HALO
    east_mask = (inner >= STEPS) & (inner < STEPS + HALO)
    for t in range(3):
        for j in range(pair):
            west, east = got(pl.ds((t * pair + j) * SUB, SUB))
            for half in range(2):
                e = half * pair + j
                at = pl.ds(e * SUB, SUB)
                strip[t, at, :] = jnp.where(
                    west_mask, turn(west, -half * (SLOT // 2)), strip_own[t, at, :]
                )
                at = pl.ds((eofs + e) * SUB, SUB)
                strip[t, at, :] = jnp.where(
                    east_mask, turn(east, STEPS - half * (SLOT // 2)), strip_own[t, at, :]
                )
        at = pl.ds(2 * eofs * SUB, 4 * SUB)
        strip[t, at, :] = strip_own[t, at, :]
        west, east = got(pl.ds((3 * pair + t) * SUB, SUB))
        at = pl.ds(t * SUB, SUB)
        for k in range(4):
            for side, (cells, mask, shift) in enumerate(
                ((west, west_mask, 0), (east, east_mask, STEPS))
            ):
                mine = jnp.where(lane // SLOT == k, cells, 0.0)
                mine = mine + turn(mine, SLOT)
                mine = mine + turn(mine, 2 * SLOT)
                if shift:
                    mine = turn(mine, shift)
                if k < 3:
                    mine = time_step * mine
                coeff_strip[side, k, at, :] = jnp.where(mask, mine, coeff_own[side, k, at, :])
    strip_coefficients(coeff_strip, wide_strip, eofs)

    for g in range(3):
        rows = {}
        for w in range(WINDOW):
            t, y = place(w)
            rows[w] = strip[t, pl.ds(g * SUB * SUB + y, SUB, stride=SUB), :]
        rows = diffuse(rows, lambda k, w: wide_strip[k, w, pl.ds(g * SUB, SUB), :], True)
        for y in range(SUB):
            adj_strip[pl.ds(g * SUB * SUB + y, SUB, stride=SUB), :] = rows[y + STEPS]

    base = 3 * (pair + 1) * SUB
    levels = got_a.shape[0] - base
    west, east = got(pl.ds(base, levels))
    panel_in[...] = jnp.concatenate([west, east], axis=1).astype(jnp.bfloat16)
    count, depth = basis.shape[0], basis.shape[3]
    wide_lane = lax.broadcasted_iota(jnp.int32, (eofs * SUB, 2 * LANES), 1) & (LANES - 1)
    halo = jnp.zeros((eofs * SUB, 2 * LANES), jnp.float32)
    for f in range(fields):
        total = None
        for h in range(count):
            part = jnp.dot(
                basis[h, f], panel_in[pl.ds(h * depth, depth), :], preferred_element_type=jnp.float32
            )
            total = part if total is None else total + part
        halo = jnp.where(wide_lane // SLOT == f, total, halo)
    proj_strip[pl.ds(0, eofs * SUB), :] = halo[:, :LANES]
    proj_strip[pl.ds(eofs * SUB, eofs * SUB), :] = halo[:, LANES:]

    scores = [jnp.zeros((SUB, LANES), jnp.float32) for _ in range(members)]
    for f in range(fields):
        for e in range(eofs):
            at = pl.ds((f * eofs + e) * SUB, SUB)
            west = turn(adj_strip[pl.ds(e * SUB, SUB), :], -f * SLOT - HALO)
            east = turn(adj_strip[pl.ds((eofs + e) * SUB, SUB), :], LANES - STEPS - f * SLOT)
            cells = jnp.where(
                lane < STEPS, west, jnp.where(lane >= LANES - STEPS, east, adj[at, :])
            )
            for m in range(members):
                scores[m] = scores[m] + proj[m, at, :] * cells
    scores = [s / (members - 1) for s in scores]
    for i in range(fields * eofs):
        at = pl.ds(i * SUB, SUB)
        total = proj[0, at, :] * scores[0]
        for m in range(1, members):
            total = total + proj[m, at, :] * scores[m]
        combined[at, :] = total

    slot = inner // SUB
    packed = [jnp.zeros((SUB, LANES), jnp.float32) for _ in range(2 * eofs // 4)]
    for side in range(2):
        total = jnp.zeros((SUB, LANES), jnp.float32)
        for e in range(eofs):
            at = pl.ds((side * eofs + e) * SUB, SUB)
            cells = adj_strip[at, :]
            spread = turn(cells, -STEPS)
            for m in range(1, members):
                spread = jnp.where(slot == m, turn(cells, m * SUB - STEPS), spread)
            total = total + proj_strip[at, :] * spread
        total = total + turn(total, SLOT)
        total = (total + turn(total, 2 * SLOT)) / (members - 1)
        for e in range(eofs):
            i = side * eofs + e
            cells = proj_strip[pl.ds(i * SUB, SUB), :] * total
            cells = cells + turn(cells, -2 * SUB)
            cells = cells + turn(cells, -SUB)
            packed[i // 4] = jnp.where(slot == i % 4, turn(cells, (i % 4) * SUB), packed[i // 4])
    for j in range(len(packed)):
        combined[pl.ds((fields * eofs + j) * SUB, SUB), :] = packed[j]


def forward_kernel(
    fields, eofs, place_ref, own, from_a, from_b, coeff_main, coeff_strip,
    out, strip, strip_out, wide, wide_strip,
):
    odd = place_ref[1] == 1
    tile = tile_picker(own, from_a, from_b, odd)
    row = row_picker(own, from_a, from_b, odd)
    lane = lane_grid()
    inner = lane & (SLOT - 1)
    shifted = (lane + STEPS) & (LANES - 1)
    zero = jnp.zeros((SUB, LANES), jnp.float32)
    halo = (inner >= STEPS) & (inner < HALO)

    for k in range(4):
        for w in range(WINDOW):
            wide[k, w] = jnp.broadcast_to(coeff_main[k, pl.ds(w + 2, 1), :], (SUB, LANES))
    strip_coefficients(coeff_strip, wide_strip, eofs)

    for t in range(3):
        for e in range(eofs):
            west, east = zero, zero
            for f in range(fields):
                cells = tile(t, f * eofs + e)
                west = jnp.where(lane // SLOT == f, turn(cells, f * SLOT + HALO), west)
                east = jnp.where(
                    shifted // SLOT == f, turn(cells, f * SLOT - STEPS - LANES + HALO), east
                )
            for side, cells in enumerate((west, east)):
                i = side * eofs + e
                beyond = turn(tile(t, fields * eofs + i // 4), STEPS - (i % 4) * SUB)
                strip[t, pl.ds(i * SUB, SUB), :] = jnp.where(halo, beyond, cells)
        strip[t, pl.ds(2 * eofs * SUB, 4 * SUB), :] = jnp.zeros((4 * SUB, LANES), jnp.float32)

    for g in range(3):
        rows = {}
        for w in range(WINDOW):
            t, y = place(w)
            rows[w] = strip[t, pl.ds(g * SUB * SUB + y, SUB, stride=SUB), :]
        rows = diffuse(rows, lambda k, w: wide_strip[k, w, pl.ds(g * SUB, SUB), :], False)
        for y in range(SUB):
            strip_out[pl.ds(g * SUB * SUB + y, SUB, stride=SUB), :] = rows[y + STEPS]

    def group(g, carry):
        rows = {w: row(w, g) for w in range(WINDOW)}
        rows = diffuse(rows, lambda k, w: wide[k, w], False)
        for y in range(SUB):
            out[pl.ds(g * SUB * SUB + y, SUB, stride=SUB), :] = rows[y + STEPS]
        return carry

    lax.fori_loop(0, fields * eofs // SUB, group, 0)
    for f in range(fields):
        for e in range(eofs):
            at = pl.ds((f * eofs + e) * SUB, SUB)
            west = turn(strip_out[pl.ds(e * SUB, SUB), :], -f * SLOT - HALO)
            east = turn(strip_out[pl.ds((eofs + e) * SUB, SUB), :], LANES - STEPS - f * SLOT)
            out[at, :] = jnp.where(
                lane < STEPS, west, jnp.where(lane >= LANES - STEPS, east, out[at, :])
            )


def call(kernel, args, outs, scratch=(), flops=1_000_000):
    whole = pl.BlockSpec(memory_space=pltpu.VMEM)
    moved = sum(a.size * a.dtype.itemsize for a in list(args) + list(outs))
    return pl.pallas_call(
        kernel,
        in_specs=[pl.BlockSpec(memory_space=pltpu.SMEM)] + [whole] * (len(args) - 1),
        out_specs=[whole] * len(outs),
        out_shape=list(outs),
        scratch_shapes=list(scratch),
        compiler_params=pltpu.CompilerParams(vmem_limit_bytes=32 * 2**20),
        cost_estimate=pl.CostEstimate(flops=flops, bytes_accessed=moved, transcendentals=0),
    )(*args)


def per_device(panels, eof_basis, control, coefficients):
    members, fields, depth, row_count, _ = panels.shape
    _, eofs, _, col_count = control.shape
    count = lax.axis_size("gz")
    me = lax.axis_index("gz")
    ring = lax.axis_index("gx") * count + me
    where_am_i = jnp.stack([ring % 2, lax.axis_index("gy") % 2, me]).astype(jnp.int32)

    def columns(of):
        return lax.dynamic_slice_in_dim(panels, of * col_count, col_count, axis=4)

    arrived = [
        lax.ppermute(
            columns((me + s) % count), "gz", [(i, (i + s) % count) for i in range(count)]
        )
        for s in range(1, count)
    ]
    panel = columns(me)
    total_fields = fields * eofs
    own = jnp.concatenate(
        [
            control.reshape(total_fields * row_count, col_count),
            coefficients.reshape(4 * row_count, col_count),
        ]
    )
    from_a, from_b = swap_a(own, "gy"), swap_b(own, "gy", False)

    basis = eof_basis.transpose(0, 2, 1).reshape(fields, eofs, 1, count, depth, 1)
    basis = basis * jnp.eye(row_count, dtype=eof_basis.dtype)[:, None, None, :]
    basis = basis.transpose(3, 0, 1, 2, 4, 5).reshape(
        count, fields, eofs * row_count, depth * row_count
    )

    f32 = lambda *shape: jax.ShapeDtypeStruct(shape, jnp.float32)
    rows_sent = 3 * (eofs // 2 + 1) * row_count + count * depth * row_count
    sent_a, sent_b = call(
        functools.partial(pack_kernel, fields, eofs, members),
        [where_am_i, own, from_a, from_b, panel, *arrived],
        [f32(rows_sent, col_count)] * 2,
    )
    got_a, got_b = swap_a(sent_a, RING), swap_b(sent_b, RING, True)

    strip_rows = (2 * eofs + 4) * row_count
    adj, proj, strip, coeff_main, coeff_strip = call(
        functools.partial(main_kernel, fields, eofs, members),
        [where_am_i, own, from_a, from_b, basis, panel, *arrived],
        [
            f32(total_fields * row_count, col_count),
            f32(members, total_fields * row_count, col_count),
            f32(3, strip_rows, col_count),
            f32(4, 3 * row_count, col_count),
            f32(2, 4, 3 * row_count, col_count),
        ],
        [pltpu.VMEM((4, WINDOW, SUB, LANES), jnp.float32)],
        flops=20_000_000,
    )
    combined, coeff_strip = call(
        functools.partial(combine_kernel, fields, eofs, members),
        [where_am_i, got_a, got_b, basis, adj, proj, strip, coeff_strip],
        [
            f32(total_fields * row_count + 2 * eofs // 4 * row_count, col_count),
            f32(2, 4, 3 * row_count, col_count),
        ],
        [
            pltpu.VMEM((3, strip_rows, LANES), jnp.float32),
            pltpu.VMEM((4, WINDOW, 3 * SUB, LANES), jnp.float32),
            pltpu.VMEM((strip_rows, LANES), jnp.float32),
            pltpu.VMEM((count * depth * row_count, 2 * LANES), jnp.bfloat16),
            pltpu.VMEM((strip_rows, LANES), jnp.float32),
        ],
    )
    from_a, from_b = swap_a(combined, "gy"), swap_b(combined, "gy", False)
    (result,) = call(
        functools.partial(forward_kernel, fields, eofs),
        [where_am_i, combined, from_a, from_b, coeff_main, coeff_strip],
        [f32(total_fields * row_count, col_count)],
        [
            pltpu.VMEM((3, strip_rows, LANES), jnp.float32),
            pltpu.VMEM((strip_rows, LANES), jnp.float32),
            pltpu.VMEM((4, WINDOW, SUB, LANES), jnp.float32),
            pltpu.VMEM((4, WINDOW, 3 * SUB, LANES), jnp.float32),
        ],
    )
    return result.reshape(control.shape)


def solution(mesh):
    in_specs = (
        P(None, None, "gz", "gy", "gx"),
        P(),
        P(None, None, "gy", ("gx", "gz")),
        P(None, "gy", ("gx", "gz")),
    )
    out_specs = P(None, None, "gy", ("gx", "gz"))
    return jax.shard_map(
        per_device, mesh=mesh, in_specs=in_specs, out_specs=out_specs, check_vma=False
    )
```

```python
import functools

import jax
import jax.numpy as jnp
from jax import lax
from jax.experimental import pallas as pl
from jax.experimental.pallas import tpu as pltpu
from jax.sharding import PartitionSpec as P

STEPS = 6
LANES = 128
SUB = 8
RING = ("gx", "gz")

time_step = 0.09

WINDOW = SUB + 2 * STEPS
HALO = 2 * STEPS
SLOT = 32


def turn(cells, shift):
    return pltpu.roll(cells, shift % LANES, 1)


def swap_a(values, axes):
    count = lax.axis_size(axes)
    return lax.ppermute(values, axes, [(i, i ^ 1) for i in range(count)])


def swap_b(values, axes, closed):
    count = lax.axis_size(axes)
    pairs = [(i, i + 1) for i in range(1, count - 1, 2)]
    if closed:
        pairs.append((count - 1, 0))
    return lax.ppermute(values, axes, pairs + [(j, i) for i, j in pairs])


def place(w):
    return (w + 2) // SUB, (w + 2) % SUB


def lane_grid():
    return lax.broadcasted_iota(jnp.int32, (SUB, LANES), 1)


def diffuse(read, write, coeff, groups, first, second, adjoint):
    state, spare = None, first
    for step in range(STEPS):
        low, high = step, WINDOW - 1 - step

        def fetch(w):
            if state is None:
                return [read(w, g) for g in range(groups)]
            return [state[w, pl.ds(g * SUB, SUB), :] for g in range(groups)]

        here, seen, south = fetch(low), None, None
        for w in range(low, high):
            k = [coeff(i, w) for i in range(4)]
            north = fetch(w + 1)
            if adjoint:
                if seen is None:
                    seen = [k[3][g] * here[g] for g in range(groups)]
                area = coeff(3, w + 1)
                seen_north = [area[g] * north[g] for g in range(groups)]
            else:
                seen, seen_north = here, north
            flux = []
            for g in range(groups):
                east_diff = turn(seen[g], -1) - seen[g]
                north_diff = seen_north[g] - seen[g]
                flux.append(k[1][g] * east_diff + k[2][g] * north_diff)
                if w > low:
                    flux_east = k[0][g] * east_diff + k[1][g] * north_diff
                    div = flux_east - turn(flux_east, 1) + (flux[g] - south[g])
                    moved = here[g] + (div if adjoint else k[3][g] * div)
                    if step == STEPS - 1:
                        write(w, g, moved)
                    else:
                        spare[w, pl.ds(g * SUB, SUB), :] = moved
            here, seen, south = north, seen_north, flux
        state, spare = spare, (second if spare is first else first)


def tile_picker(own, from_a, from_b, odd):
    def tile(t, index):
        at = pl.ds(index * SUB, SUB)
        if t == 1:
            return own[at, :]
        first, second = (from_a, from_b) if t == 0 else (from_b, from_a)
        return jnp.where(odd, first[at, :], second[at, :])

    return tile


def row_picker(own, from_a, from_b, odd):
    def row(w, group):
        t, y = place(w)
        at = pl.ds(group * SUB * SUB + y, SUB, stride=SUB)
        if t == 1:
            return own[at, :]
        first, second = (from_a, from_b) if t == 0 else (from_b, from_a)
        return jnp.where(odd, first[at, :], second[at, :])

    return row


def pack_kernel(
    fields, eofs, members, place_ref, own, from_a, from_b, panel, *rest
):
    arrived, (out_a, out_b) = rest[:-2], rest[-2:]
    ring_odd, odd, me = place_ref[0] == 1, place_ref[1] == 1, place_ref[2]
    tile = tile_picker(own, from_a, from_b, odd)
    lane = lane_grid()
    pair = eofs // 2
    zero = jnp.zeros((SUB, LANES), jnp.float32)

    def put(at, west, east):
        out_a[at, :] = jnp.where(ring_odd, west, east)
        out_b[at, :] = jnp.where(ring_odd, east, west)

    for t in range(3):
        for j in range(pair):
            west, east = zero, zero
            for half in range(2):
                for f in range(fields):
                    cells = tile(t, f * eofs + half * pair + j)
                    start = f * SLOT + half * (SLOT // 2)
                    mask = (lane >= start) & (lane < start + HALO)
                    west = jnp.where(mask, turn(cells, start), west)
                    east = jnp.where(mask, turn(cells, start + HALO - LANES), east)
            put(pl.ds((t * pair + j) * SUB, SUB), west, east)
        west, east = zero, zero
        for k in range(4):
            cells = tile(t, fields * eofs + k)
            start = k * SLOT
            mask = (lane >= start) & (lane < start + HALO)
            west = jnp.where(mask, turn(cells, start), west)
            east = jnp.where(mask, turn(cells, start + HALO - LANES), east)
        put(pl.ds((3 * pair + t) * SUB, SUB), west, east)

    base = 3 * (pair + 1) * SUB
    depth = panel.shape[2] * SUB
    column = lax.broadcasted_iota(jnp.int32, (LANES, 2 * LANES), 0)
    target = lax.broadcasted_iota(jnp.int32, (LANES, 2 * LANES), 1)
    west_ok = (target < LANES) & (column < STEPS)
    east_ok = (target >= LANES) & (column >= LANES - STEPS)
    offset = jnp.where(
        west_ok,
        target - column,
        jnp.where(east_ok, target - LANES - column + LANES - STEPS, -1),
    )
    blocks = (panel,) + arrived
    count = len(blocks)
    for s, block in enumerate(blocks):
        total = jnp.zeros((depth, 2 * LANES), jnp.float32)
        for m in range(members):
            for f in range(fields):
                pick = (offset == f * SLOT + m * SUB).astype(jnp.bfloat16)
                total += jnp.dot(
                    block[m, f].reshape(depth, LANES), pick, preferred_element_type=jnp.float32
                )
        start = pl.multiple_of(base + lax.rem(me - s + count, count) * depth, SUB)
        put(pl.ds(start, depth), total[:, :LANES], total[:, LANES:])


def main_kernel(
    fields, eofs, members, place_ref, own, from_a, from_b, basis, panel, *rest
):
    arrived = rest[:-8]
    adj, proj, strip, coeff_main, coeff_strip, wide, first, second = rest[-8:]
    odd, me = place_ref[1] == 1, place_ref[2]
    tile = tile_picker(own, from_a, from_b, odd)
    row = row_picker(own, from_a, from_b, odd)
    lane = lane_grid()
    inner = lane & (SLOT - 1)
    shifted = (lane + STEPS) & (LANES - 1)
    zero = jnp.zeros((SUB, LANES), jnp.float32)

    blocks = (panel,) + arrived
    count = len(blocks)
    depth = panel.shape[2] * SUB
    for f in range(fields):
        total = None
        for s, block in enumerate(blocks):
            cells = jnp.concatenate(
                [block[m, f].reshape(depth, LANES) for m in range(members)], axis=1
            )
            part = jnp.dot(
                basis[lax.rem(me - s + count, count), f], cells, preferred_element_type=jnp.float32
            )
            total = part if total is None else total + part
        for m in range(members):
            proj[m, pl.ds(f * eofs * SUB, eofs * SUB), :] = total[:, m * LANES : (m + 1) * LANES]

    for k in range(4):
        for t in range(3):
            cells = tile(t, fields * eofs + k)
            if k < 3:
                cells = time_step * cells
            at = pl.ds(t * SUB, SUB)
            coeff_main[k, at, :] = cells
            west, east = zero, zero
            for f in range(fields):
                start = f * SLOT
                west = jnp.where(lane // SLOT == f, turn(cells, start + HALO), west)
                east = jnp.where(shifted // SLOT == f, turn(cells, start - STEPS - LANES + HALO), east)
            coeff_strip[0, k, at, :] = jnp.where((inner >= HALO) & (inner < 2 * HALO), west, 0.0)
            coeff_strip[1, k, at, :] = jnp.where((shifted & (SLOT - 1)) < HALO, east, 0.0)
        for w in range(WINDOW):
            wide[k, w] = jnp.broadcast_to(coeff_main[k, pl.ds(w + 2, 1), :], (SUB, LANES))

    groups = fields * eofs // SUB

    def write(w, g, cells):
        adj[pl.ds(g * SUB * SUB + w - STEPS, SUB, stride=SUB), :] = cells

    diffuse(row, write, lambda k, w: [wide[k, w]] * groups, groups, first, second, True)

    for t in range(3):
        for e in range(eofs):
            west, east = zero, zero
            for f in range(fields):
                cells = tile(t, f * eofs + e)
                west = jnp.where(lane // SLOT == f, turn(cells, f * SLOT + HALO), west)
                east = jnp.where(
                    shifted // SLOT == f, turn(cells, f * SLOT - STEPS - LANES + HALO), east
                )
            strip[t, pl.ds(e * SUB, SUB), :] = west
            strip[t, pl.ds((eofs + e) * SUB, SUB), :] = east
        strip[t, pl.ds(2 * eofs * SUB, 4 * SUB), :] = jnp.zeros((4 * SUB, LANES), jnp.float32)


def strip_coefficients(coeff_strip, wide_strip, eofs):
    sub = lax.broadcasted_iota(jnp.int32, (SUB, LANES), 0)
    for k in range(4):
        for w in range(WINDOW):
            west = jnp.broadcast_to(coeff_strip[0, k, pl.ds(w + 2, 1), :], (SUB, LANES))
            east = jnp.broadcast_to(coeff_strip[1, k, pl.ds(w + 2, 1), :], (SUB, LANES))
            wide_strip[k, w, pl.ds(0, SUB), :] = west
            wide_strip[k, w, pl.ds(SUB, SUB), :] = jnp.where(sub < eofs - SUB, west, east)
            wide_strip[k, w, pl.ds(2 * SUB, SUB), :] = east


def diffuse_strip(strip, out, wide_strip, first, second, adjoint):
    def read(w, g):
        t, y = place(w)
        return strip[t, pl.ds(g * SUB * SUB + y, SUB, stride=SUB), :]

    def write(w, g, cells):
        out[pl.ds(g * SUB * SUB + w - STEPS, SUB, stride=SUB), :] = cells

    def coeff(k, w):
        return [wide_strip[k, w, pl.ds(g * SUB, SUB), :] for g in range(3)]

    diffuse(read, write, coeff, 3, first, second, adjoint)


def combine_kernel(
    fields, eofs, members, place_ref, got_a, got_b, basis, adj, proj, strip_own, coeff_own,
    combined, coeff_strip, strip, wide_strip, adj_strip, panel_in, proj_strip, first, second,
):
    ring_odd = place_ref[0] == 1
    lane = lane_grid()
    inner = lane & (SLOT - 1)
    pair = eofs // 2

    def got(at):
        first, second = got_a[at, :], got_b[at, :]
        return jnp.where(ring_odd, first, second), jnp.where(ring_odd, second, first)

    west_mask = inner < HALO
    east_mask = (inner >= STEPS) & (inner < STEPS + HALO)
    for t in range(3):
        for j in range(pair):
            west, east = got(pl.ds((t * pair + j) * SUB, SUB))
            for half in range(2):
                e = half * pair + j
                at = pl.ds(e * SUB, SUB)
                strip[t, at, :] = jnp.where(
                    west_mask, turn(west, -half * (SLOT // 2)), strip_own[t, at, :]
                )
                at = pl.ds((eofs + e) * SUB, SUB)
                strip[t, at, :] = jnp.where(
                    east_mask, turn(east, STEPS - half * (SLOT // 2)), strip_own[t, at, :]
                )
        at = pl.ds(2 * eofs * SUB, 4 * SUB)
        strip[t, at, :] = strip_own[t, at, :]
        west, east = got(pl.ds((3 * pair + t) * SUB, SUB))
        at = pl.ds(t * SUB, SUB)
        for k in range(4):
            for side, (cells, mask, shift) in enumerate(
                ((west, west_mask, 0), (east, east_mask, STEPS))
            ):
                mine = jnp.where(lane // SLOT == k, cells, 0.0)
                mine = mine + turn(mine, SLOT)
                mine = mine + turn(mine, 2 * SLOT)
                if shift:
                    mine = turn(mine, shift)
                if k < 3:
                    mine = time_step * mine
                coeff_strip[side, k, at, :] = jnp.where(mask, mine, coeff_own[side, k, at, :])
    strip_coefficients(coeff_strip, wide_strip, eofs)

    diffuse_strip(strip, adj_strip, wide_strip, first, second, True)

    base = 3 * (pair + 1) * SUB
    levels = got_a.shape[0] - base
    west, east = got(pl.ds(base, levels))
    panel_in[...] = jnp.concatenate([west, east], axis=1).astype(jnp.bfloat16)
    count, depth = basis.shape[0], basis.shape[3]
    wide_lane = lax.broadcasted_iota(jnp.int32, (eofs * SUB, 2 * LANES), 1) & (LANES - 1)
    halo = jnp.zeros((eofs * SUB, 2 * LANES), jnp.float32)
    for f in range(fields):
        total = None
        for h in range(count):
            part = jnp.dot(
                basis[h, f], panel_in[pl.ds(h * depth, depth), :], preferred_element_type=jnp.float32
            )
            total = part if total is None else total + part
        halo = jnp.where(wide_lane // SLOT == f, total, halo)
    proj_strip[pl.ds(0, eofs * SUB), :] = halo[:, :LANES]
    proj_strip[pl.ds(eofs * SUB, eofs * SUB), :] = halo[:, LANES:]

    scores = [jnp.zeros((SUB, LANES), jnp.float32) for _ in range(members)]
    for f in range(fields):
        for e in range(eofs):
            at = pl.ds((f * eofs + e) * SUB, SUB)
            west = turn(adj_strip[pl.ds(e * SUB, SUB), :], -f * SLOT - HALO)
            east = turn(adj_strip[pl.ds((eofs + e) * SUB, SUB), :], LANES - STEPS - f * SLOT)
            cells = jnp.where(
                lane < STEPS, west, jnp.where(lane >= LANES - STEPS, east, adj[at, :])
            )
            for m in range(members):
                scores[m] = scores[m] + proj[m, at, :] * cells
    scores = [s / (members - 1) for s in scores]
    for i in range(fields * eofs):
        at = pl.ds(i * SUB, SUB)
        total = proj[0, at, :] * scores[0]
        for m in range(1, members):
            total = total + proj[m, at, :] * scores[m]
        combined[at, :] = total

    slot = inner // SUB
    packed = [jnp.zeros((SUB, LANES), jnp.float32) for _ in range(2 * eofs // 4)]
    for side in range(2):
        total = jnp.zeros((SUB, LANES), jnp.float32)
        for e in range(eofs):
            at = pl.ds((side * eofs + e) * SUB, SUB)
            cells = adj_strip[at, :]
            spread = turn(cells, -STEPS)
            for m in range(1, members):
                spread = jnp.where(slot == m, turn(cells, m * SUB - STEPS), spread)
            total = total + proj_strip[at, :] * spread
        total = total + turn(total, SLOT)
        total = (total + turn(total, 2 * SLOT)) / (members - 1)
        for e in range(eofs):
            i = side * eofs + e
            cells = proj_strip[pl.ds(i * SUB, SUB), :] * total
            cells = cells + turn(cells, -2 * SUB)
            cells = cells + turn(cells, -SUB)
            packed[i // 4] = jnp.where(slot == i % 4, turn(cells, (i % 4) * SUB), packed[i // 4])
    for j in range(len(packed)):
        combined[pl.ds((fields * eofs + j) * SUB, SUB), :] = packed[j]


def forward_kernel(
    fields, eofs, place_ref, own, from_a, from_b, coeff_main, coeff_strip,
    out, strip, strip_out, wide, wide_strip, first, second,
):
    odd = place_ref[1] == 1
    tile = tile_picker(own, from_a, from_b, odd)
    row = row_picker(own, from_a, from_b, odd)
    lane = lane_grid()
    inner = lane & (SLOT - 1)
    shifted = (lane + STEPS) & (LANES - 1)
    zero = jnp.zeros((SUB, LANES), jnp.float32)
    halo = (inner >= STEPS) & (inner < HALO)

    for k in range(4):
        for w in range(WINDOW):
            wide[k, w] = jnp.broadcast_to(coeff_main[k, pl.ds(w + 2, 1), :], (SUB, LANES))
    strip_coefficients(coeff_strip, wide_strip, eofs)

    for t in range(3):
        for e in range(eofs):
            west, east = zero, zero
            for f in range(fields):
                cells = tile(t, f * eofs + e)
                west = jnp.where(lane // SLOT == f, turn(cells, f * SLOT + HALO), west)
                east = jnp.where(
                    shifted // SLOT == f, turn(cells, f * SLOT - STEPS - LANES + HALO), east
                )
            for side, cells in enumerate((west, east)):
                i = side * eofs + e
                beyond = turn(tile(t, fields * eofs + i // 4), STEPS - (i % 4) * SUB)
                strip[t, pl.ds(i * SUB, SUB), :] = jnp.where(halo, beyond, cells)
        strip[t, pl.ds(2 * eofs * SUB, 4 * SUB), :] = jnp.zeros((4 * SUB, LANES), jnp.float32)

    diffuse_strip(strip, strip_out, wide_strip, first, second, False)
    groups = fields * eofs // SUB

    def write(w, g, cells):
        out[pl.ds(g * SUB * SUB + w - STEPS, SUB, stride=SUB), :] = cells

    diffuse(row, write, lambda k, w: [wide[k, w]] * groups, groups, first, second, False)
    for f in range(fields):
        for e in range(eofs):
            at = pl.ds((f * eofs + e) * SUB, SUB)
            west = turn(strip_out[pl.ds(e * SUB, SUB), :], -f * SLOT - HALO)
            east = turn(strip_out[pl.ds((eofs + e) * SUB, SUB), :], LANES - STEPS - f * SLOT)
            out[at, :] = jnp.where(
                lane < STEPS, west, jnp.where(lane >= LANES - STEPS, east, out[at, :])
            )


def call(kernel, args, outs, scratch=(), flops=1_000_000):
    whole = pl.BlockSpec(memory_space=pltpu.VMEM)
    moved = sum(a.size * a.dtype.itemsize for a in list(args) + list(outs))
    return pl.pallas_call(
        kernel,
        in_specs=[pl.BlockSpec(memory_space=pltpu.SMEM)] + [whole] * (len(args) - 1),
        out_specs=[whole] * len(outs),
        out_shape=list(outs),
        scratch_shapes=list(scratch),
        compiler_params=pltpu.CompilerParams(vmem_limit_bytes=32 * 2**20),
        cost_estimate=pl.CostEstimate(flops=flops, bytes_accessed=moved, transcendentals=0),
    )(*args)


def per_device(panels, eof_basis, control, coefficients):
    members, fields, depth, row_count, _ = panels.shape
    _, eofs, _, col_count = control.shape
    count = lax.axis_size("gz")
    me = lax.axis_index("gz")
    ring = lax.axis_index("gx") * count + me
    where_am_i = jnp.stack([ring % 2, lax.axis_index("gy") % 2, me]).astype(jnp.int32)

    def columns(of):
        return lax.dynamic_slice_in_dim(panels, of * col_count, col_count, axis=4)

    arrived = [
        lax.ppermute(
            columns((me + s) % count), "gz", [(i, (i + s) % count) for i in range(count)]
        )
        for s in range(1, count)
    ]
    panel = columns(me)
    total_fields = fields * eofs
    own = jnp.concatenate(
        [
            control.reshape(total_fields * row_count, col_count),
            coefficients.reshape(4 * row_count, col_count),
        ]
    )
    from_a, from_b = swap_a(own, "gy"), swap_b(own, "gy", False)

    basis = eof_basis.transpose(0, 2, 1).reshape(fields, eofs, 1, count, depth, 1)
    basis = basis * jnp.eye(row_count, dtype=eof_basis.dtype)[:, None, None, :]
    basis = basis.transpose(3, 0, 1, 2, 4, 5).reshape(
        count, fields, eofs * row_count, depth * row_count
    )

    f32 = lambda *shape: jax.ShapeDtypeStruct(shape, jnp.float32)
    rows_sent = 3 * (eofs // 2 + 1) * row_count + count * depth * row_count
    sent_a, sent_b = call(
        functools.partial(pack_kernel, fields, eofs, members),
        [where_am_i, own, from_a, from_b, panel, *arrived],
        [f32(rows_sent, col_count)] * 2,
    )
    got_a, got_b = swap_a(sent_a, RING), swap_b(sent_b, RING, True)

    strip_rows = (2 * eofs + 4) * row_count
    adj, proj, strip, coeff_main, coeff_strip = call(
        functools.partial(main_kernel, fields, eofs, members),
        [where_am_i, own, from_a, from_b, basis, panel, *arrived],
        [
            f32(total_fields * row_count, col_count),
            f32(members, total_fields * row_count, col_count),
            f32(3, strip_rows, col_count),
            f32(4, 3 * row_count, col_count),
            f32(2, 4, 3 * row_count, col_count),
        ],
        [pltpu.VMEM((4, WINDOW, SUB, LANES), jnp.float32)]
        + [pltpu.VMEM((WINDOW, total_fields, LANES), jnp.float32)] * 2,
        flops=20_000_000,
    )
    combined, coeff_strip = call(
        functools.partial(combine_kernel, fields, eofs, members),
        [where_am_i, got_a, got_b, basis, adj, proj, strip, coeff_strip],
        [
            f32(total_fields * row_count + 2 * eofs // 4 * row_count, col_count),
            f32(2, 4, 3 * row_count, col_count),
        ],
        [
            pltpu.VMEM((3, strip_rows, LANES), jnp.float32),
            pltpu.VMEM((4, WINDOW, 3 * SUB, LANES), jnp.float32),
            pltpu.VMEM((strip_rows, LANES), jnp.float32),
            pltpu.VMEM((count * depth * row_count, 2 * LANES), jnp.bfloat16),
            pltpu.VMEM((strip_rows, LANES), jnp.float32),
        ]
        + [pltpu.VMEM((WINDOW, 3 * SUB, LANES), jnp.float32)] * 2,
    )
    from_a, from_b = swap_a(combined, "gy"), swap_b(combined, "gy", False)
    (result,) = call(
        functools.partial(forward_kernel, fields, eofs),
        [where_am_i, combined, from_a, from_b, coeff_main, coeff_strip],
        [f32(total_fields * row_count, col_count)],
        [
            pltpu.VMEM((3, strip_rows, LANES), jnp.float32),
            pltpu.VMEM((strip_rows, LANES), jnp.float32),
            pltpu.VMEM((4, WINDOW, SUB, LANES), jnp.float32),
            pltpu.VMEM((4, WINDOW, 3 * SUB, LANES), jnp.float32),
        ]
        + [pltpu.VMEM((WINDOW, total_fields, LANES), jnp.float32)] * 2,
    )
    return result.reshape(control.shape)


def solution(mesh):
    in_specs = (
        P(None, None, "gz", "gy", "gx"),
        P(),
        P(None, None, "gy", ("gx", "gz")),
        P(None, "gy", ("gx", "gz")),
    )
    out_specs = P(None, None, "gy", ("gx", "gz"))
    return jax.shard_map(
        per_device, mesh=mesh, in_specs=in_specs, out_specs=out_specs, check_vma=False
    )
```

```python
import functools

import jax
import jax.numpy as jnp
from jax import lax
from jax.experimental import pallas as pl
from jax.experimental.pallas import tpu as pltpu
from jax.sharding import PartitionSpec as P

STEPS = 6
LANES = 128
SUB = 8
RING = ("gx", "gz")

time_step = 0.09

WINDOW = SUB + 2 * STEPS
HALO = 2 * STEPS
SLOT = 32


def turn(cells, shift):
    return pltpu.roll(cells, shift % LANES, 1)


def swap_a(values, axes):
    count = lax.axis_size(axes)
    return lax.ppermute(values, axes, [(i, i ^ 1) for i in range(count)])


def swap_b(values, axes, closed):
    count = lax.axis_size(axes)
    pairs = [(i, i + 1) for i in range(1, count - 1, 2)]
    if closed:
        pairs.append((count - 1, 0))
    return lax.ppermute(values, axes, pairs + [(j, i) for i, j in pairs])


def place(w):
    return (w + 2) // SUB, (w + 2) % SUB


def lane_grid():
    return lax.broadcasted_iota(jnp.int32, (SUB, LANES), 1)


def diffuse(read, write, coeff, groups, first, second, adjoint):
    state, spare = None, first
    for step in range(STEPS):
        low, high = step, WINDOW - 1 - step

        def fetch(w):
            if state is None:
                return [read(w, g) for g in range(groups)]
            return [state[w, pl.ds(g * SUB, SUB), :] for g in range(groups)]

        here, seen, south = fetch(low), None, None
        for w in range(low, high):
            k = [coeff(i, w) for i in range(4)]
            north = fetch(w + 1)
            if adjoint:
                if seen is None:
                    seen = [k[3][g] * here[g] for g in range(groups)]
                area = coeff(3, w + 1)
                seen_north = [area[g] * north[g] for g in range(groups)]
            else:
                seen, seen_north = here, north
            flux = []
            for g in range(groups):
                east_diff = turn(seen[g], -1) - seen[g]
                north_diff = seen_north[g] - seen[g]
                flux.append(k[1][g] * east_diff + k[2][g] * north_diff)
                if w > low:
                    flux_east = k[0][g] * east_diff + k[1][g] * north_diff
                    div = flux_east - turn(flux_east, 1) + (flux[g] - south[g])
                    moved = here[g] + (div if adjoint else k[3][g] * div)
                    if step == STEPS - 1:
                        write(w, g, moved)
                    else:
                        spare[w, pl.ds(g * SUB, SUB), :] = moved
            here, seen, south = north, seen_north, flux
        state, spare = spare, (second if spare is first else first)


def read_pair(ref, pair):
    cells = ref[pl.ds(pair * 2 * SUB, 2 * SUB), :].astype(jnp.float32)
    return cells[:SUB], cells[SUB:]


def write_pair(ref, pair, first, second):
    cells = jnp.concatenate([first, second], axis=0).astype(jnp.bfloat16)
    ref[pl.ds(pair * 2 * SUB, 2 * SUB), :] = cells


def split(cells):
    high = cells.astype(jnp.bfloat16).astype(jnp.float32)
    return high, cells - high


def encode_rows(cells, sub):
    high, low = split(cells)
    edge = SUB - STEPS
    to_north = jnp.where(sub < STEPS, high, pltpu.roll(low, STEPS, 0))
    to_south = jnp.where(sub >= edge, high, pltpu.roll(low, edge, 0))
    return to_north, to_south


def decode_rows(from_a, from_b, odd, sub, pair):
    edge = SUB - STEPS
    north, south = [], []
    for a, b in zip(read_pair(from_a, pair), read_pair(from_b, pair)):
        above, below = jnp.where(odd, a, b), jnp.where(odd, b, a)
        north.append(above + jnp.where(sub >= STEPS, pltpu.roll(above, STEPS, 0), 0.0))
        south.append(below + jnp.where(sub < edge, pltpu.roll(below, edge, 0), 0.0))
    return north, south


def send_rows_kernel(place_ref, control, coefficients, out_a, out_b):
    odd = place_ref[1] == 1
    sub = lax.broadcasted_iota(jnp.int32, (SUB, LANES), 0)
    first = control.shape[0] // SUB
    count = first + coefficients.shape[0] // SUB

    def tile(i):
        if i < first:
            return control[pl.ds(i * SUB, SUB), :]
        return coefficients[pl.ds((i - first) * SUB, SUB), :]

    put_rows(out_a, out_b, [tile(i) for i in range(count)], odd, sub)


def put_rows(out_a, out_b, tiles, odd, sub):
    for pair in range(len(tiles) // 2):
        north, south = zip(*[encode_rows(t, sub) for t in tiles[2 * pair : 2 * pair + 2]])
        write_pair(out_a, pair, *[jnp.where(odd, n, s) for n, s in zip(north, south)])
        write_pair(out_b, pair, *[jnp.where(odd, s, n) for n, s in zip(north, south)])


def strip_tiles(fields, eofs, tile, lane):
    pair = eofs // 2
    zero = jnp.zeros((SUB, LANES), jnp.float32)
    west_out, east_out = [], []
    at = lane & (SLOT // 2 - 1)
    for j in range(pair):
        west, east = zero, zero
        for half in range(2):
            for f in range(fields):
                cells = tile(f * eofs + half * pair + j)
                start = f * SLOT + half * (SLOT // 2)
                mask = (lane >= start) & (lane < start + HALO)
                west = jnp.where(mask, turn(cells, start), west)
                east = jnp.where(mask, turn(cells, start + HALO - LANES), east)
        high, low = split(west)
        west_out.append(jnp.where(at < HALO, high, turn(low, HALO)))
        high, low = split(east)
        east_out.append(jnp.where(at < HALO, high, turn(low, 4)))
    west, east = zero, zero
    for k in range(4):
        cells = tile(fields * eofs + k)
        start = k * SLOT
        mask = (lane >= start) & (lane < start + HALO)
        west = jnp.where(mask, turn(cells, start), west)
        east = jnp.where(mask, turn(cells, start + HALO - LANES), east)
    for cells, out in ((west, west_out), (east, east_out)):
        high, low = split(cells)
        out.append(high + turn(low, SLOT // 2))
    return west_out, east_out


def own_strips_kernel(fields, eofs, members, control, coefficients, *rest):
    panels, (west, east, edges) = rest[:-3], rest[-3:]
    lane = lane_grid()
    total = fields * eofs

    def tile(i):
        if i < total:
            return control[pl.ds(i * SUB, SUB), :]
        return coefficients[pl.ds((i - total) * SUB, SUB), :]

    for ref, tiles in zip((west, east), strip_tiles(fields, eofs, tile, lane)):
        for pair in range(len(tiles) // 2):
            write_pair(ref, pair, *tiles[2 * pair : 2 * pair + 2])

    depth = panels[0].shape[2] * SUB
    column = lax.broadcasted_iota(jnp.int32, (LANES, 2 * LANES), 0)
    target = lax.broadcasted_iota(jnp.int32, (LANES, 2 * LANES), 1)
    west_ok = (target < LANES) & (column < STEPS)
    east_ok = (target >= LANES) & (column >= LANES - STEPS)
    offset = jnp.where(
        west_ok,
        target - column,
        jnp.where(east_ok, target - LANES - column + LANES - STEPS, -1),
    )
    for s, block in enumerate(panels):
        total = jnp.zeros((depth, 2 * LANES), jnp.float32)
        for m in range(members):
            for f in range(fields):
                pick = (offset == f * SLOT + m * SUB).astype(jnp.bfloat16)
                total += jnp.dot(
                    block[m, f].reshape(depth, LANES), pick, preferred_element_type=jnp.float32
                )
        total = total.astype(jnp.bfloat16)
        edges[s, 0] = total[:, :LANES]
        edges[s, 1] = total[:, LANES:]


def pack_kernel(fields, eofs, place_ref, from_a, from_b, west, east, *rest):
    panel_edges, (out_a, out_b, north, south) = rest[:-4], rest[-4:]
    ring_odd, odd = place_ref[0] == 1, place_ref[1] == 1
    lane = lane_grid()
    sub = lax.broadcasted_iota(jnp.int32, (SUB, LANES), 0)
    for pair in range((fields * eofs + 4) // 2):
        above, below = decode_rows(from_a, from_b, odd, sub, pair)
        at = pl.ds(pair * 2 * SUB, 2 * SUB)
        north[at, :] = jnp.concatenate(above, axis=0)
        south[at, :] = jnp.concatenate(below, axis=0)

    def put(pair, mine_west, mine_east):
        write_pair(out_a, pair, *[jnp.where(ring_odd, w, e) for w, e in zip(mine_west, mine_east)])
        write_pair(out_b, pair, *[jnp.where(ring_odd, e, w) for w, e in zip(mine_west, mine_east)])

    pairs = (eofs // 2 + 1) // 2
    for t, ref in ((0, north), (2, south)):
        tiles = strip_tiles(fields, eofs, lambda i: ref[pl.ds(i * SUB, SUB), :], lane)
        for j in range(pairs):
            put(t * pairs + j, tiles[0][2 * j : 2 * j + 2], tiles[1][2 * j : 2 * j + 2])
    for j in range(pairs):
        put(pairs + j, read_pair(west, j), read_pair(east, j))
    for edges in panel_edges:
        for j in range(edges.shape[2] // (2 * SUB)):
            put(3 * pairs + j, read_pair(edges.at[0, 0], j), read_pair(edges.at[0, 1], j))


def own_columns(fields, eofs, tile, strip, t, lane):
    shifted = (lane + STEPS) & (LANES - 1)
    zero = jnp.zeros((SUB, LANES), jnp.float32)
    for e in range(eofs):
        west, east = zero, zero
        for f in range(fields):
            cells = tile(f * eofs + e)
            west = jnp.where(lane // SLOT == f, turn(cells, f * SLOT + HALO), west)
            east = jnp.where(
                shifted // SLOT == f, turn(cells, f * SLOT - STEPS - LANES + HALO), east
            )
        strip[t, pl.ds(e * SUB, SUB), :] = west
        strip[t, pl.ds((eofs + e) * SUB, SUB), :] = east
    strip[t, pl.ds(2 * eofs * SUB, 4 * SUB), :] = jnp.zeros((4 * SUB, LANES), jnp.float32)


def main_kernel(
    fields, eofs, control, coefficients, north, south,
    adj, strip, coeff_main, coeff_strip, wide, first, second,
):
    lane = lane_grid()
    inner = lane & (SLOT - 1)
    shifted = (lane + STEPS) & (LANES - 1)
    zero = jnp.zeros((SUB, LANES), jnp.float32)
    total = fields * eofs

    def tile(t, i):
        if t != 1:
            return (north, south)[t // 2][pl.ds(i * SUB, SUB), :]
        if i < total:
            return control[pl.ds(i * SUB, SUB), :]
        return coefficients[pl.ds((i - total) * SUB, SUB), :]

    for k in range(4):
        for t in range(3):
            cells = tile(t, total + k)
            if k < 3:
                cells = time_step * cells
            at = pl.ds(t * SUB, SUB)
            coeff_main[k, at, :] = cells
            west, east = zero, zero
            for f in range(fields):
                start = f * SLOT
                west = jnp.where(lane // SLOT == f, turn(cells, start + HALO), west)
                east = jnp.where(
                    shifted // SLOT == f, turn(cells, start - STEPS - LANES + HALO), east
                )
            coeff_strip[0, k, at, :] = jnp.where((inner >= HALO) & (inner < 2 * HALO), west, 0.0)
            coeff_strip[1, k, at, :] = jnp.where((shifted & (SLOT - 1)) < HALO, east, 0.0)
    main_coefficients(coeff_main, wide)
    diffuse_main(control, north, south, adj, wide, first, second, True)
    for t in range(3):
        own_columns(fields, eofs, lambda i: tile(t, i), strip, t, lane)


def project_kernel(fields, eofs, members, place_ref, basis, panel, *rest):
    arrived, proj = rest[:-1], rest[-1]
    me = place_ref[2]
    blocks = (panel,) + arrived
    count = len(blocks)
    depth = panel.shape[2] * SUB
    for f in range(fields):
        total = None
        for s, block in enumerate(blocks):
            cells = jnp.concatenate(
                [block[m, f].reshape(depth, LANES) for m in range(members)], axis=1
            )
            part = jnp.dot(
                basis[lax.rem(me - s + count, count), f], cells, preferred_element_type=jnp.float32
            )
            total = part if total is None else total + part
        for m in range(members):
            proj[m, pl.ds(f * eofs * SUB, eofs * SUB), :] = total[:, m * LANES : (m + 1) * LANES]


def main_coefficients(coeff_main, wide):
    for k in range(4):
        for w in range(WINDOW):
            wide[k, w] = jnp.broadcast_to(coeff_main[k, pl.ds(w + 2, 1), :], (SUB, LANES))


def strip_coefficients(coeff_strip, wide_strip, eofs):
    sub = lax.broadcasted_iota(jnp.int32, (SUB, LANES), 0)
    for k in range(4):
        for w in range(WINDOW):
            west = jnp.broadcast_to(coeff_strip[0, k, pl.ds(w + 2, 1), :], (SUB, LANES))
            east = jnp.broadcast_to(coeff_strip[1, k, pl.ds(w + 2, 1), :], (SUB, LANES))
            wide_strip[k, w, pl.ds(0, SUB), :] = west
            wide_strip[k, w, pl.ds(SUB, SUB), :] = jnp.where(sub < eofs - SUB, west, east)
            wide_strip[k, w, pl.ds(2 * SUB, SUB), :] = east


def diffuse_main(own, north, south, out, wide, first, second, adjoint):
    groups = own.shape[0] // (SUB * SUB)

    def read(w, g):
        t, y = place(w)
        return (north, own, south)[t][pl.ds(g * SUB * SUB + y, SUB, stride=SUB), :]

    def write(w, g, cells):
        out[pl.ds(g * SUB * SUB + w - STEPS, SUB, stride=SUB), :] = cells

    diffuse(read, write, lambda k, w: [wide[k, w]] * groups, groups, first, second, adjoint)


def diffuse_strip(strip, out, wide_strip, first, second, adjoint):
    def read(w, g):
        t, y = place(w)
        return strip[t, pl.ds(g * SUB * SUB + y, SUB, stride=SUB), :]

    def write(w, g, cells):
        out[pl.ds(g * SUB * SUB + w - STEPS, SUB, stride=SUB), :] = cells

    def coeff(k, w):
        return [wide_strip[k, w, pl.ds(g * SUB, SUB), :] for g in range(3)]

    diffuse(read, write, coeff, 3, first, second, adjoint)


def combine_kernel(fields, eofs, members, place_ref, got_a, got_b, *rest):
    (
        basis, adj, proj, strip_own, coeff_own,
        out_a, out_b, combined, halo_out, coeff_strip,
        strip, wide_strip, adj_strip, panel_in, proj_strip, first, second,
    ) = rest[-17:]
    panel_parts = rest[:-17]
    ring_odd, odd, me = place_ref[0] == 1, place_ref[1] == 1, place_ref[2]
    lane = lane_grid()
    sub = lax.broadcasted_iota(jnp.int32, (SUB, LANES), 0)
    inner = lane & (SLOT - 1)
    pair = eofs // 2

    def got(j):
        found = zip(read_pair(got_a, j), read_pair(got_b, j))
        sides = [(jnp.where(ring_odd, a, b), jnp.where(ring_odd, b, a)) for a, b in found]
        return zip(*sides)

    west_mask = inner < HALO
    east_mask = (inner >= STEPS) & (inner < STEPS + HALO)
    at16 = lane & (SLOT // 2 - 1)
    pairs = (pair + 1) // 2
    for t in range(3):
        west_tiles, east_tiles = [], []
        for j in range(pairs):
            west, east = got(t * pairs + j)
            west_tiles += west
            east_tiles += east
        for j in range(pair):
            west, east = west_tiles[j], east_tiles[j]
            west = west + jnp.where((at16 >= HALO - 4) & (at16 < HALO), turn(west, -4), 0.0)
            east = east + jnp.where(at16 < 4, turn(east, -HALO), 0.0)
            for half in range(2):
                e = half * pair + j
                at = pl.ds(e * SUB, SUB)
                strip[t, at, :] = jnp.where(
                    west_mask, turn(west, -half * (SLOT // 2)), strip_own[t, at, :]
                )
                at = pl.ds((eofs + e) * SUB, SUB)
                strip[t, at, :] = jnp.where(
                    east_mask, turn(east, STEPS - half * (SLOT // 2)), strip_own[t, at, :]
                )
        at = pl.ds(2 * eofs * SUB, 4 * SUB)
        strip[t, at, :] = strip_own[t, at, :]
        at = pl.ds(t * SUB, SUB)
        for side, (cells, mask) in enumerate(
            ((west_tiles[pair], west_mask), (east_tiles[pair], east_mask))
        ):
            cells = cells + turn(cells, -(SLOT // 2))
            for k in range(4):
                mine = jnp.where(lane // SLOT == k, cells, 0.0)
                mine = mine + turn(mine, SLOT)
                mine = mine + turn(mine, 2 * SLOT)
                if side == 1:
                    mine = turn(mine, STEPS)
                if k < 3:
                    mine = time_step * mine
                coeff_strip[side, k, at, :] = jnp.where(mask, mine, coeff_own[side, k, at, :])
    strip_coefficients(coeff_strip, wide_strip, eofs)
    diffuse_strip(strip, adj_strip, wide_strip, first, second, True)

    count, depth = basis.shape[0], basis.shape[3]
    if len(panel_parts) == 2:
        edges, far = panel_parts
        near_west, near_east, far = edges[1, 0], edges[1, 1], far[...]
        at = pl.ds(3 * pairs * 2 * SUB, depth)
        a, b = got_a[at, :], got_b[at, :]
        wests = [jnp.where(ring_odd, near_east, far), jnp.where(ring_odd, a, b)]
        easts = [jnp.where(ring_odd, far, near_west), jnp.where(ring_odd, b, a)]
    else:
        wests = [ref[...] for ref in panel_parts[:count]]
        easts = [ref[...] for ref in panel_parts[count:]]
    for s in range(count):
        panel_in[s] = jnp.concatenate([wests[s], easts[s]], axis=1)
    wide_lane = lax.broadcasted_iota(jnp.int32, (eofs * SUB, 2 * LANES), 1) & (LANES - 1)
    halo = jnp.zeros((eofs * SUB, 2 * LANES), jnp.float32)
    for f in range(fields):
        total = None
        for s in range(count):
            part = jnp.dot(
                basis[lax.rem(me + s, count), f], panel_in[s], preferred_element_type=jnp.float32
            )
            total = part if total is None else total + part
        halo = jnp.where(wide_lane // SLOT == f, total, halo)
    proj_strip[pl.ds(0, eofs * SUB), :] = halo[:, :LANES]
    proj_strip[pl.ds(eofs * SUB, eofs * SUB), :] = halo[:, LANES:]

    scores = [jnp.zeros((SUB, LANES), jnp.float32) for _ in range(members)]
    for f in range(fields):
        for e in range(eofs):
            at = pl.ds((f * eofs + e) * SUB, SUB)
            west = turn(adj_strip[pl.ds(e * SUB, SUB), :], -f * SLOT - HALO)
            east = turn(adj_strip[pl.ds((eofs + e) * SUB, SUB), :], LANES - STEPS - f * SLOT)
            cells = jnp.where(
                lane < STEPS, west, jnp.where(lane >= LANES - STEPS, east, adj[at, :])
            )
            for m in range(members):
                scores[m] = scores[m] + proj[m, at, :] * cells
    scores = [s / (members - 1) for s in scores]
    tiles = []
    for i in range(fields * eofs):
        at = pl.ds(i * SUB, SUB)
        total = proj[0, at, :] * scores[0]
        for m in range(1, members):
            total = total + proj[m, at, :] * scores[m]
        combined[at, :] = total
        tiles.append(total)

    slot = inner // SUB
    packed = [jnp.zeros((SUB, LANES), jnp.float32) for _ in range(2 * eofs // 4)]
    for side in range(2):
        total = jnp.zeros((SUB, LANES), jnp.float32)
        for e in range(eofs):
            at = pl.ds((side * eofs + e) * SUB, SUB)
            cells = adj_strip[at, :]
            spread = turn(cells, -STEPS)
            for m in range(1, members):
                spread = jnp.where(slot == m, turn(cells, m * SUB - STEPS), spread)
            total = total + proj_strip[at, :] * spread
        total = total + turn(total, SLOT)
        total = (total + turn(total, 2 * SLOT)) / (members - 1)
        for e in range(eofs):
            i = side * eofs + e
            cells = proj_strip[pl.ds(i * SUB, SUB), :] * total
            cells = cells + turn(cells, -2 * SUB)
            cells = cells + turn(cells, -SUB)
            packed[i // 4] = jnp.where(slot == i % 4, turn(cells, (i % 4) * SUB), packed[i // 4])
    for j, cells in enumerate(packed):
        halo_out[pl.ds(j * SUB, SUB), :] = cells
    tiles += packed
    if len(tiles) % 2:
        tiles.append(jnp.zeros((SUB, LANES), jnp.float32))
    put_rows(out_a, out_b, tiles, odd, sub)


def beyond_columns(eofs, packed, strip, t, lane):
    inner = lane & (SLOT - 1)
    mask = (inner >= STEPS) & (inner < HALO)
    for i in range(2 * eofs):
        cells = turn(packed[pl.ds(i // 4 * SUB, SUB), :], STEPS - (i % 4) * SUB)
        at = pl.ds(i * SUB, SUB)
        strip[t, at, :] = jnp.where(mask, cells, strip[t, at, :])


def before_forward_kernel(fields, eofs, own, halo, coeff_main, coeff_strip, wide, wide_strip, strip):
    lane = lane_grid()
    main_coefficients(coeff_main, wide)
    strip_coefficients(coeff_strip, wide_strip, eofs)
    own_columns(fields, eofs, lambda i: own[pl.ds(i * SUB, SUB), :], strip, 0, lane)
    beyond_columns(eofs, halo, strip, 0, lane)


def forward_kernel(
    fields, eofs, place_ref, own, from_a, from_b, wide, wide_strip, strip_own,
    out, north, south, strip, strip_out, first, second,
):
    odd = place_ref[1] == 1
    lane = lane_grid()
    sub = lax.broadcasted_iota(jnp.int32, (SUB, LANES), 0)
    total = fields * eofs
    for pair in range(north.shape[0] // (2 * SUB)):
        above, below = decode_rows(from_a, from_b, odd, sub, pair)
        at = pl.ds(pair * 2 * SUB, 2 * SUB)
        north[at, :] = jnp.concatenate(above, axis=0)
        south[at, :] = jnp.concatenate(below, axis=0)
    for t, ref in ((0, north), (2, south)):
        own_columns(fields, eofs, lambda i: ref[pl.ds(i * SUB, SUB), :], strip, t, lane)
        beyond_columns(eofs, ref.at[pl.ds(total * SUB, 2 * eofs // 4 * SUB)], strip, t, lane)
    strip[1] = strip_own[0]
    diffuse_strip(strip, strip_out, wide_strip, first, second, False)
    diffuse_main(own, north, south, out, wide, first, second, False)
    for f in range(fields):
        for e in range(eofs):
            at = pl.ds((f * eofs + e) * SUB, SUB)
            west = turn(strip_out[pl.ds(e * SUB, SUB), :], -f * SLOT - HALO)
            east = turn(strip_out[pl.ds((eofs + e) * SUB, SUB), :], LANES - STEPS - f * SLOT)
            out[at, :] = jnp.where(
                lane < STEPS, west, jnp.where(lane >= LANES - STEPS, east, out[at, :])
            )


def call(kernel, args, outs, scratch=(), flops=1_000_000):
    whole = pl.BlockSpec(memory_space=pltpu.VMEM)
    scalars = pl.BlockSpec(memory_space=pltpu.SMEM)
    moved = sum(a.size * a.dtype.itemsize for a in list(args) + list(outs))
    return pl.pallas_call(
        kernel,
        in_specs=[scalars if a.dtype == jnp.int32 else whole for a in args],
        out_specs=[whole] * len(outs),
        out_shape=list(outs),
        scratch_shapes=[pltpu.VMEM(*s) for s in scratch],
        compiler_params=pltpu.CompilerParams(vmem_limit_bytes=24 * 2**20),
        cost_estimate=pl.CostEstimate(flops=flops, bytes_accessed=moved, transcendentals=0),
    )(*args)


def panel_edges_apart(edges, count, me):
    groups = lax.axis_size("gx")
    wests, easts = [], []
    for s in range(count):
        for side, into in ((1, wests), (0, easts)):
            pairs = []
            for group in range(groups):
                for held in range(count):
                    tile = (held - s) % count
                    if side == 1:
                        to = group + (tile == 0)
                    else:
                        to = group - (tile == count - 1)
                    pairs.append((group * count + held, to % groups * count + tile))
            ahead = (-s - 1) if side == 1 else (1 - s)
            into.append(lax.ppermute(edges[ahead % count, side], RING, pairs))
    return wests + easts


def per_device(panels, eof_basis, control, coefficients):
    members, fields, depth, row_count, _ = panels.shape
    _, eofs, _, col_count = control.shape
    count = lax.axis_size("gz")
    me = lax.axis_index("gz")
    ring = lax.axis_index("gx") * count + me
    where_am_i = jnp.stack([ring % 2, lax.axis_index("gy") % 2, me]).astype(jnp.int32)
    total = fields * eofs
    rows = total * row_count
    control_in = control.reshape(rows, col_count)
    coeff_in = coefficients.reshape(4 * row_count, col_count)
    f32 = lambda *shape: jax.ShapeDtypeStruct(shape, jnp.float32)
    bf16 = lambda *shape: jax.ShapeDtypeStruct(shape, jnp.bfloat16)

    def columns(of):
        return lax.dynamic_slice_in_dim(panels, of * col_count, col_count, axis=4)

    tiles = [columns((me + s) % count) for s in range(count)]
    arrived = [
        lax.ppermute(tiles[s], "gz", [(i, (i + s) % count) for i in range(count)])
        for s in range(1, count)
    ]

    sent_a, sent_b = call(
        send_rows_kernel,
        [where_am_i, control_in, coeff_in],
        [bf16(rows + 4 * row_count, col_count)] * 2,
    )
    from_a, from_b = swap_a(sent_a, "gy"), swap_b(sent_b, "gy", False)

    strip_sent = (eofs // 2 + 1) * row_count
    west, east, edges = call(
        functools.partial(own_strips_kernel, fields, eofs, members),
        [control_in, coeff_in, *tiles],
        [bf16(strip_sent, col_count)] * 2 + [bf16(count, 2, depth * row_count, col_count)],
    )
    if count == 2:
        groups = lax.axis_size("gx")
        pairs = [(2 * g, (g + 1) % groups * 2) for g in range(groups)]
        pairs += [(2 * g + 1, (g - 1) % groups * 2 + 1) for g in range(groups)]
        far = lax.ppermute(jnp.where(me == 1, edges[1, 0], edges[1, 1]), RING, pairs)
        panel_sent, panel_parts = [edges], [edges, far]
    else:
        panel_sent, panel_parts = [], panel_edges_apart(edges, count, me)

    basis = eof_basis.transpose(0, 2, 1).reshape(fields, eofs, 1, count, depth, 1)
    basis = basis * jnp.eye(row_count, dtype=eof_basis.dtype)[:, None, None, :]
    basis = basis.transpose(3, 0, 1, 2, 4, 5).reshape(
        count, fields, eofs * row_count, depth * row_count
    )

    sent_a, sent_b, north, south = call(
        functools.partial(pack_kernel, fields, eofs),
        [where_am_i, from_a, from_b, west, east, *panel_sent],
        [bf16(3 * strip_sent + len(panel_sent) * depth * row_count, col_count)] * 2
        + [f32(rows + 4 * row_count, col_count)] * 2,
    )
    got_a, got_b = swap_a(sent_a, RING), swap_b(sent_b, RING, True)

    strip_rows = (2 * eofs + 4) * row_count
    main_scratch = [((WINDOW, total, LANES), jnp.float32)] * 2
    strip_scratch = [((WINDOW, 3 * SUB, LANES), jnp.float32)] * 2
    adj, strip, coeff_main, coeff_strip = call(
        functools.partial(main_kernel, fields, eofs),
        [control_in, coeff_in, north, south],
        [
            f32(rows, col_count),
            f32(3, strip_rows, col_count),
            f32(4, 3 * row_count, col_count),
            f32(2, 4, 3 * row_count, col_count),
        ],
        [((4, WINDOW, SUB, LANES), jnp.float32)] + main_scratch,
        flops=20_000_000,
    )
    (proj,) = call(
        functools.partial(project_kernel, fields, eofs, members),
        [where_am_i, basis, tiles[0], *arrived],
        [f32(members, rows, col_count)],
        flops=20_000_000,
    )
    packed = 2 * eofs // 4
    sent_a, sent_b, combined, halo, coeff_strip = call(
        functools.partial(combine_kernel, fields, eofs, members),
        [where_am_i, got_a, got_b, *panel_parts, basis, adj, proj, strip, coeff_strip],
        [bf16((total + packed + 1) // 2 * 2 * row_count, col_count)] * 2
        + [
            f32(rows, col_count),
            f32(packed * row_count, col_count),
            f32(2, 4, 3 * row_count, col_count),
        ],
        [
            ((3, strip_rows, LANES), jnp.float32),
            ((4, WINDOW, 3 * SUB, LANES), jnp.float32),
            ((strip_rows, LANES), jnp.float32),
            ((count, depth * row_count, 2 * LANES), jnp.bfloat16),
            ((2 * eofs * row_count, LANES), jnp.float32),
        ]
        + strip_scratch,
    )
    from_a, from_b = swap_a(sent_a, "gy"), swap_b(sent_b, "gy", False)
    wide, wide_strip, strip = call(
        functools.partial(before_forward_kernel, fields, eofs),
        [combined, halo, coeff_main, coeff_strip],
        [
            f32(4, WINDOW, SUB, LANES),
            f32(4, WINDOW, 3 * SUB, LANES),
            f32(1, strip_rows, LANES),
        ],
        flops=20_000_000,
    )
    (result,) = call(
        functools.partial(forward_kernel, fields, eofs),
        [where_am_i, combined, from_a, from_b, wide, wide_strip, strip],
        [f32(rows, col_count)],
        [((sent_a.shape[0], LANES), jnp.float32)] * 2
        + [((3, strip_rows, LANES), jnp.float32), ((strip_rows, LANES), jnp.float32)]
        + main_scratch,
    )
    return result.reshape(control.shape)


def solution(mesh):
    in_specs = (
        P(None, None, "gz", "gy", "gx"),
        P(),
        P(None, None, "gy", ("gx", "gz")),
        P(None, "gy", ("gx", "gz")),
    )
    out_specs = P(None, None, "gy", ("gx", "gz"))
    return jax.shard_map(
        per_device, mesh=mesh, in_specs=in_specs, out_specs=out_specs, check_vma=False
    )
```

```python
import functools

import jax
import jax.numpy as jnp
from jax import lax
from jax.experimental import pallas as pl
from jax.experimental.pallas import tpu as pltpu
from jax.sharding import PartitionSpec as P

STEPS = 6
LANES = 128
SUB = 8
RING = ("gx", "gz")

time_step = 0.09

WINDOW = SUB + 2 * STEPS
HALO = 2 * STEPS
SLOT = 32


def turn(cells, shift):
    return pltpu.roll(cells, shift % LANES, 1)


def swap_a(values, axes):
    count = lax.axis_size(axes)
    return lax.ppermute(values, axes, [(i, i ^ 1) for i in range(count)])


def swap_b(values, axes, closed):
    count = lax.axis_size(axes)
    pairs = [(i, i + 1) for i in range(1, count - 1, 2)]
    if closed:
        pairs.append((count - 1, 0))
    return lax.ppermute(values, axes, pairs + [(j, i) for i, j in pairs])


def place(w):
    return (w + 2) // SUB, (w + 2) % SUB


def position():
    me = lax.axis_index("gz")
    ring = lax.axis_index("gx") * lax.axis_size("gz") + me
    return lax.rem(ring, 2) == 1, lax.rem(lax.axis_index("gy"), 2) == 1, me


def lane_grid():
    return lax.broadcasted_iota(jnp.int32, (SUB, LANES), 1)


def diffuse(read, write, coeff, groups, first, second, adjoint):
    state, spare = None, first
    for step in range(STEPS):
        low, high = step, WINDOW - 1 - step

        def fetch(w):
            if state is None:
                return [read(w, g) for g in range(groups)]
            return [state[w, pl.ds(g * SUB, SUB), :] for g in range(groups)]

        here, seen, south = fetch(low), None, None
        for w in range(low, high):
            k = [coeff(i, w) for i in range(4)]
            north = fetch(w + 1)
            if adjoint:
                if seen is None:
                    seen = [k[3][g] * here[g] for g in range(groups)]
                area = coeff(3, w + 1)
                seen_north = [area[g] * north[g] for g in range(groups)]
            else:
                seen, seen_north = here, north
            flux = []
            for g in range(groups):
                east_diff = turn(seen[g], -1) - seen[g]
                north_diff = seen_north[g] - seen[g]
                flux.append(k[1][g] * east_diff + k[2][g] * north_diff)
                if w > low:
                    flux_east = k[0][g] * east_diff + k[1][g] * north_diff
                    div = flux_east - turn(flux_east, 1) + (flux[g] - south[g])
                    moved = here[g] + (div if adjoint else k[3][g] * div)
                    if step == STEPS - 1:
                        write(w, g, moved)
                    else:
                        spare[w, pl.ds(g * SUB, SUB), :] = moved
            here, seen, south = north, seen_north, flux
        state, spare = spare, (second if spare is first else first)


def read_pair(ref, pair):
    cells = ref[pl.ds(pair * 2 * SUB, 2 * SUB), :].astype(jnp.float32)
    return cells[:SUB], cells[SUB:]


def write_pair(ref, pair, first, second):
    cells = jnp.concatenate([first, second], axis=0).astype(jnp.bfloat16)
    ref[pl.ds(pair * 2 * SUB, 2 * SUB), :] = cells


def split(cells):
    high = cells.astype(jnp.bfloat16).astype(jnp.float32)
    return high, cells - high


def encode_rows(cells, sub):
    high, low = split(cells)
    edge = SUB - STEPS
    to_north = jnp.where(sub < STEPS, high, pltpu.roll(low, STEPS, 0))
    to_south = jnp.where(sub >= edge, high, pltpu.roll(low, edge, 0))
    return to_north, to_south


def decode_rows(from_a, from_b, odd, sub, pair):
    edge = SUB - STEPS
    north, south = [], []
    for a, b in zip(read_pair(from_a, pair), read_pair(from_b, pair)):
        above, below = jnp.where(odd, a, b), jnp.where(odd, b, a)
        north.append(above + jnp.where(sub >= STEPS, pltpu.roll(above, STEPS, 0), 0.0))
        south.append(below + jnp.where(sub < edge, pltpu.roll(below, edge, 0), 0.0))
    return north, south


def start_kernel(own, out_a, out_b):
    _, odd, _ = position()
    sub = lax.broadcasted_iota(jnp.int32, (SUB, LANES), 0)
    tiles = [own[pl.ds(i * SUB, SUB), :] for i in range(own.shape[0] // SUB)]
    put_rows(out_a, out_b, tiles, odd, sub)


def put_rows(out_a, out_b, tiles, odd, sub):
    for pair in range(len(tiles) // 2):
        north, south = zip(*[encode_rows(t, sub) for t in tiles[2 * pair : 2 * pair + 2]])
        write_pair(out_a, pair, *[jnp.where(odd, n, s) for n, s in zip(north, south)])
        write_pair(out_b, pair, *[jnp.where(odd, s, n) for n, s in zip(north, south)])


def strip_tiles(fields, eofs, tile, lane):
    pair = eofs // 2
    zero = jnp.zeros((SUB, LANES), jnp.float32)
    west_out, east_out = [], []
    at = lane & (SLOT // 2 - 1)
    for j in range(pair):
        west, east = zero, zero
        for half in range(2):
            for f in range(fields):
                cells = tile(f * eofs + half * pair + j)
                start = f * SLOT + half * (SLOT // 2)
                mask = (lane >= start) & (lane < start + HALO)
                west = jnp.where(mask, turn(cells, start), west)
                east = jnp.where(mask, turn(cells, start + HALO - LANES), east)
        high, low = split(west)
        west_out.append(jnp.where(at < HALO, high, turn(low, HALO)))
        high, low = split(east)
        east_out.append(jnp.where(at < HALO, high, turn(low, 4)))
    west, east = zero, zero
    for k in range(4):
        cells = tile(fields * eofs + k)
        start = k * SLOT
        mask = (lane >= start) & (lane < start + HALO)
        west = jnp.where(mask, turn(cells, start), west)
        east = jnp.where(mask, turn(cells, start + HALO - LANES), east)
    for cells, out in ((west, west_out), (east, east_out)):
        high, low = split(cells)
        out.append(high + turn(low, SLOT // 2))
    return west_out, east_out


def own_strips_kernel(fields, eofs, members, own, panels, west, east, edges, *tiles):
    _, _, me = position()
    lane = lane_grid()

    def tile(i):
        return own[pl.ds(i * SUB, SUB), :]

    for ref, packed in zip((west, east), strip_tiles(fields, eofs, tile, lane)):
        for pair in range(len(packed) // 2):
            write_pair(ref, pair, *packed[2 * pair : 2 * pair + 2])

    count = len(tiles)
    for s, block in enumerate(tiles):
        start = pl.multiple_of(lax.rem(me + s, count) * LANES, LANES)
        for m in range(members):
            for f in range(fields):
                block[m, f] = panels[m, f, :, :, pl.ds(start, LANES)]
    depth = panels.shape[2] * SUB
    column = lax.broadcasted_iota(jnp.int32, (LANES, 2 * LANES), 0)
    target = lax.broadcasted_iota(jnp.int32, (LANES, 2 * LANES), 1)
    west_ok = (target < LANES) & (column < STEPS)
    east_ok = (target >= LANES) & (column >= LANES - STEPS)
    offset = jnp.where(
        west_ok,
        target - column,
        jnp.where(east_ok, target - LANES - column + LANES - STEPS, -1),
    )
    for s, block in enumerate(tiles):
        total = jnp.zeros((depth, 2 * LANES), jnp.float32)
        for m in range(members):
            for f in range(fields):
                pick = (offset == f * SLOT + m * SUB).astype(jnp.bfloat16)
                total += jnp.dot(
                    block[m, f].reshape(depth, LANES), pick, preferred_element_type=jnp.float32
                )
        total = total.astype(jnp.bfloat16)
        edges[s, 0] = total[:, :LANES]
        edges[s, 1] = total[:, LANES:]


def pack_kernel(fields, eofs, from_a, from_b, west, east, *rest):
    panel_edges, (out_a, out_b, north, south) = rest[:-4], rest[-4:]
    ring_odd, odd, _ = position()
    lane = lane_grid()
    sub = lax.broadcasted_iota(jnp.int32, (SUB, LANES), 0)
    for pair in range((fields * eofs + 4) // 2):
        above, below = decode_rows(from_a, from_b, odd, sub, pair)
        at = pl.ds(pair * 2 * SUB, 2 * SUB)
        north[at, :] = jnp.concatenate(above, axis=0)
        south[at, :] = jnp.concatenate(below, axis=0)

    def put(pair, mine_west, mine_east):
        write_pair(out_a, pair, *[jnp.where(ring_odd, w, e) for w, e in zip(mine_west, mine_east)])
        write_pair(out_b, pair, *[jnp.where(ring_odd, e, w) for w, e in zip(mine_west, mine_east)])

    pairs = (eofs // 2 + 1) // 2
    for t, ref in ((0, north), (2, south)):
        tiles = strip_tiles(fields, eofs, lambda i: ref[pl.ds(i * SUB, SUB), :], lane)
        for j in range(pairs):
            put(t * pairs + j, tiles[0][2 * j : 2 * j + 2], tiles[1][2 * j : 2 * j + 2])
    for j in range(pairs):
        put(pairs + j, read_pair(west, j), read_pair(east, j))
    for edges in panel_edges:
        for j in range(edges.shape[2] // (2 * SUB)):
            put(3 * pairs + j, read_pair(edges.at[0, 0], j), read_pair(edges.at[0, 1], j))


def own_columns(fields, eofs, tile, strip, t, lane):
    shifted = (lane + STEPS) & (LANES - 1)
    zero = jnp.zeros((SUB, LANES), jnp.float32)
    for e in range(eofs):
        west, east = zero, zero
        for f in range(fields):
            cells = tile(f * eofs + e)
            west = jnp.where(lane // SLOT == f, turn(cells, f * SLOT + HALO), west)
            east = jnp.where(
                shifted // SLOT == f, turn(cells, f * SLOT - STEPS - LANES + HALO), east
            )
        strip[t, pl.ds(e * SUB, SUB), :] = west
        strip[t, pl.ds((eofs + e) * SUB, SUB), :] = east
    strip[t, pl.ds(2 * eofs * SUB, 4 * SUB), :] = jnp.zeros((4 * SUB, LANES), jnp.float32)


def main_kernel(
    fields, eofs, own, north, south,
    adj, strip, coeff_main, coeff_strip, wide, first, second,
):
    lane = lane_grid()
    inner = lane & (SLOT - 1)
    shifted = (lane + STEPS) & (LANES - 1)
    zero = jnp.zeros((SUB, LANES), jnp.float32)
    total = fields * eofs

    def tile(t, i):
        return (north, own, south)[t][pl.ds(i * SUB, SUB), :]

    for k in range(4):
        for t in range(3):
            cells = tile(t, total + k)
            if k < 3:
                cells = time_step * cells
            at = pl.ds(t * SUB, SUB)
            coeff_main[k, at, :] = cells
            west, east = zero, zero
            for f in range(fields):
                start = f * SLOT
                west = jnp.where(lane // SLOT == f, turn(cells, start + HALO), west)
                east = jnp.where(
                    shifted // SLOT == f, turn(cells, start - STEPS - LANES + HALO), east
                )
            coeff_strip[0, k, at, :] = jnp.where((inner >= HALO) & (inner < 2 * HALO), west, 0.0)
            coeff_strip[1, k, at, :] = jnp.where((shifted & (SLOT - 1)) < HALO, east, 0.0)
    main_coefficients(coeff_main, wide)
    groups = total // SUB
    read, write = main_rows(own, north, south, adj)
    diffuse(read, write, lambda k, w: [wide[k, w]] * groups, groups, first, second, True)
    for t in range(3):
        own_columns(fields, eofs, lambda i: tile(t, i), strip, t, lane)


def project_kernel(fields, eofs, members, eof_basis, panel, *rest):
    arrived, (basis, proj) = rest[:-2], rest[-2:]
    _, _, me = position()
    blocks = (panel,) + arrived
    count = len(blocks)
    depth = panel.shape[2] * SUB
    levels = eof_basis.shape[1]

    def grid(shape, dim):
        return lax.broadcasted_iota(jnp.int32, shape, dim)

    shape = (eofs * SUB, eofs)
    widen = (grid(shape, 0) // SUB == grid(shape, 1)).astype(jnp.bfloat16)
    shape = (levels, levels * SUB)
    spread = (grid(shape, 1) // SUB == grid(shape, 0)).astype(jnp.bfloat16)
    shape = (eofs * SUB, levels * SUB)
    same_row = grid(shape, 0) % SUB == grid(shape, 1) % SUB
    for f in range(fields):
        wide = lax.dot_general(
            widen, eof_basis[f], (((1,), (1,)), ((), ())), preferred_element_type=jnp.float32
        ).astype(jnp.bfloat16)
        wide = jnp.dot(wide, spread, preferred_element_type=jnp.float32)
        wide = jnp.where(same_row, wide, 0.0).astype(jnp.bfloat16)
        for h in range(count):
            basis[h, f] = wide[:, h * depth : (h + 1) * depth]
    for f in range(fields):
        total = None
        for s, block in enumerate(blocks):
            cells = jnp.concatenate(
                [block[m, f].reshape(depth, LANES) for m in range(members)], axis=1
            )
            part = jnp.dot(
                basis[lax.rem(me - s + count, count), f], cells, preferred_element_type=jnp.float32
            )
            total = part if total is None else total + part
        for m in range(members):
            proj[m, pl.ds(f * eofs * SUB, eofs * SUB), :] = total[:, m * LANES : (m + 1) * LANES]


def main_coefficients(coeff_main, wide):
    for k in range(4):
        for w in range(WINDOW):
            wide[k, w] = jnp.broadcast_to(coeff_main[k, pl.ds(w + 2, 1), :], (SUB, LANES))


def strip_coefficients(coeff_strip, wide_strip, eofs):
    sub = lax.broadcasted_iota(jnp.int32, (SUB, LANES), 0)
    for k in range(4):
        for w in range(WINDOW):
            west = jnp.broadcast_to(coeff_strip[0, k, pl.ds(w + 2, 1), :], (SUB, LANES))
            east = jnp.broadcast_to(coeff_strip[1, k, pl.ds(w + 2, 1), :], (SUB, LANES))
            wide_strip[k, w, pl.ds(0, SUB), :] = west
            wide_strip[k, w, pl.ds(SUB, SUB), :] = jnp.where(sub < eofs - SUB, west, east)
            wide_strip[k, w, pl.ds(2 * SUB, SUB), :] = east


def main_rows(own, north, south, out):
    def read(w, g):
        t, y = place(w)
        return (north, own, south)[t][pl.ds(g * SUB * SUB + y, SUB, stride=SUB), :]

    def write(w, g, cells):
        out[pl.ds(g * SUB * SUB + w - STEPS, SUB, stride=SUB), :] = cells

    return read, write


def strip_rows(strip, out, wide_strip):
    def read(w, g):
        t, y = place(w)
        return strip[t, pl.ds(g * SUB * SUB + y, SUB, stride=SUB), :]

    def write(w, g, cells):
        out[pl.ds(g * SUB * SUB + w - STEPS, SUB, stride=SUB), :] = cells

    def coeff(k, w):
        return [wide_strip[k, w, pl.ds(g * SUB, SUB), :] for g in range(3)]

    return read, write, coeff


def combine_kernel(fields, eofs, members, got_a, got_b, *rest):
    (
        basis, adj, proj, strip_own, coeff_own,
        out_a, out_b, combined, halo_out, coeff_strip,
        strip, wide_strip, adj_strip, panel_in, proj_strip, first, second,
    ) = rest[-17:]
    panel_parts = rest[:-17]
    ring_odd, odd, me = position()
    lane = lane_grid()
    sub = lax.broadcasted_iota(jnp.int32, (SUB, LANES), 0)
    inner = lane & (SLOT - 1)
    pair = eofs // 2

    def got(j):
        found = zip(read_pair(got_a, j), read_pair(got_b, j))
        sides = [(jnp.where(ring_odd, a, b), jnp.where(ring_odd, b, a)) for a, b in found]
        return zip(*sides)

    west_mask = inner < HALO
    east_mask = (inner >= STEPS) & (inner < STEPS + HALO)
    at16 = lane & (SLOT // 2 - 1)
    pairs = (pair + 1) // 2
    for t in range(3):
        west_tiles, east_tiles = [], []
        for j in range(pairs):
            west, east = got(t * pairs + j)
            west_tiles += west
            east_tiles += east
        for j in range(pair):
            west, east = west_tiles[j], east_tiles[j]
            west = west + jnp.where((at16 >= HALO - 4) & (at16 < HALO), turn(west, -4), 0.0)
            east = east + jnp.where(at16 < 4, turn(east, -HALO), 0.0)
            for half in range(2):
                e = half * pair + j
                at = pl.ds(e * SUB, SUB)
                strip[t, at, :] = jnp.where(
                    west_mask, turn(west, -half * (SLOT // 2)), strip_own[t, at, :]
                )
                at = pl.ds((eofs + e) * SUB, SUB)
                strip[t, at, :] = jnp.where(
                    east_mask, turn(east, STEPS - half * (SLOT // 2)), strip_own[t, at, :]
                )
        at = pl.ds(2 * eofs * SUB, 4 * SUB)
        strip[t, at, :] = strip_own[t, at, :]
        at = pl.ds(t * SUB, SUB)
        for side, (cells, mask) in enumerate(
            ((west_tiles[pair], west_mask), (east_tiles[pair], east_mask))
        ):
            cells = cells + turn(cells, -(SLOT // 2))
            for k in range(4):
                mine = jnp.where(lane // SLOT == k, cells, 0.0)
                mine = mine + turn(mine, SLOT)
                mine = mine + turn(mine, 2 * SLOT)
                if side == 1:
                    mine = turn(mine, STEPS)
                if k < 3:
                    mine = time_step * mine
                coeff_strip[side, k, at, :] = jnp.where(mask, mine, coeff_own[side, k, at, :])
    strip_coefficients(coeff_strip, wide_strip, eofs)
    read, write, coeff = strip_rows(strip, adj_strip, wide_strip)
    diffuse(read, write, coeff, 3, first, second, True)

    count, depth = basis.shape[0], basis.shape[3]
    if len(panel_parts) == 2:
        edges, far = panel_parts
        near_west, near_east, far = edges[1, 0], edges[1, 1], far[...]
        at = pl.ds(3 * pairs * 2 * SUB, depth)
        a, b = got_a[at, :], got_b[at, :]
        wests = [jnp.where(ring_odd, near_east, far), jnp.where(ring_odd, a, b)]
        easts = [jnp.where(ring_odd, far, near_west), jnp.where(ring_odd, b, a)]
    else:
        wests = [ref[...] for ref in panel_parts[:count]]
        easts = [ref[...] for ref in panel_parts[count:]]
    for s in range(count):
        panel_in[s] = jnp.concatenate([wests[s], easts[s]], axis=1)
    wide_lane = lax.broadcasted_iota(jnp.int32, (eofs * SUB, 2 * LANES), 1) & (LANES - 1)
    halo = jnp.zeros((eofs * SUB, 2 * LANES), jnp.float32)
    for f in range(fields):
        total = None
        for s in range(count):
            part = jnp.dot(
                basis[lax.rem(me + s, count), f], panel_in[s], preferred_element_type=jnp.float32
            )
            total = part if total is None else total + part
        halo = jnp.where(wide_lane // SLOT == f, total, halo)
    proj_strip[pl.ds(0, eofs * SUB), :] = halo[:, :LANES]
    proj_strip[pl.ds(eofs * SUB, eofs * SUB), :] = halo[:, LANES:]

    scores = [jnp.zeros((SUB, LANES), jnp.float32) for _ in range(members)]
    for f in range(fields):
        for e in range(eofs):
            at = pl.ds((f * eofs + e) * SUB, SUB)
            west = turn(adj_strip[pl.ds(e * SUB, SUB), :], -f * SLOT - HALO)
            east = turn(adj_strip[pl.ds((eofs + e) * SUB, SUB), :], LANES - STEPS - f * SLOT)
            cells = jnp.where(
                lane < STEPS, west, jnp.where(lane >= LANES - STEPS, east, adj[at, :])
            )
            for m in range(members):
                scores[m] = scores[m] + proj[m, at, :] * cells
    scores = [s / (members - 1) for s in scores]
    tiles = []
    for i in range(fields * eofs):
        at = pl.ds(i * SUB, SUB)
        total = proj[0, at, :] * scores[0]
        for m in range(1, members):
            total = total + proj[m, at, :] * scores[m]
        combined[at, :] = total
        tiles.append(total)

    slot = inner // SUB
    packed = [jnp.zeros((SUB, LANES), jnp.float32) for _ in range(2 * eofs // 4)]
    for side in range(2):
        total = jnp.zeros((SUB, LANES), jnp.float32)
        for e in range(eofs):
            at = pl.ds((side * eofs + e) * SUB, SUB)
            cells = adj_strip[at, :]
            spread = turn(cells, -STEPS)
            for m in range(1, members):
                spread = jnp.where(slot == m, turn(cells, m * SUB - STEPS), spread)
            total = total + proj_strip[at, :] * spread
        total = total + turn(total, SLOT)
        total = (total + turn(total, 2 * SLOT)) / (members - 1)
        for e in range(eofs):
            i = side * eofs + e
            cells = proj_strip[pl.ds(i * SUB, SUB), :] * total
            cells = cells + turn(cells, -2 * SUB)
            cells = cells + turn(cells, -SUB)
            packed[i // 4] = jnp.where(slot == i % 4, turn(cells, (i % 4) * SUB), packed[i // 4])
    for j, cells in enumerate(packed):
        halo_out[pl.ds(j * SUB, SUB), :] = cells
    tiles += packed
    if len(tiles) % 2:
        tiles.append(jnp.zeros((SUB, LANES), jnp.float32))
    put_rows(out_a, out_b, tiles, odd, sub)


def beyond_columns(eofs, packed, strip, t, lane):
    inner = lane & (SLOT - 1)
    mask = (inner >= STEPS) & (inner < HALO)
    for i in range(2 * eofs):
        cells = turn(packed[pl.ds(i // 4 * SUB, SUB), :], STEPS - (i % 4) * SUB)
        at = pl.ds(i * SUB, SUB)
        strip[t, at, :] = jnp.where(mask, cells, strip[t, at, :])


def before_forward_kernel(fields, eofs, own, halo, coeff_main, coeff_strip, wide, wide_strip, strip):
    lane = lane_grid()
    main_coefficients(coeff_main, wide)
    strip_coefficients(coeff_strip, wide_strip, eofs)
    own_columns(fields, eofs, lambda i: own[pl.ds(i * SUB, SUB), :], strip, 0, lane)
    beyond_columns(eofs, halo, strip, 0, lane)


def forward_kernel(
    fields, eofs, own, from_a, from_b, wide, wide_strip, strip_own,
    out, north, south, strip, strip_out, first, second,
):
    _, odd, _ = position()
    lane = lane_grid()
    sub = lax.broadcasted_iota(jnp.int32, (SUB, LANES), 0)
    total = fields * eofs
    for pair in range(north.shape[0] // (2 * SUB)):
        above, below = decode_rows(from_a, from_b, odd, sub, pair)
        at = pl.ds(pair * 2 * SUB, 2 * SUB)
        north[at, :] = jnp.concatenate(above, axis=0)
        south[at, :] = jnp.concatenate(below, axis=0)
    for t, ref in ((0, north), (2, south)):
        own_columns(fields, eofs, lambda i: ref[pl.ds(i * SUB, SUB), :], strip, t, lane)
        beyond_columns(eofs, ref.at[pl.ds(total * SUB, 2 * eofs // 4 * SUB)], strip, t, lane)
    strip[1] = strip_own[0]
    groups = total // SUB
    read_main, write_main = main_rows(own, north, south, out)
    read_strip, write_strip, coeff_strip = strip_rows(strip, strip_out, wide_strip)

    def read(w, g):
        return read_main(w, g) if g < groups else read_strip(w, g - groups)

    def write(w, g, cells):
        if g < groups:
            write_main(w, g, cells)
        else:
            write_strip(w, g - groups, cells)

    def coeff(k, w):
        return [wide[k, w]] * groups + coeff_strip(k, w)

    diffuse(read, write, coeff, groups + 3, first, second, False)
    for f in range(fields):
        for e in range(eofs):
            at = pl.ds((f * eofs + e) * SUB, SUB)
            west = turn(strip_out[pl.ds(e * SUB, SUB), :], -f * SLOT - HALO)
            east = turn(strip_out[pl.ds((eofs + e) * SUB, SUB), :], LANES - STEPS - f * SLOT)
            out[at, :] = jnp.where(
                lane < STEPS, west, jnp.where(lane >= LANES - STEPS, east, out[at, :])
            )


def call(kernel, args, outs, scratch=(), flops=1_000_000):
    whole = pl.BlockSpec(memory_space=pltpu.VMEM)
    moved = sum(a.size * a.dtype.itemsize for a in list(args) + list(outs))
    return pl.pallas_call(
        kernel,
        in_specs=[whole] * len(args),
        out_specs=[whole] * len(outs),
        out_shape=list(outs),
        scratch_shapes=[pltpu.VMEM(*s) for s in scratch],
        compiler_params=pltpu.CompilerParams(vmem_limit_bytes=24 * 2**20),
        cost_estimate=pl.CostEstimate(flops=flops, bytes_accessed=moved, transcendentals=0),
    )(*args)


def panel_edges_apart(edges, count, me):
    groups = lax.axis_size("gx")
    wests, easts = [], []
    for s in range(count):
        for side, into in ((1, wests), (0, easts)):
            pairs = []
            for group in range(groups):
                for held in range(count):
                    tile = (held - s) % count
                    if side == 1:
                        to = group + (tile == 0)
                    else:
                        to = group - (tile == count - 1)
                    pairs.append((group * count + held, to % groups * count + tile))
            ahead = (-s - 1) if side == 1 else (1 - s)
            into.append(lax.ppermute(edges[ahead % count, side], RING, pairs))
    return wests + easts


def per_device(panels, eof_basis, control, coefficients):
    members, fields, depth, row_count, _ = panels.shape
    _, eofs, _, col_count = control.shape
    count = lax.axis_size("gz")
    me = lax.axis_index("gz")
    total = fields * eofs
    rows = total * row_count
    f32 = lambda *shape: jax.ShapeDtypeStruct(shape, jnp.float32)
    bf16 = lambda *shape: jax.ShapeDtypeStruct(shape, jnp.bfloat16)

    all_rows = rows + 4 * row_count
    own = jnp.concatenate(
        [control.reshape(rows, col_count), coefficients.reshape(4 * row_count, col_count)]
    )
    sent_a, sent_b = call(start_kernel, [own], [bf16(all_rows, col_count)] * 2)
    from_a, from_b = swap_a(sent_a, "gy"), swap_b(sent_b, "gy", False)
    strip_sent = (eofs // 2 + 1) * row_count
    west, east, edges, *tiles = call(
        functools.partial(own_strips_kernel, fields, eofs, members),
        [own, panels],
        [bf16(strip_sent, col_count)] * 2
        + [bf16(count, 2, depth * row_count, col_count)]
        + [bf16(*panels.shape[:-1], col_count)] * count,
    )
    arrived = [
        lax.ppermute(tiles[s], "gz", [(i, (i + s) % count) for i in range(count)])
        for s in range(1, count)
    ]

    if count == 2:
        groups = lax.axis_size("gx")
        pairs = [(2 * g, (g + 1) % groups * 2) for g in range(groups)]
        pairs += [(2 * g + 1, (g - 1) % groups * 2 + 1) for g in range(groups)]
        far = lax.ppermute(jnp.where(me == 1, edges[1, 0], edges[1, 1]), RING, pairs)
        panel_sent, panel_parts = [edges], [edges, far]
    else:
        panel_sent, panel_parts = [], panel_edges_apart(edges, count, me)

    sent_a, sent_b, north, south = call(
        functools.partial(pack_kernel, fields, eofs),
        [from_a, from_b, west, east, *panel_sent],
        [bf16(3 * strip_sent + len(panel_sent) * depth * row_count, col_count)] * 2
        + [f32(rows + 4 * row_count, col_count)] * 2,
    )
    got_a, got_b = swap_a(sent_a, RING), swap_b(sent_b, RING, True)

    strip_rows = (2 * eofs + 4) * row_count
    main_scratch = [((WINDOW, total, LANES), jnp.float32)] * 2
    strip_scratch = [((WINDOW, 3 * SUB, LANES), jnp.float32)] * 2
    adj, strip, coeff_main, coeff_strip = call(
        functools.partial(main_kernel, fields, eofs),
        [own, north, south],
        [
            f32(rows, col_count),
            f32(3, strip_rows, col_count),
            f32(4, 3 * row_count, col_count),
            f32(2, 4, 3 * row_count, col_count),
        ],
        [((4, WINDOW, SUB, LANES), jnp.float32)] + main_scratch,
        flops=20_000_000,
    )
    basis, proj = call(
        functools.partial(project_kernel, fields, eofs, members),
        [eof_basis, tiles[0], *arrived],
        [
            bf16(count, fields, eofs * row_count, depth * row_count),
            f32(members, rows, col_count),
        ],
        flops=20_000_000,
    )
    packed = 2 * eofs // 4
    sent_a, sent_b, combined, halo, coeff_strip = call(
        functools.partial(combine_kernel, fields, eofs, members),
        [got_a, got_b, *panel_parts, basis, adj, proj, strip, coeff_strip],
        [bf16((total + packed + 1) // 2 * 2 * row_count, col_count)] * 2
        + [
            f32(rows, col_count),
            f32(packed * row_count, col_count),
            f32(2, 4, 3 * row_count, col_count),
        ],
        [
            ((3, strip_rows, LANES), jnp.float32),
            ((4, WINDOW, 3 * SUB, LANES), jnp.float32),
            ((strip_rows, LANES), jnp.float32),
            ((count, depth * row_count, 2 * LANES), jnp.bfloat16),
            ((2 * eofs * row_count, LANES), jnp.float32),
        ]
        + strip_scratch,
    )
    from_a, from_b = swap_a(sent_a, "gy"), swap_b(sent_b, "gy", False)
    wide, wide_strip, strip = call(
        functools.partial(before_forward_kernel, fields, eofs),
        [combined, halo, coeff_main, coeff_strip],
        [
            f32(4, WINDOW, SUB, LANES),
            f32(4, WINDOW, 3 * SUB, LANES),
            f32(1, strip_rows, LANES),
        ],
        flops=20_000_000,
    )
    (result,) = call(
        functools.partial(forward_kernel, fields, eofs),
        [combined, from_a, from_b, wide, wide_strip, strip],
        [f32(rows, col_count)],
        [((sent_a.shape[0], LANES), jnp.float32)] * 2
        + [((3, strip_rows, LANES), jnp.float32), ((strip_rows, LANES), jnp.float32)]
        + [((WINDOW, total + 3 * SUB, LANES), jnp.float32)] * 2,
    )
    return result.reshape(control.shape)


def solution(mesh):
    in_specs = (
        P(None, None, "gz", "gy", "gx"),
        P(),
        P(None, None, "gy", ("gx", "gz")),
        P(None, "gy", ("gx", "gz")),
    )
    out_specs = P(None, None, "gy", ("gx", "gz"))
    return jax.shard_map(
        per_device, mesh=mesh, in_specs=in_specs, out_specs=out_specs, check_vma=False
    )
```

```python
import functools

import jax
import jax.numpy as jnp
from jax import lax
from jax.experimental import pallas as pl
from jax.experimental.pallas import tpu as pltpu
from jax.sharding import PartitionSpec as P

STEPS = 6
LANES = 128
SUB = 8
RING = ("gx", "gz")

time_step = 0.09

WINDOW = SUB + 2 * STEPS
HALO = 2 * STEPS
SLOT = 32


def turn(cells, shift):
    return pltpu.roll(cells, shift % LANES, 1)


def swap_a(values, axes):
    count = lax.axis_size(axes)
    return lax.ppermute(values, axes, [(i, i ^ 1) for i in range(count)])


def swap_b(values, axes, closed):
    count = lax.axis_size(axes)
    pairs = [(i, i + 1) for i in range(1, count - 1, 2)]
    if closed:
        pairs.append((count - 1, 0))
    return lax.ppermute(values, axes, pairs + [(j, i) for i, j in pairs])


def place(w):
    return (w + 2) // SUB, (w + 2) % SUB


def position():
    me = lax.axis_index("gz")
    ring = lax.axis_index("gx") * lax.axis_size("gz") + me
    return lax.rem(ring, 2) == 1, lax.rem(lax.axis_index("gy"), 2) == 1, me


def lane_grid():
    return lax.broadcasted_iota(jnp.int32, (SUB, LANES), 1)


def diffuse(read, write, coeff, groups, first, second, adjoint):
    state, spare = None, first
    for step in range(STEPS):
        low, high = step, WINDOW - 1 - step

        def fetch(w):
            if state is None:
                return [read(w, g) for g in range(groups)]
            return [state[w, pl.ds(g * SUB, SUB), :] for g in range(groups)]

        here, seen, south = fetch(low), None, None
        for w in range(low, high):
            k = [coeff(i, w) for i in range(4)]
            north = fetch(w + 1)
            if adjoint:
                if seen is None:
                    seen = [k[3][g] * here[g] for g in range(groups)]
                area = coeff(3, w + 1)
                seen_north = [area[g] * north[g] for g in range(groups)]
            else:
                seen, seen_north = here, north
            flux = []
            for g in range(groups):
                east_diff = turn(seen[g], -1) - seen[g]
                north_diff = seen_north[g] - seen[g]
                flux.append(k[1][g] * east_diff + k[2][g] * north_diff)
                if w > low:
                    flux_east = k[0][g] * east_diff + k[1][g] * north_diff
                    div = (flux[g] - south[g]) + flux_east - turn(flux_east, 1)
                    moved = here[g] + (div if adjoint else k[3][g] * div)
                    if step == STEPS - 1:
                        write(w, g, moved)
                    else:
                        spare[w, pl.ds(g * SUB, SUB), :] = moved
            here, seen, south = north, seen_north, flux
        state, spare = spare, (second if spare is first else first)


def read_pair(ref, pair):
    cells = ref[pl.ds(pair * 2 * SUB, 2 * SUB), :].astype(jnp.float32)
    return cells[:SUB], cells[SUB:]


def write_pair(ref, pair, first, second):
    cells = jnp.concatenate([first, second], axis=0).astype(jnp.bfloat16)
    ref[pl.ds(pair * 2 * SUB, 2 * SUB), :] = cells


def split(cells):
    high = cells.astype(jnp.bfloat16).astype(jnp.float32)
    return high, cells - high


def encode_rows(cells, sub):
    high, low = split(cells)
    edge = SUB - STEPS
    to_north = jnp.where(sub < STEPS, high, pltpu.roll(low, STEPS, 0))
    to_south = jnp.where(sub >= edge, high, pltpu.roll(low, edge, 0))
    return to_north, to_south


def decode_rows(from_a, from_b, odd, sub, pair):
    edge = SUB - STEPS
    north, south = [], []
    for a, b in zip(read_pair(from_a, pair), read_pair(from_b, pair)):
        above, below = jnp.where(odd, a, b), jnp.where(odd, b, a)
        north.append(above + jnp.where(sub >= STEPS, pltpu.roll(above, STEPS, 0), 0.0))
        south.append(below + jnp.where(sub < edge, pltpu.roll(below, edge, 0), 0.0))
    return north, south


def start_kernel(own, out_a, out_b):
    _, odd, _ = position()
    sub = lax.broadcasted_iota(jnp.int32, (SUB, LANES), 0)
    tiles = [own[pl.ds(i * SUB, SUB), :] for i in range(own.shape[0] // SUB)]
    put_rows(out_a, out_b, tiles, odd, sub)


def put_rows(out_a, out_b, tiles, odd, sub):
    for pair in range(len(tiles) // 2):
        north, south = zip(*[encode_rows(t, sub) for t in tiles[2 * pair : 2 * pair + 2]])
        write_pair(out_a, pair, *[jnp.where(odd, n, s) for n, s in zip(north, south)])
        write_pair(out_b, pair, *[jnp.where(odd, s, n) for n, s in zip(north, south)])


def edge_columns(fields, tile, lane):
    edges = turn(tile(0), HALO)
    for f in range(1, fields):
        edges = jnp.where(lane // SLOT == f, turn(tile(f), f * SLOT + HALO), edges)
    return edges


def strip_tiles(fields, eofs, tile, lane):
    pair = eofs // 2
    west_out, east_out = [], []
    inner = lane & (SLOT - 1)
    at = lane & (SLOT // 2 - 1)
    for j in range(pair):
        first = edge_columns(fields, lambda f: tile(f * eofs + j), lane)
        second = edge_columns(fields, lambda f: tile(f * eofs + pair + j), lane)
        second = turn(second, SLOT // 2)
        west = jnp.where((inner >= HALO - 4) & (inner < 2 * HALO), first, second)
        high, low = split(west)
        west_out.append(jnp.where((at >= HALO - 4) & (at < HALO), turn(low, -4), high))
        east = jnp.where(inner < SLOT // 2, first, second)
        high, low = split(east)
        east_out.append(jnp.where(at < HALO, high, turn(low, 4)))
    edges = edge_columns(4, lambda k: tile(fields * eofs + k), lane)
    west = jnp.where((inner >= HALO) & (inner < 2 * HALO), edges, 0.0)
    east = jnp.where(inner < HALO, edges, 0.0)
    for cells, out in ((west, west_out), (east, east_out)):
        high, low = split(cells)
        out.append(high + turn(low, SLOT // 2))
    return west_out, east_out


def slice_kernel(members, fields, panels, *tiles):
    _, _, me = position()
    for s, block in enumerate(tiles):
        start = pl.multiple_of(lax.rem(me + s, len(tiles)) * LANES, LANES)
        for m in range(members):
            for f in range(fields):
                block[m, f] = panels[m, f, :, :, pl.ds(start, LANES)]


def own_strips_kernel(fields, eofs, members, own, eof_basis, *rest):
    tiles, (west, east, edges, basis) = rest[:-4], rest[-4:]
    lane = lane_grid()

    def tile(i):
        return own[pl.ds(i * SUB, SUB), :]

    for ref, packed in zip((west, east), strip_tiles(fields, eofs, tile, lane)):
        for pair in range(len(packed) // 2):
            write_pair(ref, pair, *packed[2 * pair : 2 * pair + 2])

    count = len(tiles)
    depth = tiles[0].shape[2] * SUB
    column = lax.broadcasted_iota(jnp.int32, (LANES, 2 * LANES), 0)
    target = lax.broadcasted_iota(jnp.int32, (LANES, 2 * LANES), 1)
    west_ok = (target < LANES) & (column < STEPS)
    east_ok = (target >= LANES) & (column >= LANES - STEPS)
    offset = jnp.where(
        west_ok,
        target - column,
        jnp.where(east_ok, target - LANES - column + LANES - STEPS, -1),
    )
    for s, block in enumerate(tiles):
        total = jnp.zeros((depth, 2 * LANES), jnp.float32)
        for m in range(members):
            for f in range(fields):
                pick = (offset == f * SLOT + m * SUB).astype(jnp.bfloat16)
                total += jnp.dot(
                    block[m, f].reshape(depth, LANES), pick, preferred_element_type=jnp.float32
                )
        total = total.astype(jnp.bfloat16)
        edges[s, 0] = total[:, :LANES]
        edges[s, 1] = total[:, LANES:]

    levels = eof_basis.shape[1]

    def grid(shape, dim):
        return lax.broadcasted_iota(jnp.int32, shape, dim)

    shape = (eofs * SUB, eofs)
    widen = (grid(shape, 0) // SUB == grid(shape, 1)).astype(jnp.bfloat16)
    shape = (levels, levels * SUB)
    spread = (grid(shape, 1) // SUB == grid(shape, 0)).astype(jnp.bfloat16)
    shape = (eofs * SUB, levels * SUB)
    same_row = grid(shape, 0) % SUB == grid(shape, 1) % SUB
    for f in range(fields):
        wide = lax.dot_general(
            widen, eof_basis[f], (((1,), (1,)), ((), ())), preferred_element_type=jnp.float32
        ).astype(jnp.bfloat16)
        wide = jnp.dot(wide, spread, preferred_element_type=jnp.float32)
        wide = jnp.where(same_row, wide, 0.0).astype(jnp.bfloat16)
        for h in range(count):
            basis[h, f] = wide[:, h * depth : (h + 1) * depth]


def pack_kernel(fields, eofs, from_a, from_b, west, east, *rest):
    panel_edges, (out_a, out_b, north, south) = rest[:-4], rest[-4:]
    ring_odd, odd, _ = position()
    lane = lane_grid()
    sub = lax.broadcasted_iota(jnp.int32, (SUB, LANES), 0)
    for pair in range((fields * eofs + 4) // 2):
        above, below = decode_rows(from_a, from_b, odd, sub, pair)
        at = pl.ds(pair * 2 * SUB, 2 * SUB)
        north[at, :] = jnp.concatenate(above, axis=0)
        south[at, :] = jnp.concatenate(below, axis=0)

    def put(pair, mine_west, mine_east):
        write_pair(out_a, pair, *[jnp.where(ring_odd, w, e) for w, e in zip(mine_west, mine_east)])
        write_pair(out_b, pair, *[jnp.where(ring_odd, e, w) for w, e in zip(mine_west, mine_east)])

    pairs = (eofs // 2 + 1) // 2
    for t, ref in ((0, north), (2, south)):
        tiles = strip_tiles(fields, eofs, lambda i: ref[pl.ds(i * SUB, SUB), :], lane)
        for j in range(pairs):
            put(t * pairs + j, tiles[0][2 * j : 2 * j + 2], tiles[1][2 * j : 2 * j + 2])
    for j in range(pairs):
        put(pairs + j, read_pair(west, j), read_pair(east, j))
    for edges in panel_edges[:1]:
        for j in range(edges.shape[2] // (2 * SUB)):
            put(3 * pairs + j, read_pair(edges.at[0, 0], j), read_pair(edges.at[0, 1], j))


def main_kernel(
    fields, eofs, own, north, south,
    adj, strip, coeff_main, coeff_strip, wide, first, second,
):
    lane = lane_grid()
    inner = lane & (SLOT - 1)
    total = fields * eofs

    def tile(t, i):
        return (north, own, south)[t][pl.ds(i * SUB, SUB), :]

    for k in range(4):
        for t in range(3):
            cells = tile(t, total + k)
            if k < 3:
                cells = time_step * cells
            at = pl.ds(t * SUB, SUB)
            coeff_main[k, at, :] = cells
            edges = edge_columns(fields, lambda f: cells, lane)
            west = (inner >= HALO) & (inner < 2 * HALO)
            coeff_strip[0, k, at, :] = jnp.where(west, edges, 0.0)
            coeff_strip[1, k, at, :] = jnp.where(inner < HALO, edges, 0.0)
    main_coefficients(coeff_main, wide)
    groups = total // SUB
    read, write = main_rows(own, north, south, adj)
    diffuse(read, write, lambda k, w: [wide[k, w]] * groups, groups, first, second, True)
    for t in range(3):
        for e in range(eofs):
            strip[t, pl.ds(e * SUB, SUB), :] = edge_columns(
                fields, lambda f: tile(t, f * eofs + e), lane
            )


def project_kernel(fields, eofs, members, basis, panel, *rest):
    arrived, proj = rest[:-1], rest[-1]
    _, _, me = position()
    blocks = (panel,) + arrived
    count = len(blocks)
    depth = panel.shape[2] * SUB
    for f in range(fields):
        total = None
        for s, block in enumerate(blocks):
            cells = jnp.concatenate(
                [block[m, f].reshape(depth, LANES) for m in range(members)], axis=1
            )
            part = jnp.dot(
                basis[lax.rem(me - s + count, count), f], cells, preferred_element_type=jnp.float32
            )
            total = part if total is None else total + part
        for m in range(members):
            proj[m, pl.ds(f * eofs * SUB, eofs * SUB), :] = total[:, m * LANES : (m + 1) * LANES]


def main_coefficients(coeff_main, wide):
    for k in range(4):
        for w in range(WINDOW):
            wide[k, w] = jnp.broadcast_to(coeff_main[k, pl.ds(w + 2, 1), :], (SUB, LANES))


def strip_coefficients(coeff_strip, wide_strip, eofs):
    sub = lax.broadcasted_iota(jnp.int32, (SUB, LANES), 0)
    for k in range(4):
        for w in range(WINDOW):
            west = jnp.broadcast_to(coeff_strip[0, k, pl.ds(w + 2, 1), :], (SUB, LANES))
            east = jnp.broadcast_to(coeff_strip[1, k, pl.ds(w + 2, 1), :], (SUB, LANES))
            wide_strip[k, w, pl.ds(0, SUB), :] = west
            wide_strip[k, w, pl.ds(SUB, SUB), :] = jnp.where(sub < eofs - SUB, west, east)
            wide_strip[k, w, pl.ds(2 * SUB, SUB), :] = east


def main_rows(own, north, south, out):
    def read(w, g):
        t, y = place(w)
        return (north, own, south)[t][pl.ds(g * SUB * SUB + y, SUB, stride=SUB), :]

    def write(w, g, cells):
        out[pl.ds(g * SUB * SUB + w - STEPS, SUB, stride=SUB), :] = cells

    return read, write


def strip_rows(strip, out, wide_strip):
    def read(w, g):
        t, y = place(w)
        return strip[t, pl.ds(g * SUB * SUB + y, SUB, stride=SUB), :]

    def write(w, g, cells):
        out[pl.ds(g * SUB * SUB + w - STEPS, SUB, stride=SUB), :] = cells

    def coeff(k, w):
        return [wide_strip[k, w, pl.ds(g * SUB, SUB), :] for g in range(3)]

    return read, write, coeff


def combine_kernel(fields, eofs, members, got_a, got_b, *rest):
    (
        basis, adj, proj, strip_own, coeff_own,
        out_a, out_b, combined, halo_out, coeff_strip,
        strip, wide_strip, adj_strip, panel_in, proj_strip, first, second,
    ) = rest[-17:]
    panel_parts = rest[:-17]
    ring_odd, odd, me = position()
    lane = lane_grid()
    sub = lax.broadcasted_iota(jnp.int32, (SUB, LANES), 0)
    inner = lane & (SLOT - 1)
    pair = eofs // 2

    def got(j):
        found = zip(read_pair(got_a, j), read_pair(got_b, j))
        sides = [(jnp.where(ring_odd, a, b), jnp.where(ring_odd, b, a)) for a, b in found]
        return zip(*sides)

    west_mask = inner < HALO
    east_mask = (inner >= HALO) & (inner < 2 * HALO)
    at16 = lane & (SLOT // 2 - 1)
    pairs = (pair + 1) // 2
    for t in range(3):
        west_tiles, east_tiles = [], []
        for j in range(pairs):
            west, east = got(t * pairs + j)
            west_tiles += west
            east_tiles += east
        for j in range(pair):
            west, east = west_tiles[j], east_tiles[j]
            west = west + jnp.where((at16 >= HALO - 4) & (at16 < HALO), turn(west, -4), 0.0)
            east = east + jnp.where(at16 >= HALO, turn(east, 4), 0.0)
            for half in range(2):
                e = half * pair + j
                mine = strip_own[t, pl.ds(e * SUB, SUB), :]
                if half:
                    west, east = turn(west, -(SLOT // 2)), turn(east, -(SLOT // 2))
                strip[t, pl.ds(e * SUB, SUB), :] = jnp.where(west_mask, west, mine)
                strip[t, pl.ds((eofs + e) * SUB, SUB), :] = jnp.where(east_mask, east, mine)
        strip[t, pl.ds(2 * eofs * SUB, 4 * SUB), :] = jnp.zeros((4 * SUB, LANES), jnp.float32)
        at = pl.ds(t * SUB, SUB)
        for side, (cells, mask) in enumerate(
            ((west_tiles[pair], west_mask), (east_tiles[pair], east_mask))
        ):
            cells = cells + turn(cells, -(SLOT // 2))
            turned = [cells] + [turn(cells, i * SLOT) for i in range(1, 4)]
            for k in range(4):
                mine = turned[-k % 4]
                for f in range(1, 4):
                    mine = jnp.where(lane // SLOT == f, turned[(f - k) % 4], mine)
                if k < 3:
                    mine = time_step * mine
                coeff_strip[side, k, at, :] = jnp.where(mask, mine, coeff_own[side, k, at, :])
    strip_coefficients(coeff_strip, wide_strip, eofs)
    read, write, coeff = strip_rows(strip, adj_strip, wide_strip)
    diffuse(read, write, coeff, 3, first, second, True)

    count, depth = basis.shape[0], basis.shape[3]
    if len(panel_parts) == 2:
        edges, far = panel_parts
        near_west, near_east, far = edges[1, 0], edges[1, 1], far[...]
        at = pl.ds(3 * pairs * 2 * SUB, depth)
        a, b = got_a[at, :], got_b[at, :]
        wests = [jnp.where(ring_odd, near_east, far), jnp.where(ring_odd, a, b)]
        easts = [jnp.where(ring_odd, far, near_west), jnp.where(ring_odd, b, a)]
    else:
        wests = [ref[...] for ref in panel_parts[:count]]
        easts = [ref[...] for ref in panel_parts[count:]]
    for s in range(count):
        panel_in[s] = jnp.concatenate([wests[s], easts[s]], axis=1)
    wide_lane = lax.broadcasted_iota(jnp.int32, (eofs * SUB, 2 * LANES), 1) & (LANES - 1)
    halo = jnp.zeros((eofs * SUB, 2 * LANES), jnp.float32)
    for f in range(fields):
        total = None
        for s in range(count):
            part = jnp.dot(
                basis[lax.rem(me + s, count), f], panel_in[s], preferred_element_type=jnp.float32
            )
            total = part if total is None else total + part
        halo = jnp.where(wide_lane // SLOT == f, total, halo)
    proj_strip[pl.ds(0, eofs * SUB), :] = halo[:, :LANES]
    proj_strip[pl.ds(eofs * SUB, eofs * SUB), :] = halo[:, LANES:]

    scores = [jnp.zeros((SUB, LANES), jnp.float32) for _ in range(members)]
    for e in range(eofs):
        edges = both_edges(eofs, adj_strip, e, inner)
        for f in range(fields):
            at = pl.ds((f * eofs + e) * SUB, SUB)
            cells = jnp.where(own_edge(lane), turn(edges, -f * SLOT - HALO), adj[at, :])
            for m in range(members):
                scores[m] = scores[m] + proj[m, at, :] * cells
    scores = [s / (members - 1) for s in scores]
    tiles = []
    for i in range(fields * eofs):
        at = pl.ds(i * SUB, SUB)
        total = proj[0, at, :] * scores[0]
        for m in range(1, members):
            total = total + proj[m, at, :] * scores[m]
        combined[at, :] = total
        tiles.append(total)

    slot = inner // SUB
    packed = [jnp.zeros((SUB, LANES), jnp.float32) for _ in range(2 * eofs // 4)]
    for side in range(2):
        total = jnp.zeros((SUB, LANES), jnp.float32)
        for e in range(eofs):
            at = pl.ds((side * eofs + e) * SUB, SUB)
            cells = adj_strip[at, :]
            start = HALO if side else STEPS
            spread = turn(cells, -start)
            for m in range(1, members):
                spread = jnp.where(slot == m, turn(cells, m * SUB - start), spread)
            total = total + proj_strip[at, :] * spread
        total = total + turn(total, SLOT)
        total = (total + turn(total, 2 * SLOT)) / (members - 1)
        for e in range(eofs):
            i = side * eofs + e
            cells = proj_strip[pl.ds(i * SUB, SUB), :] * total
            cells = cells + turn(cells, -2 * SUB)
            cells = cells + turn(cells, -SUB)
            packed[i // 4] = jnp.where(slot == i % 4, turn(cells, (i % 4) * SUB), packed[i // 4])
    for j, cells in enumerate(packed):
        halo_out[pl.ds(j * SUB, SUB), :] = cells
    tiles += packed
    if len(tiles) % 2:
        tiles.append(jnp.zeros((SUB, LANES), jnp.float32))
    put_rows(out_a, out_b, tiles, odd, sub)


def both_edges(eofs, strip, e, inner):
    west, east = strip[pl.ds(e * SUB, SUB), :], strip[pl.ds((eofs + e) * SUB, SUB), :]
    return jnp.where(inner < HALO, east, west)


def own_edge(lane):
    return (lane < STEPS) | (lane >= LANES - STEPS)


def fill_strip(fields, eofs, tile, packed, strip, t, lane):
    inner = lane & (SLOT - 1)
    west = (inner >= STEPS) & (inner < HALO)
    east = (inner >= HALO) & (inner < HALO + STEPS)
    for e in range(eofs):
        edges = edge_columns(fields, lambda f: tile(f * eofs + e), lane)
        for side, mask in enumerate((west, east)):
            i = side * eofs + e
            shift = (HALO if side else STEPS) - (i % 4) * SUB
            beyond = turn(packed[pl.ds(i // 4 * SUB, SUB), :], shift)
            strip[t, pl.ds(i * SUB, SUB), :] = jnp.where(mask, beyond, edges)
    strip[t, pl.ds(2 * eofs * SUB, 4 * SUB), :] = jnp.zeros((4 * SUB, LANES), jnp.float32)


def before_forward_kernel(fields, eofs, own, halo, coeff_main, coeff_strip, wide, wide_strip, strip):
    lane = lane_grid()
    main_coefficients(coeff_main, wide)
    strip_coefficients(coeff_strip, wide_strip, eofs)
    fill_strip(fields, eofs, lambda i: own[pl.ds(i * SUB, SUB), :], halo, strip, 0, lane)


def forward_kernel(
    fields, eofs, own, from_a, from_b, wide, wide_strip, strip_own,
    result, out, north, south, strip, strip_out, first, second, sems,
):
    _, odd, _ = position()
    lane = lane_grid()
    sub = lax.broadcasted_iota(jnp.int32, (SUB, LANES), 0)
    total = fields * eofs
    for pair in range(north.shape[0] // (2 * SUB)):
        above, below = decode_rows(from_a, from_b, odd, sub, pair)
        at = pl.ds(pair * 2 * SUB, 2 * SUB)
        north[at, :] = jnp.concatenate(above, axis=0)
        south[at, :] = jnp.concatenate(below, axis=0)
    for t, ref in ((0, north), (2, south)):
        packed = ref.at[pl.ds(total * SUB, 2 * eofs // 4 * SUB)]
        fill_strip(
            fields, eofs, lambda i: ref[pl.ds(i * SUB, SUB), :], packed, strip, t, lane
        )
    strip[1] = strip_own[0]
    groups = total // SUB
    read_main, write_main = main_rows(own, north, south, out)
    read_strip, write_strip, coeff_strip = strip_rows(strip, strip_out, wide_strip)

    def read(w, g):
        return read_strip(w, g) if g < 3 else read_main(w, g - 3)

    def write(w, g, cells):
        if g < 3:
            write_strip(w, g, cells)
        else:
            write_main(w, g - 3, cells)

    def coeff(k, w):
        return coeff_strip(k, w) + [wide[k, w]] * groups

    diffuse(read, write, coeff, groups + 3, first, second, False)
    edges = [both_edges(eofs, strip_out, e, lane & (SLOT - 1)) for e in range(eofs)]
    copies = []
    for f in range(fields):
        for e in range(eofs):
            at = pl.ds((f * eofs + e) * SUB, SUB)
            out[at, :] = jnp.where(own_edge(lane), turn(edges[e], -f * SLOT - HALO), out[at, :])
        part = pl.ds(f * eofs * SUB, eofs * SUB)
        copies.append(pltpu.make_async_copy(out.at[part], result.at[part], sems.at[f]))
        copies[-1].start()
    for copy in copies:
        copy.wait()


def call(kernel, args, outs, scratch=(), flops=1_000_000, out_space=pltpu.VMEM):
    whole = pl.BlockSpec(memory_space=pltpu.VMEM)
    moved = sum(a.size * a.dtype.itemsize for a in list(args) + list(outs))
    return pl.pallas_call(
        kernel,
        in_specs=[whole] * len(args),
        out_specs=[pl.BlockSpec(memory_space=out_space)] * len(outs),
        out_shape=list(outs),
        scratch_shapes=[pltpu.VMEM(*s) if isinstance(s, tuple) else s for s in scratch],
        compiler_params=pltpu.CompilerParams(vmem_limit_bytes=24 * 2**20),
        cost_estimate=pl.CostEstimate(flops=flops, bytes_accessed=moved, transcendentals=0),
    )(*args)


def panel_edges_apart(edges, count, me):
    groups = lax.axis_size("gx")
    wests, easts = [], []
    for s in range(count):
        for side, into in ((1, wests), (0, easts)):
            pairs = []
            for group in range(groups):
                for held in range(count):
                    tile = (held - s) % count
                    if side == 1:
                        to = group + (tile == 0)
                    else:
                        to = group - (tile == count - 1)
                    pairs.append((group * count + held, to % groups * count + tile))
            ahead = (-s - 1) if side == 1 else (1 - s)
            into.append(lax.ppermute(edges[ahead % count, side], RING, pairs))
    return wests + easts


def per_device(panels, eof_basis, control, coefficients):
    members, fields, depth, row_count, _ = panels.shape
    _, eofs, _, col_count = control.shape
    count = lax.axis_size("gz")
    me = lax.axis_index("gz")
    total = fields * eofs
    rows = total * row_count
    f32 = lambda *shape: jax.ShapeDtypeStruct(shape, jnp.float32)
    bf16 = lambda *shape: jax.ShapeDtypeStruct(shape, jnp.bfloat16)

    all_rows = rows + 4 * row_count
    own = jnp.concatenate(
        [control.reshape(rows, col_count), coefficients.reshape(4 * row_count, col_count)]
    )
    sent_a, sent_b = call(start_kernel, [own], [bf16(all_rows, col_count)] * 2)
    from_a, from_b = swap_a(sent_a, "gy"), swap_b(sent_b, "gy", False)
    strip_sent = (eofs // 2 + 1) * row_count
    tiles = call(
        functools.partial(slice_kernel, members, fields),
        [panels],
        [bf16(*panels.shape[:-1], col_count)] * count,
    )
    west, east, edges, basis = call(
        functools.partial(own_strips_kernel, fields, eofs, members),
        [own, eof_basis, *tiles],
        [bf16(strip_sent, col_count)] * 2
        + [
            bf16(count, 2, depth * row_count, col_count),
            bf16(count, fields, eofs * row_count, depth * row_count),
        ],
    )
    arrived = [
        lax.ppermute(tiles[s], "gz", [(i, (i + s) % count) for i in range(count)])
        for s in range(1, count)
    ]

    if count == 2:
        groups = lax.axis_size("gx")
        pairs = [(2 * g, (g + 1) % groups * 2) for g in range(groups)]
        pairs += [(2 * g + 1, (g - 1) % groups * 2 + 1) for g in range(groups)]
        far = lax.ppermute(jnp.where(me == 1, edges[1, 0], edges[1, 1]), RING, pairs)
        panel_sent, panel_parts = [edges], [edges, far]
    else:
        panel_sent, panel_parts = [], panel_edges_apart(edges, count, me)

    sent_a, sent_b, north, south = call(
        functools.partial(pack_kernel, fields, eofs),
        [from_a, from_b, west, east, *panel_sent],
        [bf16(3 * strip_sent + (count == 2) * depth * row_count, col_count)] * 2
        + [f32(rows + 4 * row_count, col_count)] * 2,
    )
    got_a, got_b = swap_a(sent_a, RING), swap_b(sent_b, RING, True)

    strip_rows = (2 * eofs + 4) * row_count
    main_scratch = [((WINDOW, total, LANES), jnp.float32)] * 2
    strip_scratch = [((WINDOW, 3 * SUB, LANES), jnp.float32)] * 2
    adj, strip, coeff_main, coeff_strip = call(
        functools.partial(main_kernel, fields, eofs),
        [own, north, south],
        [
            f32(rows, col_count),
            f32(3, eofs * row_count, col_count),
            f32(4, 3 * row_count, col_count),
            f32(2, 4, 3 * row_count, col_count),
        ],
        [((4, WINDOW, SUB, LANES), jnp.float32)] + main_scratch,
        flops=20_000_000,
    )
    (proj,) = call(
        functools.partial(project_kernel, fields, eofs, members),
        [basis, tiles[0], *arrived],
        [f32(members, rows, col_count)],
        flops=20_000_000,
    )
    packed = 2 * eofs // 4
    sent_a, sent_b, combined, halo, coeff_strip = call(
        functools.partial(combine_kernel, fields, eofs, members),
        [got_a, got_b, *panel_parts, basis, adj, proj, strip, coeff_strip],
        [bf16((total + packed + 1) // 2 * 2 * row_count, col_count)] * 2
        + [
            f32(rows, col_count),
            f32(packed * row_count, col_count),
            f32(2, 4, 3 * row_count, col_count),
        ],
        [
            ((3, strip_rows, LANES), jnp.float32),
            ((4, WINDOW, 3 * SUB, LANES), jnp.float32),
            ((strip_rows, LANES), jnp.float32),
            ((count, depth * row_count, 2 * LANES), jnp.bfloat16),
            ((2 * eofs * row_count, LANES), jnp.float32),
        ]
        + strip_scratch,
    )
    from_a, from_b = swap_a(sent_a, "gy"), swap_b(sent_b, "gy", False)
    wide, wide_strip, strip = call(
        functools.partial(before_forward_kernel, fields, eofs),
        [combined, halo, coeff_main, coeff_strip],
        [
            f32(4, WINDOW, SUB, LANES),
            f32(4, WINDOW, 3 * SUB, LANES),
            f32(1, strip_rows, LANES),
        ],
        flops=20_000_000,
    )
    (result,) = call(
        functools.partial(forward_kernel, fields, eofs),
        [combined, from_a, from_b, wide, wide_strip, strip],
        [f32(rows, col_count)],
        [((rows, LANES), jnp.float32)]
        + [((sent_a.shape[0], LANES), jnp.float32)] * 2
        + [((3, strip_rows, LANES), jnp.float32), ((strip_rows, LANES), jnp.float32)]
        + [((WINDOW, total + 3 * SUB, LANES), jnp.float32)] * 2
        + [pltpu.SemaphoreType.DMA((fields,))],
        out_space=pltpu.HBM,
    )
    return result.reshape(control.shape)


def solution(mesh):
    in_specs = (
        P(None, None, "gz", "gy", "gx"),
        P(),
        P(None, None, "gy", ("gx", "gz")),
        P(None, "gy", ("gx", "gz")),
    )
    out_specs = P(None, None, "gy", ("gx", "gz"))
    return jax.shard_map(
        per_device, mesh=mesh, in_specs=in_specs, out_specs=out_specs, check_vma=False
    )
```

```python
import functools

import jax
import jax.numpy as jnp
from jax import lax
from jax.experimental import pallas as pl
from jax.experimental.pallas import tpu as pltpu
from jax.sharding import PartitionSpec as P

STEPS = 6
LANES = 128
SUB = 8
RING = ("gx", "gz")

time_step = 0.09

WINDOW = SUB + 2 * STEPS
HALO = 2 * STEPS
SLOT = 32


def turn(cells, shift):
    return pltpu.roll(cells, shift % LANES, 1)


def swap_a(values, axes):
    count = lax.axis_size(axes)
    return lax.ppermute(values, axes, [(i, i ^ 1) for i in range(count)])


def swap_b(values, axes, closed):
    count = lax.axis_size(axes)
    pairs = [(i, i + 1) for i in range(1, count - 1, 2)]
    if closed:
        pairs.append((count - 1, 0))
    return lax.ppermute(values, axes, pairs + [(j, i) for i, j in pairs])


def place(w):
    return (w + 2) // SUB, (w + 2) % SUB


def position():
    me = lax.axis_index("gz")
    ring = lax.axis_index("gx") * lax.axis_size("gz") + me
    return lax.rem(ring, 2) == 1, lax.rem(lax.axis_index("gy"), 2) == 1, me


def lane_grid():
    return lax.broadcasted_iota(jnp.int32, (SUB, LANES), 1)


def early_rows(step):
    rows = range(STEPS + 1 + step, STEPS + SUB - 1 - step)
    return rows, sum(len(early_rows(s)[0]) for s in range(step))


def diffuse_early(read, coeff, groups, kept, kept_flux):
    step = 0
    while len(early_rows(step)[0]):
        rows, base = early_rows(step)
        last_rows, last_base = early_rows(step - 1)

        def fetch(w):
            if step == 0:
                return [read(w, g) for g in range(groups)]
            at = last_base + w - last_rows[0]
            return [kept[at, pl.ds(g * SUB, SUB), :] for g in range(groups)]

        here, south = fetch(rows[0] - 1), None
        for w in range(rows[0] - 1, rows[-1] + 1):
            k = [coeff(i, w) for i in range(4)]
            north = fetch(w + 1)
            flux = []
            for g in range(groups):
                east_diff = turn(here[g], -1) - here[g]
                north_diff = north[g] - here[g]
                flux.append(k[1][g] * east_diff + k[2][g] * north_diff)
                if w in rows:
                    flux_east = k[0][g] * east_diff + k[1][g] * north_diff
                    div = (flux[g] - south[g]) + flux_east - turn(flux_east, 1)
                    kept[base + w - rows[0], pl.ds(g * SUB, SUB), :] = here[g] + k[3][g] * div
                if w == rows[-1]:
                    kept_flux[step, pl.ds(g * SUB, SUB), :] = flux[g]
            here, south = north, flux
        step += 1


def diffuse(read, write, coeff, groups, first, second, adjoint, early=None):
    state, spare = None, first
    made = range(0)
    for step in range(STEPS):
        low, high = step, WINDOW - 1 - step
        last, made = made, early_rows(step)[0] if early else range(0)

        def fetch(w):
            if state is None:
                return [read(w, g) for g in range(groups)]
            if w in last:
                at = early_rows(step - 1)[1] + w - last[0]
                return [early[0][at, pl.ds(g * SUB, SUB), :] for g in range(groups)]
            return [state[w, pl.ds(g * SUB, SUB), :] for g in range(groups)]

        here, seen, south = fetch(low), None, None
        for w in range(low, high):
            if w in made:
                if w == made[-1]:
                    here = fetch(w + 1)
                    south = [early[1][step, pl.ds(g * SUB, SUB), :] for g in range(groups)]
                continue
            k = [coeff(i, w) for i in range(4)]
            north = fetch(w + 1)
            if adjoint:
                if seen is None:
                    seen = [k[3][g] * here[g] for g in range(groups)]
                area = coeff(3, w + 1)
                seen_north = [area[g] * north[g] for g in range(groups)]
            else:
                seen, seen_north = here, north
            flux = []
            for g in range(groups):
                east_diff = turn(seen[g], -1) - seen[g]
                north_diff = seen_north[g] - seen[g]
                flux.append(k[1][g] * east_diff + k[2][g] * north_diff)
                if w > low:
                    flux_east = k[0][g] * east_diff + k[1][g] * north_diff
                    div = (flux[g] - south[g]) + flux_east - turn(flux_east, 1)
                    moved = here[g] + (div if adjoint else k[3][g] * div)
                    if step == STEPS - 1:
                        write(w, g, moved)
                    else:
                        spare[w, pl.ds(g * SUB, SUB), :] = moved
            here, seen, south = north, seen_north, flux
        state, spare = spare, (second if spare is first else first)


def read_pair(ref, pair):
    cells = ref[pl.ds(pair * 2 * SUB, 2 * SUB), :].astype(jnp.float32)
    return cells[:SUB], cells[SUB:]


def write_pair(ref, pair, first, second):
    cells = jnp.concatenate([first, second], axis=0).astype(jnp.bfloat16)
    ref[pl.ds(pair * 2 * SUB, 2 * SUB), :] = cells


def split(cells):
    high = cells.astype(jnp.bfloat16).astype(jnp.float32)
    return high, cells - high


def encode_rows(cells, sub):
    high, low = split(cells)
    edge = SUB - STEPS
    to_north = jnp.where(sub < STEPS, high, pltpu.roll(low, STEPS, 0))
    to_south = jnp.where(sub >= edge, high, pltpu.roll(low, edge, 0))
    return to_north, to_south


def decode_rows(from_a, from_b, odd, sub, pair):
    edge = SUB - STEPS
    north, south = [], []
    for a, b in zip(read_pair(from_a, pair), read_pair(from_b, pair)):
        above, below = jnp.where(odd, a, b), jnp.where(odd, b, a)
        north.append(above + jnp.where(sub >= STEPS, pltpu.roll(above, STEPS, 0), 0.0))
        south.append(below + jnp.where(sub < edge, pltpu.roll(below, edge, 0), 0.0))
    return north, south


def start_kernel(own, out_a, out_b):
    _, odd, _ = position()
    sub = lax.broadcasted_iota(jnp.int32, (SUB, LANES), 0)
    tiles = [own[pl.ds(i * SUB, SUB), :] for i in range(own.shape[0] // SUB)]
    put_rows(out_a, out_b, tiles, odd, sub)


def put_rows(out_a, out_b, tiles, odd, sub):
    for pair in range(len(tiles) // 2):
        north, south = zip(*[encode_rows(t, sub) for t in tiles[2 * pair : 2 * pair + 2]])
        write_pair(out_a, pair, *[jnp.where(odd, n, s) for n, s in zip(north, south)])
        write_pair(out_b, pair, *[jnp.where(odd, s, n) for n, s in zip(north, south)])


def edge_columns(fields, tile, lane):
    edges = turn(tile(0), HALO)
    for f in range(1, fields):
        edges = jnp.where(lane // SLOT == f, turn(tile(f), f * SLOT + HALO), edges)
    return edges


def strip_tiles(fields, eofs, tile, lane):
    pair = eofs // 2
    west_out, east_out = [], []
    inner = lane & (SLOT - 1)
    at = lane & (SLOT // 2 - 1)
    for j in range(pair):
        first = edge_columns(fields, lambda f: tile(f * eofs + j), lane)
        second = edge_columns(fields, lambda f: tile(f * eofs + pair + j), lane)
        second = turn(second, SLOT // 2)
        west = jnp.where((inner >= HALO - 4) & (inner < 2 * HALO), first, second)
        high, low = split(west)
        west_out.append(jnp.where((at >= HALO - 4) & (at < HALO), turn(low, -4), high))
        east = jnp.where(inner < SLOT // 2, first, second)
        high, low = split(east)
        east_out.append(jnp.where(at < HALO, high, turn(low, 4)))
    edges = edge_columns(4, lambda k: tile(fields * eofs + k), lane)
    west = jnp.where((inner >= HALO) & (inner < 2 * HALO), edges, 0.0)
    east = jnp.where(inner < HALO, edges, 0.0)
    for cells, out in ((west, west_out), (east, east_out)):
        high, low = split(cells)
        out.append(high + turn(low, SLOT // 2))
    return west_out, east_out


def slice_kernel(members, fields, panels, *tiles):
    _, _, me = position()
    for s, block in enumerate(tiles):
        start = pl.multiple_of(lax.rem(me + s, len(tiles)) * LANES, LANES)
        for m in range(members):
            for f in range(fields):
                block[m, f] = panels[m, f, :, :, pl.ds(start, LANES)]


def own_strips_kernel(fields, eofs, members, own, eof_basis, *rest):
    tiles, (west, east, edges, basis) = rest[:-4], rest[-4:]
    lane = lane_grid()

    def tile(i):
        return own[pl.ds(i * SUB, SUB), :]

    for ref, packed in zip((west, east), strip_tiles(fields, eofs, tile, lane)):
        for pair in range(len(packed) // 2):
            write_pair(ref, pair, *packed[2 * pair : 2 * pair + 2])

    count = len(tiles)
    depth = tiles[0].shape[2] * SUB
    column = lax.broadcasted_iota(jnp.int32, (LANES, 2 * LANES), 0)
    target = lax.broadcasted_iota(jnp.int32, (LANES, 2 * LANES), 1)
    west_ok = (target < LANES) & (column < STEPS)
    east_ok = (target >= LANES) & (column >= LANES - STEPS)
    offset = jnp.where(
        west_ok,
        target - column,
        jnp.where(east_ok, target - LANES - column + LANES - STEPS, -1),
    )
    for s, block in enumerate(tiles):
        total = jnp.zeros((depth, 2 * LANES), jnp.float32)
        for m in range(members):
            for f in range(fields):
                pick = (offset == f * SLOT + m * SUB).astype(jnp.bfloat16)
                total += jnp.dot(
                    block[m, f].reshape(depth, LANES), pick, preferred_element_type=jnp.float32
                )
        total = total.astype(jnp.bfloat16)
        edges[s, 0] = total[:, :LANES]
        edges[s, 1] = total[:, LANES:]

    levels = eof_basis.shape[1]

    def grid(shape, dim):
        return lax.broadcasted_iota(jnp.int32, shape, dim)

    shape = (eofs * SUB, eofs)
    widen = (grid(shape, 0) // SUB == grid(shape, 1)).astype(jnp.bfloat16)
    shape = (levels, levels * SUB)
    spread = (grid(shape, 1) // SUB == grid(shape, 0)).astype(jnp.bfloat16)
    shape = (eofs * SUB, levels * SUB)
    same_row = grid(shape, 0) % SUB == grid(shape, 1) % SUB
    for f in range(fields):
        wide = lax.dot_general(
            widen, eof_basis[f], (((1,), (1,)), ((), ())), preferred_element_type=jnp.float32
        ).astype(jnp.bfloat16)
        wide = jnp.dot(wide, spread, preferred_element_type=jnp.float32)
        wide = jnp.where(same_row, wide, 0.0).astype(jnp.bfloat16)
        for h in range(count):
            basis[h, f] = wide[:, h * depth : (h + 1) * depth]


def pack_kernel(fields, eofs, from_a, from_b, west, east, *rest):
    panel_edges, (out_a, out_b, north, south) = rest[:-4], rest[-4:]
    ring_odd, odd, _ = position()
    lane = lane_grid()
    sub = lax.broadcasted_iota(jnp.int32, (SUB, LANES), 0)
    for pair in range((fields * eofs + 4) // 2):
        above, below = decode_rows(from_a, from_b, odd, sub, pair)
        at = pl.ds(pair * 2 * SUB, 2 * SUB)
        north[at, :] = jnp.concatenate(above, axis=0)
        south[at, :] = jnp.concatenate(below, axis=0)

    def put(pair, mine_west, mine_east):
        write_pair(out_a, pair, *[jnp.where(ring_odd, w, e) for w, e in zip(mine_west, mine_east)])
        write_pair(out_b, pair, *[jnp.where(ring_odd, e, w) for w, e in zip(mine_west, mine_east)])

    pairs = (eofs // 2 + 1) // 2
    for t, ref in ((0, north), (2, south)):
        tiles = strip_tiles(fields, eofs, lambda i: ref[pl.ds(i * SUB, SUB), :], lane)
        for j in range(pairs):
            put(t * pairs + j, tiles[0][2 * j : 2 * j + 2], tiles[1][2 * j : 2 * j + 2])
    for j in range(pairs):
        put(pairs + j, read_pair(west, j), read_pair(east, j))
    for edges in panel_edges[:1]:
        for j in range(edges.shape[2] // (2 * SUB)):
            put(3 * pairs + j, read_pair(edges.at[0, 0], j), read_pair(edges.at[0, 1], j))


def main_kernel(
    fields, eofs, own, north, south,
    adj, strip, coeff_main, coeff_strip, wide, first, second,
):
    lane = lane_grid()
    inner = lane & (SLOT - 1)
    total = fields * eofs

    def tile(t, i):
        return (north, own, south)[t][pl.ds(i * SUB, SUB), :]

    for k in range(4):
        for t in range(3):
            cells = tile(t, total + k)
            if k < 3:
                cells = time_step * cells
            at = pl.ds(t * SUB, SUB)
            coeff_main[k, at, :] = cells
            edges = edge_columns(fields, lambda f: cells, lane)
            west = (inner >= HALO) & (inner < 2 * HALO)
            coeff_strip[0, k, at, :] = jnp.where(west, edges, 0.0)
            coeff_strip[1, k, at, :] = jnp.where(inner < HALO, edges, 0.0)
    main_coefficients(coeff_main, wide)
    groups = total // SUB
    read, write = main_rows(own, north, south, adj)
    diffuse(read, write, lambda k, w: [wide[k, w]] * groups, groups, first, second, True)
    for t in range(3):
        for e in range(eofs):
            strip[t, pl.ds(e * SUB, SUB), :] = edge_columns(
                fields, lambda f: tile(t, f * eofs + e), lane
            )


def project_kernel(fields, eofs, members, basis, panel, *rest):
    arrived, proj = rest[:-1], rest[-1]
    _, _, me = position()
    blocks = (panel,) + arrived
    count = len(blocks)
    depth = panel.shape[2] * SUB
    for f in range(fields):
        total = None
        for s, block in enumerate(blocks):
            cells = jnp.concatenate(
                [block[m, f].reshape(depth, LANES) for m in range(members)], axis=1
            )
            part = jnp.dot(
                basis[lax.rem(me - s + count, count), f], cells, preferred_element_type=jnp.float32
            )
            total = part if total is None else total + part
        for m in range(members):
            proj[m, pl.ds(f * eofs * SUB, eofs * SUB), :] = total[:, m * LANES : (m + 1) * LANES]


def main_coefficients(coeff_main, wide):
    for k in range(4):
        for w in range(WINDOW):
            wide[k, w] = jnp.broadcast_to(coeff_main[k, pl.ds(w + 2, 1), :], (SUB, LANES))


def strip_coefficients(coeff_strip, wide_strip, eofs):
    sub = lax.broadcasted_iota(jnp.int32, (SUB, LANES), 0)
    for k in range(4):
        for w in range(WINDOW):
            west = jnp.broadcast_to(coeff_strip[0, k, pl.ds(w + 2, 1), :], (SUB, LANES))
            east = jnp.broadcast_to(coeff_strip[1, k, pl.ds(w + 2, 1), :], (SUB, LANES))
            wide_strip[k, w, pl.ds(0, SUB), :] = west
            wide_strip[k, w, pl.ds(SUB, SUB), :] = jnp.where(sub < eofs - SUB, west, east)
            wide_strip[k, w, pl.ds(2 * SUB, SUB), :] = east


def main_rows(own, north, south, out):
    def read(w, g):
        t, y = place(w)
        return (north, own, south)[t][pl.ds(g * SUB * SUB + y, SUB, stride=SUB), :]

    def write(w, g, cells):
        out[pl.ds(g * SUB * SUB + w - STEPS, SUB, stride=SUB), :] = cells

    return read, write


def strip_rows(strip, out, wide_strip):
    def read(w, g):
        t, y = place(w)
        return strip[t, pl.ds(g * SUB * SUB + y, SUB, stride=SUB), :]

    def write(w, g, cells):
        out[pl.ds(g * SUB * SUB + w - STEPS, SUB, stride=SUB), :] = cells

    def coeff(k, w):
        return [wide_strip[k, w, pl.ds(g * SUB, SUB), :] for g in range(3)]

    return read, write, coeff


def combine_kernel(fields, eofs, members, got_a, got_b, *rest):
    (
        basis, adj, proj, strip_own, coeff_own,
        out_a, out_b, combined, halo_out, coeff_strip,
        strip, wide_strip, adj_strip, panel_in, proj_strip, first, second,
    ) = rest[-17:]
    panel_parts = rest[:-17]
    ring_odd, odd, me = position()
    lane = lane_grid()
    sub = lax.broadcasted_iota(jnp.int32, (SUB, LANES), 0)
    inner = lane & (SLOT - 1)
    pair = eofs // 2

    def got(j):
        found = zip(read_pair(got_a, j), read_pair(got_b, j))
        sides = [(jnp.where(ring_odd, a, b), jnp.where(ring_odd, b, a)) for a, b in found]
        return zip(*sides)

    west_mask = inner < HALO
    east_mask = (inner >= HALO) & (inner < 2 * HALO)
    at16 = lane & (SLOT // 2 - 1)
    pairs = (pair + 1) // 2
    for t in range(3):
        west_tiles, east_tiles = [], []
        for j in range(pairs):
            west, east = got(t * pairs + j)
            west_tiles += west
            east_tiles += east
        for j in range(pair):
            west, east = west_tiles[j], east_tiles[j]
            west = west + jnp.where((at16 >= HALO - 4) & (at16 < HALO), turn(west, -4), 0.0)
            east = east + jnp.where(at16 >= HALO, turn(east, 4), 0.0)
            for half in range(2):
                e = half * pair + j
                mine = strip_own[t, pl.ds(e * SUB, SUB), :]
                if half:
                    west, east = turn(west, -(SLOT // 2)), turn(east, -(SLOT // 2))
                strip[t, pl.ds(e * SUB, SUB), :] = jnp.where(west_mask, west, mine)
                strip[t, pl.ds((eofs + e) * SUB, SUB), :] = jnp.where(east_mask, east, mine)
        strip[t, pl.ds(2 * eofs * SUB, 4 * SUB), :] = jnp.zeros((4 * SUB, LANES), jnp.float32)
        at = pl.ds(t * SUB, SUB)
        for side, (cells, mask) in enumerate(
            ((west_tiles[pair], west_mask), (east_tiles[pair], east_mask))
        ):
            cells = cells + turn(cells, -(SLOT // 2))
            turned = [cells] + [turn(cells, i * SLOT) for i in range(1, 4)]
            for k in range(4):
                mine = turned[-k % 4]
                for f in range(1, 4):
                    mine = jnp.where(lane // SLOT == f, turned[(f - k) % 4], mine)
                if k < 3:
                    mine = time_step * mine
                coeff_strip[side, k, at, :] = jnp.where(mask, mine, coeff_own[side, k, at, :])
    strip_coefficients(coeff_strip, wide_strip, eofs)
    read, write, coeff = strip_rows(strip, adj_strip, wide_strip)
    diffuse(read, write, coeff, 3, first, second, True)

    count, depth = basis.shape[0], basis.shape[3]
    if len(panel_parts) == 2:
        edges, far = panel_parts
        near_west, near_east, far = edges[1, 0], edges[1, 1], far[...]
        at = pl.ds(3 * pairs * 2 * SUB, depth)
        a, b = got_a[at, :], got_b[at, :]
        wests = [jnp.where(ring_odd, near_east, far), jnp.where(ring_odd, a, b)]
        easts = [jnp.where(ring_odd, far, near_west), jnp.where(ring_odd, b, a)]
    else:
        wests = [ref[...] for ref in panel_parts[:count]]
        easts = [ref[...] for ref in panel_parts[count:]]
    for s in range(count):
        panel_in[s] = jnp.concatenate([wests[s], easts[s]], axis=1)
    wide_lane = lax.broadcasted_iota(jnp.int32, (eofs * SUB, 2 * LANES), 1) & (LANES - 1)
    halo = jnp.zeros((eofs * SUB, 2 * LANES), jnp.float32)
    for f in range(fields):
        total = None
        for s in range(count):
            part = jnp.dot(
                basis[lax.rem(me + s, count), f], panel_in[s], preferred_element_type=jnp.float32
            )
            total = part if total is None else total + part
        halo = jnp.where(wide_lane // SLOT == f, total, halo)
    proj_strip[pl.ds(0, eofs * SUB), :] = halo[:, :LANES]
    proj_strip[pl.ds(eofs * SUB, eofs * SUB), :] = halo[:, LANES:]

    scores = [jnp.zeros((SUB, LANES), jnp.float32) for _ in range(members)]
    for e in range(eofs):
        edges = both_edges(eofs, adj_strip, e, inner)
        for f in range(fields):
            at = pl.ds((f * eofs + e) * SUB, SUB)
            cells = jnp.where(own_edge(lane), turn(edges, -f * SLOT - HALO), adj[at, :])
            for m in range(members):
                scores[m] = scores[m] + proj[m, at, :] * cells
    scores = [s / (members - 1) for s in scores]
    tiles = []
    for i in range(fields * eofs):
        at = pl.ds(i * SUB, SUB)
        total = proj[0, at, :] * scores[0]
        for m in range(1, members):
            total = total + proj[m, at, :] * scores[m]
        combined[at, :] = total
        tiles.append(total)

    slot = inner // SUB
    packed = [jnp.zeros((SUB, LANES), jnp.float32) for _ in range(2 * eofs // 4)]
    for side in range(2):
        total = jnp.zeros((SUB, LANES), jnp.float32)
        for e in range(eofs):
            at = pl.ds((side * eofs + e) * SUB, SUB)
            cells = adj_strip[at, :]
            start = HALO if side else STEPS
            spread = turn(cells, -start)
            for m in range(1, members):
                spread = jnp.where(slot == m, turn(cells, m * SUB - start), spread)
            total = total + proj_strip[at, :] * spread
        total = total + turn(total, SLOT)
        total = (total + turn(total, 2 * SLOT)) / (members - 1)
        for e in range(eofs):
            i = side * eofs + e
            cells = proj_strip[pl.ds(i * SUB, SUB), :] * total
            cells = cells + turn(cells, -2 * SUB)
            cells = cells + turn(cells, -SUB)
            packed[i // 4] = jnp.where(slot == i % 4, turn(cells, (i % 4) * SUB), packed[i // 4])
    for j, cells in enumerate(packed):
        halo_out[pl.ds(j * SUB, SUB), :] = cells
    tiles += packed
    if len(tiles) % 2:
        tiles.append(jnp.zeros((SUB, LANES), jnp.float32))
    put_rows(out_a, out_b, tiles, odd, sub)


def both_edges(eofs, strip, e, inner):
    west, east = strip[pl.ds(e * SUB, SUB), :], strip[pl.ds((eofs + e) * SUB, SUB), :]
    return jnp.where(inner < HALO, east, west)


def own_edge(lane):
    return (lane < STEPS) | (lane >= LANES - STEPS)


def fill_strip(fields, eofs, tile, packed, strip, t, lane):
    inner = lane & (SLOT - 1)
    west = (inner >= STEPS) & (inner < HALO)
    east = (inner >= HALO) & (inner < HALO + STEPS)
    for e in range(eofs):
        edges = edge_columns(fields, lambda f: tile(f * eofs + e), lane)
        for side, mask in enumerate((west, east)):
            i = side * eofs + e
            shift = (HALO if side else STEPS) - (i % 4) * SUB
            beyond = turn(packed[pl.ds(i // 4 * SUB, SUB), :], shift)
            strip[t, pl.ds(i * SUB, SUB), :] = jnp.where(mask, beyond, edges)
    strip[t, pl.ds(2 * eofs * SUB, 4 * SUB), :] = jnp.zeros((4 * SUB, LANES), jnp.float32)


def forward_coefficients(wide, wide_strip, groups):
    def coeff(k, w):
        strip = [wide_strip[k, w, pl.ds(g * SUB, SUB), :] for g in range(3)]
        return strip + [wide[k, w]] * groups

    return coeff


def before_forward_kernel(
    fields, eofs, own, halo, coeff_main, coeff_strip, wide, wide_strip, strip, kept, kept_flux
):
    lane = lane_grid()
    main_coefficients(coeff_main, wide)
    strip_coefficients(coeff_strip, wide_strip, eofs)
    fill_strip(fields, eofs, lambda i: own[pl.ds(i * SUB, SUB), :], halo, strip, 0, lane)

    def read(w, g):
        at = pl.ds((g if g < 3 else g - 3) * SUB * SUB + w - STEPS, SUB, stride=SUB)
        return strip[0, at, :] if g < 3 else own[at, :]

    groups = own.shape[0] // (SUB * SUB)
    coeff = forward_coefficients(wide, wide_strip, groups)
    diffuse_early(read, coeff, groups + 3, kept, kept_flux)


def forward_kernel(
    fields, eofs, own, from_a, from_b, wide, wide_strip, strip_own, kept, kept_flux,
    result, out, north, south, strip, strip_out, first, second, sems,
):
    _, odd, _ = position()
    lane = lane_grid()
    sub = lax.broadcasted_iota(jnp.int32, (SUB, LANES), 0)
    total = fields * eofs
    for pair in range(north.shape[0] // (2 * SUB)):
        above, below = decode_rows(from_a, from_b, odd, sub, pair)
        at = pl.ds(pair * 2 * SUB, 2 * SUB)
        north[at, :] = jnp.concatenate(above, axis=0)
        south[at, :] = jnp.concatenate(below, axis=0)
    for t, ref in ((0, north), (2, south)):
        packed = ref.at[pl.ds(total * SUB, 2 * eofs // 4 * SUB)]
        fill_strip(
            fields, eofs, lambda i: ref[pl.ds(i * SUB, SUB), :], packed, strip, t, lane
        )
    strip[1] = strip_own[0]
    groups = total // SUB
    read_main, write_main = main_rows(own, north, south, out)
    read_strip, write_strip, _ = strip_rows(strip, strip_out, wide_strip)

    def read(w, g):
        return read_strip(w, g) if g < 3 else read_main(w, g - 3)

    def write(w, g, cells):
        if g < 3:
            write_strip(w, g, cells)
        else:
            write_main(w, g - 3, cells)

    coeff = forward_coefficients(wide, wide_strip, groups)
    early = (kept, kept_flux)
    diffuse(read, write, coeff, groups + 3, first, second, False, early)
    edges = [both_edges(eofs, strip_out, e, lane & (SLOT - 1)) for e in range(eofs)]
    copies = []
    for f in range(fields):
        for e in range(eofs):
            at = pl.ds((f * eofs + e) * SUB, SUB)
            out[at, :] = jnp.where(own_edge(lane), turn(edges[e], -f * SLOT - HALO), out[at, :])
        part = pl.ds(f * eofs * SUB, eofs * SUB)
        copies.append(pltpu.make_async_copy(out.at[part], result.at[part], sems.at[f]))
        copies[-1].start()
    for copy in copies:
        copy.wait()


def call(kernel, args, outs, scratch=(), flops=1_000_000, out_space=pltpu.VMEM):
    whole = pl.BlockSpec(memory_space=pltpu.VMEM)
    moved = sum(a.size * a.dtype.itemsize for a in list(args) + list(outs))
    return pl.pallas_call(
        kernel,
        in_specs=[whole] * len(args),
        out_specs=[pl.BlockSpec(memory_space=out_space)] * len(outs),
        out_shape=list(outs),
        scratch_shapes=[pltpu.VMEM(*s) if isinstance(s, tuple) else s for s in scratch],
        compiler_params=pltpu.CompilerParams(vmem_limit_bytes=24 * 2**20),
        cost_estimate=pl.CostEstimate(flops=flops, bytes_accessed=moved, transcendentals=0),
    )(*args)


def panel_edges_apart(edges, count, me):
    groups = lax.axis_size("gx")
    wests, easts = [], []
    for s in range(count):
        for side, into in ((1, wests), (0, easts)):
            pairs = []
            for group in range(groups):
                for held in range(count):
                    tile = (held - s) % count
                    if side == 1:
                        to = group + (tile == 0)
                    else:
                        to = group - (tile == count - 1)
                    pairs.append((group * count + held, to % groups * count + tile))
            ahead = (-s - 1) if side == 1 else (1 - s)
            into.append(lax.ppermute(edges[ahead % count, side], RING, pairs))
    return wests + easts


def per_device(panels, eof_basis, control, coefficients):
    members, fields, depth, row_count, _ = panels.shape
    _, eofs, _, col_count = control.shape
    count = lax.axis_size("gz")
    me = lax.axis_index("gz")
    total = fields * eofs
    rows = total * row_count
    f32 = lambda *shape: jax.ShapeDtypeStruct(shape, jnp.float32)
    bf16 = lambda *shape: jax.ShapeDtypeStruct(shape, jnp.bfloat16)

    all_rows = rows + 4 * row_count
    own = jnp.concatenate(
        [control.reshape(rows, col_count), coefficients.reshape(4 * row_count, col_count)]
    )
    sent_a, sent_b = call(start_kernel, [own], [bf16(all_rows, col_count)] * 2)
    from_a, from_b = swap_a(sent_a, "gy"), swap_b(sent_b, "gy", False)
    strip_sent = (eofs // 2 + 1) * row_count
    tiles = call(
        functools.partial(slice_kernel, members, fields),
        [panels],
        [bf16(*panels.shape[:-1], col_count)] * count,
    )
    west, east, edges, basis = call(
        functools.partial(own_strips_kernel, fields, eofs, members),
        [own, eof_basis, *tiles],
        [bf16(strip_sent, col_count)] * 2
        + [
            bf16(count, 2, depth * row_count, col_count),
            bf16(count, fields, eofs * row_count, depth * row_count),
        ],
    )
    arrived = [
        lax.ppermute(tiles[s], "gz", [(i, (i + s) % count) for i in range(count)])
        for s in range(1, count)
    ]

    if count == 2:
        groups = lax.axis_size("gx")
        pairs = [(2 * g, (g + 1) % groups * 2) for g in range(groups)]
        pairs += [(2 * g + 1, (g - 1) % groups * 2 + 1) for g in range(groups)]
        far = lax.ppermute(jnp.where(me == 1, edges[1, 0], edges[1, 1]), RING, pairs)
        panel_sent, panel_parts = [edges], [edges, far]
    else:
        panel_sent, panel_parts = [], panel_edges_apart(edges, count, me)

    sent_a, sent_b, north, south = call(
        functools.partial(pack_kernel, fields, eofs),
        [from_a, from_b, west, east, *panel_sent],
        [bf16(3 * strip_sent + (count == 2) * depth * row_count, col_count)] * 2
        + [f32(rows + 4 * row_count, col_count)] * 2,
    )
    got_a, got_b = swap_a(sent_a, RING), swap_b(sent_b, RING, True)

    strip_rows = (2 * eofs + 4) * row_count
    main_scratch = [((WINDOW, total, LANES), jnp.float32)] * 2
    strip_scratch = [((WINDOW, 3 * SUB, LANES), jnp.float32)] * 2
    adj, strip, coeff_main, coeff_strip = call(
        functools.partial(main_kernel, fields, eofs),
        [own, north, south],
        [
            f32(rows, col_count),
            f32(3, eofs * row_count, col_count),
            f32(4, 3 * row_count, col_count),
            f32(2, 4, 3 * row_count, col_count),
        ],
        [((4, WINDOW, SUB, LANES), jnp.float32)] + main_scratch,
        flops=20_000_000,
    )
    (proj,) = call(
        functools.partial(project_kernel, fields, eofs, members),
        [basis, tiles[0], *arrived],
        [f32(members, rows, col_count)],
        flops=20_000_000,
    )
    packed = 2 * eofs // 4
    sent_a, sent_b, combined, halo, coeff_strip = call(
        functools.partial(combine_kernel, fields, eofs, members),
        [got_a, got_b, *panel_parts, basis, adj, proj, strip, coeff_strip],
        [bf16((total + packed + 1) // 2 * 2 * row_count, col_count)] * 2
        + [
            f32(rows, col_count),
            f32(packed * row_count, col_count),
            f32(2, 4, 3 * row_count, col_count),
        ],
        [
            ((3, strip_rows, LANES), jnp.float32),
            ((4, WINDOW, 3 * SUB, LANES), jnp.float32),
            ((strip_rows, LANES), jnp.float32),
            ((count, depth * row_count, 2 * LANES), jnp.bfloat16),
            ((2 * eofs * row_count, LANES), jnp.float32),
        ]
        + strip_scratch,
    )
    from_a, from_b = swap_a(sent_a, "gy"), swap_b(sent_b, "gy", False)
    early_steps = (SUB - 1) // 2
    early_count = sum(len(early_rows(step)[0]) for step in range(early_steps))
    wide, wide_strip, strip, kept, kept_flux = call(
        functools.partial(before_forward_kernel, fields, eofs),
        [combined, halo, coeff_main, coeff_strip],
        [
            f32(4, WINDOW, SUB, LANES),
            f32(4, WINDOW, 3 * SUB, LANES),
            f32(1, strip_rows, LANES),
            f32(early_count, total + 3 * SUB, LANES),
            f32(early_steps, total + 3 * SUB, LANES),
        ],
        flops=20_000_000,
    )
    (result,) = call(
        functools.partial(forward_kernel, fields, eofs),
        [combined, from_a, from_b, wide, wide_strip, strip, kept, kept_flux],
        [f32(rows, col_count)],
        [((rows, LANES), jnp.float32)]
        + [((sent_a.shape[0], LANES), jnp.float32)] * 2
        + [((3, strip_rows, LANES), jnp.float32), ((strip_rows, LANES), jnp.float32)]
        + [((WINDOW, total + 3 * SUB, LANES), jnp.float32)] * 2
        + [pltpu.SemaphoreType.DMA((fields,))],
        out_space=pltpu.HBM,
    )
    return result.reshape(control.shape)


def solution(mesh):
    in_specs = (
        P(None, None, "gz", "gy", "gx"),
        P(),
        P(None, None, "gy", ("gx", "gz")),
        P(None, "gy", ("gx", "gz")),
    )
    out_specs = P(None, None, "gy", ("gx", "gz"))
    return jax.shard_map(
        per_device, mesh=mesh, in_specs=in_specs, out_specs=out_specs, check_vma=False
    )
```

```python
import functools

import jax
import jax.numpy as jnp
from jax import lax
from jax.experimental import pallas as pl
from jax.experimental.pallas import tpu as pltpu
from jax.sharding import PartitionSpec as P

STEPS = 6
LANES = 128
SUB = 8
RING = ("gx", "gz")

time_step = 0.09

WINDOW = SUB + 2 * STEPS
HALO = 2 * STEPS
SLOT = 32


def turn(cells, shift):
    return pltpu.roll(cells, shift % LANES, 1)


def swap_a(values, axes):
    count = lax.axis_size(axes)
    return lax.ppermute(values, axes, [(i, i ^ 1) for i in range(count)])


def swap_b(values, axes, closed):
    count = lax.axis_size(axes)
    pairs = [(i, i + 1) for i in range(1, count - 1, 2)]
    if closed:
        pairs.append((count - 1, 0))
    return lax.ppermute(values, axes, pairs + [(j, i) for i, j in pairs])


def place(w):
    return (w + 2) // SUB, (w + 2) % SUB


def position():
    me = lax.axis_index("gz")
    ring = lax.axis_index("gx") * lax.axis_size("gz") + me
    return lax.rem(ring, 2) == 1, lax.rem(lax.axis_index("gy"), 2) == 1, me


def lane_grid():
    return lax.broadcasted_iota(jnp.int32, (SUB, LANES), 1)


def early_rows(step):
    rows = range(STEPS + 1 + step, STEPS + SUB - 1 - step)
    return rows, sum(len(early_rows(s)[0]) for s in range(step))


def diffuse_early(read, coeff, groups, kept, kept_flux):
    step = 0
    while len(early_rows(step)[0]):
        rows, base = early_rows(step)
        last_rows, last_base = early_rows(step - 1)

        def fetch(w):
            if step == 0:
                return [read(w, g) for g in range(groups)]
            at = last_base + w - last_rows[0]
            return [kept[at, pl.ds(g * SUB, SUB), :] for g in range(groups)]

        here, south = fetch(rows[0] - 1), None
        for w in range(rows[0] - 1, rows[-1] + 1):
            k = [coeff(i, w) for i in range(4)]
            north = fetch(w + 1)
            flux = []
            for g in range(groups):
                east_diff = turn(here[g], -1) - here[g]
                north_diff = north[g] - here[g]
                flux.append(k[1][g] * east_diff + k[2][g] * north_diff)
                if w in rows:
                    flux_east = k[0][g] * east_diff + k[1][g] * north_diff
                    div = (flux[g] - south[g]) + flux_east - turn(flux_east, 1)
                    kept[base + w - rows[0], pl.ds(g * SUB, SUB), :] = here[g] + k[3][g] * div
                if w == rows[-1]:
                    kept_flux[step, pl.ds(g * SUB, SUB), :] = flux[g]
            here, south = north, flux
        step += 1


def diffuse(read, write, coeff, groups, first, second, adjoint, early=None):
    state, spare = None, first
    made = range(0)
    for step in range(STEPS):
        low, high = step, WINDOW - 1 - step
        last, made = made, early_rows(step)[0] if early else range(0)

        def fetch(w):
            if state is None:
                return [read(w, g) for g in range(groups)]
            if w in last:
                at = early_rows(step - 1)[1] + w - last[0]
                return [early[0][at, pl.ds(g * SUB, SUB), :] for g in range(groups)]
            return [state[w, pl.ds(g * SUB, SUB), :] for g in range(groups)]

        here, seen, south = fetch(low), None, None
        for w in range(low, high):
            if w in made:
                if w == made[-1]:
                    here = fetch(w + 1)
                    south = [early[1][step, pl.ds(g * SUB, SUB), :] for g in range(groups)]
                continue
            k = [coeff(i, w) for i in range(4)]
            north = fetch(w + 1)
            if adjoint:
                if seen is None:
                    seen = [k[3][g] * here[g] for g in range(groups)]
                area = coeff(3, w + 1)
                seen_north = [area[g] * north[g] for g in range(groups)]
            else:
                seen, seen_north = here, north
            flux = []
            for g in range(groups):
                east_diff = turn(seen[g], -1) - seen[g]
                north_diff = seen_north[g] - seen[g]
                flux.append(k[1][g] * east_diff + k[2][g] * north_diff)
                if w > low:
                    flux_east = k[0][g] * east_diff + k[1][g] * north_diff
                    div = (flux[g] - south[g]) + flux_east - turn(flux_east, 1)
                    moved = here[g] + (div if adjoint else k[3][g] * div)
                    if step == STEPS - 1:
                        write(w, g, moved)
                    else:
                        spare[w, pl.ds(g * SUB, SUB), :] = moved
            here, seen, south = north, seen_north, flux
        state, spare = spare, (second if spare is first else first)


def read_pair(ref, pair):
    cells = ref[pl.ds(pair * 2 * SUB, 2 * SUB), :].astype(jnp.float32)
    return cells[:SUB], cells[SUB:]


def write_pair(ref, pair, first, second):
    cells = jnp.concatenate([first, second], axis=0).astype(jnp.bfloat16)
    ref[pl.ds(pair * 2 * SUB, 2 * SUB), :] = cells


def split(cells):
    high = cells.astype(jnp.bfloat16).astype(jnp.float32)
    return high, cells - high


def encode_rows(cells, sub):
    high, low = split(cells)
    edge = SUB - STEPS
    to_north = jnp.where(sub < STEPS, high, pltpu.roll(low, STEPS, 0))
    to_south = jnp.where(sub >= edge, high, pltpu.roll(low, edge, 0))
    return to_north, to_south


def decode_rows(from_a, from_b, odd, sub, pair):
    edge = SUB - STEPS
    north, south = [], []
    for a, b in zip(read_pair(from_a, pair), read_pair(from_b, pair)):
        above, below = jnp.where(odd, a, b), jnp.where(odd, b, a)
        north.append(above + jnp.where(sub >= STEPS, pltpu.roll(above, STEPS, 0), 0.0))
        south.append(below + jnp.where(sub < edge, pltpu.roll(below, edge, 0), 0.0))
    return north, south


def start_kernel(own, out_a, out_b):
    _, odd, _ = position()
    sub = lax.broadcasted_iota(jnp.int32, (SUB, LANES), 0)
    tiles = [own[pl.ds(i * SUB, SUB), :] for i in range(own.shape[0] // SUB)]
    put_rows(out_a, out_b, tiles, odd, sub)


def put_rows(out_a, out_b, tiles, odd, sub):
    for pair in range(len(tiles) // 2):
        north, south = zip(*[encode_rows(t, sub) for t in tiles[2 * pair : 2 * pair + 2]])
        write_pair(out_a, pair, *[jnp.where(odd, n, s) for n, s in zip(north, south)])
        write_pair(out_b, pair, *[jnp.where(odd, s, n) for n, s in zip(north, south)])


def edge_columns(fields, tile, lane):
    edges = turn(tile(0), HALO)
    for f in range(1, fields):
        edges = jnp.where(lane // SLOT == f, turn(tile(f), f * SLOT + HALO), edges)
    return edges


def strip_tiles(fields, eofs, tile, lane):
    pair = eofs // 2
    west_out, east_out = [], []
    inner = lane & (SLOT - 1)
    at = lane & (SLOT // 2 - 1)
    for j in range(pair):
        first = edge_columns(fields, lambda f: tile(f * eofs + j), lane)
        second = edge_columns(fields, lambda f: tile(f * eofs + pair + j), lane)
        second = turn(second, SLOT // 2)
        west = jnp.where((inner >= HALO - 4) & (inner < 2 * HALO), first, second)
        high, low = split(west)
        west_out.append(jnp.where((at >= HALO - 4) & (at < HALO), turn(low, -4), high))
        east = jnp.where(inner < SLOT // 2, first, second)
        high, low = split(east)
        east_out.append(jnp.where(at < HALO, high, turn(low, 4)))
    edges = edge_columns(4, lambda k: tile(fields * eofs + k), lane)
    west = jnp.where((inner >= HALO) & (inner < 2 * HALO), edges, 0.0)
    east = jnp.where(inner < HALO, edges, 0.0)
    for cells, out in ((west, west_out), (east, east_out)):
        high, low = split(cells)
        out.append(high + turn(low, SLOT // 2))
    return west_out, east_out


def slice_kernel(members, fields, panels, *tiles):
    _, _, me = position()
    for s, block in enumerate(tiles):
        start = pl.multiple_of(lax.rem(me + s, len(tiles)) * LANES, LANES)
        for m in range(members):
            for f in range(fields):
                block[m, f] = panels[m, f, :, :, pl.ds(start, LANES)]


def own_strips_kernel(fields, eofs, members, own, eof_basis, *rest):
    tiles, (west, east, edges, basis) = rest[:-4], rest[-4:]
    lane = lane_grid()

    def tile(i):
        return own[pl.ds(i * SUB, SUB), :]

    for ref, packed in zip((west, east), strip_tiles(fields, eofs, tile, lane)):
        for pair in range(len(packed) // 2):
            write_pair(ref, pair, *packed[2 * pair : 2 * pair + 2])

    count = len(tiles)
    depth = tiles[0].shape[2] * SUB
    column = lax.broadcasted_iota(jnp.int32, (LANES, 2 * LANES), 0)
    target = lax.broadcasted_iota(jnp.int32, (LANES, 2 * LANES), 1)
    west_ok = (target < LANES) & (column < STEPS)
    east_ok = (target >= LANES) & (column >= LANES - STEPS)
    offset = jnp.where(
        west_ok,
        target - column,
        jnp.where(east_ok, target - LANES - column + LANES - STEPS, -1),
    )
    for s, block in enumerate(tiles):
        total = jnp.zeros((depth, 2 * LANES), jnp.float32)
        for m in range(members):
            for f in range(fields):
                pick = (offset == f * SLOT + m * SUB).astype(jnp.bfloat16)
                total += jnp.dot(
                    block[m, f].reshape(depth, LANES), pick, preferred_element_type=jnp.float32
                )
        total = total.astype(jnp.bfloat16)
        edges[s, 0] = total[:, :LANES]
        edges[s, 1] = total[:, LANES:]

    levels = eof_basis.shape[1]

    def grid(shape, dim):
        return lax.broadcasted_iota(jnp.int32, shape, dim)

    shape = (eofs * SUB, eofs)
    widen = (grid(shape, 0) // SUB == grid(shape, 1)).astype(jnp.bfloat16)
    shape = (levels, levels * SUB)
    spread = (grid(shape, 1) // SUB == grid(shape, 0)).astype(jnp.bfloat16)
    shape = (eofs * SUB, levels * SUB)
    same_row = grid(shape, 0) % SUB == grid(shape, 1) % SUB
    for f in range(fields):
        wide = lax.dot_general(
            widen, eof_basis[f], (((1,), (1,)), ((), ())), preferred_element_type=jnp.float32
        ).astype(jnp.bfloat16)
        wide = jnp.dot(wide, spread, preferred_element_type=jnp.float32)
        wide = jnp.where(same_row, wide, 0.0).astype(jnp.bfloat16)
        for h in range(count):
            basis[h, f] = wide[:, h * depth : (h + 1) * depth]


def pack_kernel(fields, eofs, from_a, from_b, west, east, *rest):
    panel_edges, (out_a, out_b, north, south) = rest[:-4], rest[-4:]
    ring_odd, odd, _ = position()
    lane = lane_grid()
    sub = lax.broadcasted_iota(jnp.int32, (SUB, LANES), 0)
    for pair in range((fields * eofs + 4) // 2):
        above, below = decode_rows(from_a, from_b, odd, sub, pair)
        at = pl.ds(pair * 2 * SUB, 2 * SUB)
        north[at, :] = jnp.concatenate(above, axis=0)
        south[at, :] = jnp.concatenate(below, axis=0)

    def put(pair, mine_west, mine_east):
        write_pair(out_a, pair, *[jnp.where(ring_odd, w, e) for w, e in zip(mine_west, mine_east)])
        write_pair(out_b, pair, *[jnp.where(ring_odd, e, w) for w, e in zip(mine_west, mine_east)])

    pairs = (eofs // 2 + 1) // 2
    for t, ref in ((0, north), (2, south)):
        tiles = strip_tiles(fields, eofs, lambda i: ref[pl.ds(i * SUB, SUB), :], lane)
        for j in range(pairs):
            put(t * pairs + j, tiles[0][2 * j : 2 * j + 2], tiles[1][2 * j : 2 * j + 2])
    for j in range(pairs):
        put(pairs + j, read_pair(west, j), read_pair(east, j))
    for edges in panel_edges[:1]:
        for j in range(edges.shape[2] // (2 * SUB)):
            put(3 * pairs + j, read_pair(edges.at[0, 0], j), read_pair(edges.at[0, 1], j))


def main_kernel(
    fields, eofs, own, north, south,
    adj, strip, coeff_main, coeff_strip, wide, first, second,
):
    lane = lane_grid()
    inner = lane & (SLOT - 1)
    total = fields * eofs

    def tile(t, i):
        return (north, own, south)[t][pl.ds(i * SUB, SUB), :]

    for k in range(4):
        for t in range(3):
            cells = tile(t, total + k)
            if k < 3:
                cells = time_step * cells
            at = pl.ds(t * SUB, SUB)
            coeff_main[k, at, :] = cells
            edges = edge_columns(fields, lambda f: cells, lane)
            west = (inner >= HALO) & (inner < 2 * HALO)
            coeff_strip[0, k, at, :] = jnp.where(west, edges, 0.0)
            coeff_strip[1, k, at, :] = jnp.where(inner < HALO, edges, 0.0)
    main_coefficients(coeff_main, wide)
    groups = total // SUB
    read, write = main_rows(own, north, south, adj)
    diffuse(read, write, lambda k, w: [wide[k, w]] * groups, groups, first, second, True)
    for t in range(3):
        for e in range(eofs):
            strip[t, pl.ds(e * SUB, SUB), :] = edge_columns(
                fields, lambda f: tile(t, f * eofs + e), lane
            )


def project_kernel(fields, eofs, members, basis, panel, *rest):
    arrived, proj = rest[:-1], rest[-1]
    _, _, me = position()
    blocks = (panel,) + arrived
    count = len(blocks)
    depth = panel.shape[2] * SUB
    for f in range(fields):
        total = None
        for s, block in enumerate(blocks):
            cells = jnp.concatenate(
                [block[m, f].reshape(depth, LANES) for m in range(members)], axis=1
            )
            part = jnp.dot(
                basis[lax.rem(me - s + count, count), f], cells, preferred_element_type=jnp.float32
            )
            total = part if total is None else total + part
        for m in range(members):
            proj[m, pl.ds(f * eofs * SUB, eofs * SUB), :] = total[:, m * LANES : (m + 1) * LANES]


def main_coefficients(coeff_main, wide):
    for k in range(4):
        for w in range(WINDOW):
            wide[k, w] = jnp.broadcast_to(coeff_main[k, pl.ds(w + 2, 1), :], (SUB, LANES))


def strip_coefficients(coeff_strip, wide_strip, eofs):
    sub = lax.broadcasted_iota(jnp.int32, (SUB, LANES), 0)
    for k in range(4):
        for w in range(WINDOW):
            west = jnp.broadcast_to(coeff_strip[0, k, pl.ds(w + 2, 1), :], (SUB, LANES))
            east = jnp.broadcast_to(coeff_strip[1, k, pl.ds(w + 2, 1), :], (SUB, LANES))
            wide_strip[k, w, pl.ds(0, SUB), :] = west
            wide_strip[k, w, pl.ds(SUB, SUB), :] = jnp.where(sub < eofs - SUB, west, east)
            wide_strip[k, w, pl.ds(2 * SUB, SUB), :] = east


def main_rows(own, north, south, out):
    def read(w, g):
        t, y = place(w)
        return (north, own, south)[t][pl.ds(g * SUB * SUB + y, SUB, stride=SUB), :]

    def write(w, g, cells):
        out[pl.ds(g * SUB * SUB + w - STEPS, SUB, stride=SUB), :] = cells

    return read, write


def strip_rows(strip, out, wide_strip):
    def read(w, g):
        t, y = place(w)
        return strip[t, pl.ds(g * SUB * SUB + y, SUB, stride=SUB), :]

    def write(w, g, cells):
        out[pl.ds(g * SUB * SUB + w - STEPS, SUB, stride=SUB), :] = cells

    def coeff(k, w):
        return [wide_strip[k, w, pl.ds(g * SUB, SUB), :] for g in range(3)]

    return read, write, coeff


def combine_kernel(fields, eofs, members, got_b, got_a, *rest):
    (
        basis, adj, proj, strip_own, coeff_own,
        out_a, out_b, combined, halo_out, coeff_strip,
        strip, wide_strip, adj_strip, panel_in, proj_strip, first, second,
    ) = rest[-17:]
    panel_parts = rest[:-17]
    ring_odd, odd, me = position()
    lane = lane_grid()
    sub = lax.broadcasted_iota(jnp.int32, (SUB, LANES), 0)
    inner = lane & (SLOT - 1)
    pair = eofs // 2

    def got(j):
        found = zip(read_pair(got_a, j), read_pair(got_b, j))
        sides = [(jnp.where(ring_odd, a, b), jnp.where(ring_odd, b, a)) for a, b in found]
        return zip(*sides)

    west_mask = inner < HALO
    east_mask = (inner >= HALO) & (inner < 2 * HALO)
    at16 = lane & (SLOT // 2 - 1)
    pairs = (pair + 1) // 2
    for t in range(3):
        west_tiles, east_tiles = [], []
        for j in range(pairs):
            west, east = got(t * pairs + j)
            west_tiles += west
            east_tiles += east
        for j in range(pair):
            west, east = west_tiles[j], east_tiles[j]
            west = west + jnp.where((at16 >= HALO - 4) & (at16 < HALO), turn(west, -4), 0.0)
            east = east + jnp.where(at16 >= HALO, turn(east, 4), 0.0)
            for half in range(2):
                e = half * pair + j
                mine = strip_own[t, pl.ds(e * SUB, SUB), :]
                if half:
                    west, east = turn(west, -(SLOT // 2)), turn(east, -(SLOT // 2))
                strip[t, pl.ds(e * SUB, SUB), :] = jnp.where(west_mask, west, mine)
                strip[t, pl.ds((eofs + e) * SUB, SUB), :] = jnp.where(east_mask, east, mine)
        strip[t, pl.ds(2 * eofs * SUB, 4 * SUB), :] = jnp.zeros((4 * SUB, LANES), jnp.float32)
        at = pl.ds(t * SUB, SUB)
        for side, (cells, mask) in enumerate(
            ((west_tiles[pair], west_mask), (east_tiles[pair], east_mask))
        ):
            cells = cells + turn(cells, -(SLOT // 2))
            turned = [cells] + [turn(cells, i * SLOT) for i in range(1, 4)]
            for k in range(4):
                mine = turned[-k % 4]
                for f in range(1, 4):
                    mine = jnp.where(lane // SLOT == f, turned[(f - k) % 4], mine)
                if k < 3:
                    mine = time_step * mine
                coeff_strip[side, k, at, :] = jnp.where(mask, mine, coeff_own[side, k, at, :])
    strip_coefficients(coeff_strip, wide_strip, eofs)
    read, write, coeff = strip_rows(strip, adj_strip, wide_strip)
    diffuse(read, write, coeff, 3, first, second, True)

    count, depth = basis.shape[0], basis.shape[3]
    if len(panel_parts) == 2:
        edges, far = panel_parts
        near_west, near_east, far = edges[1, 0], edges[1, 1], far[...]
        at = pl.ds(3 * pairs * 2 * SUB, depth)
        a, b = got_a[at, :], got_b[at, :]
        wests = [jnp.where(ring_odd, near_east, far), jnp.where(ring_odd, a, b)]
        easts = [jnp.where(ring_odd, far, near_west), jnp.where(ring_odd, b, a)]
    else:
        wests = [ref[...] for ref in panel_parts[:count]]
        easts = [ref[...] for ref in panel_parts[count:]]
    for s in range(count):
        panel_in[s] = jnp.concatenate([wests[s], easts[s]], axis=1)
    wide_lane = lax.broadcasted_iota(jnp.int32, (eofs * SUB, 2 * LANES), 1) & (LANES - 1)
    halo = jnp.zeros((eofs * SUB, 2 * LANES), jnp.float32)
    for f in range(fields):
        total = None
        for s in range(count):
            part = jnp.dot(
                basis[lax.rem(me + s, count), f], panel_in[s], preferred_element_type=jnp.float32
            )
            total = part if total is None else total + part
        halo = jnp.where(wide_lane // SLOT == f, total, halo)
    proj_strip[pl.ds(0, eofs * SUB), :] = halo[:, :LANES]
    proj_strip[pl.ds(eofs * SUB, eofs * SUB), :] = halo[:, LANES:]

    scores = [jnp.zeros((SUB, LANES), jnp.float32) for _ in range(members)]
    for e in range(eofs):
        edges = both_edges(eofs, adj_strip, e, inner)
        for f in range(fields):
            at = pl.ds((f * eofs + e) * SUB, SUB)
            cells = jnp.where(own_edge(lane), turn(edges, -f * SLOT - HALO), adj[at, :])
            for m in range(members):
                scores[m] = scores[m] + proj[m, at, :] * cells
    scores = [s / (members - 1) for s in scores]
    tiles = []
    for i in range(fields * eofs):
        at = pl.ds(i * SUB, SUB)
        total = proj[0, at, :] * scores[0]
        for m in range(1, members):
            total = total + proj[m, at, :] * scores[m]
        combined[at, :] = total
        tiles.append(total)

    slot = inner // SUB
    packed = [jnp.zeros((SUB, LANES), jnp.float32) for _ in range(2 * eofs // 4)]
    for side in range(2):
        total = jnp.zeros((SUB, LANES), jnp.float32)
        for e in range(eofs):
            at = pl.ds((side * eofs + e) * SUB, SUB)
            cells = adj_strip[at, :]
            start = HALO if side else STEPS
            spread = turn(cells, -start)
            for m in range(1, members):
                spread = jnp.where(slot == m, turn(cells, m * SUB - start), spread)
            total = total + proj_strip[at, :] * spread
        total = total + turn(total, SLOT)
        total = (total + turn(total, 2 * SLOT)) / (members - 1)
        for e in range(eofs):
            i = side * eofs + e
            cells = proj_strip[pl.ds(i * SUB, SUB), :] * total
            cells = cells + turn(cells, -2 * SUB)
            cells = cells + turn(cells, -SUB)
            packed[i // 4] = jnp.where(slot == i % 4, turn(cells, (i % 4) * SUB), packed[i // 4])
    for j, cells in enumerate(packed):
        halo_out[pl.ds(j * SUB, SUB), :] = cells
    tiles += packed
    if len(tiles) % 2:
        tiles.append(jnp.zeros((SUB, LANES), jnp.float32))
    put_rows(out_a, out_b, tiles, odd, sub)


def both_edges(eofs, strip, e, inner):
    west, east = strip[pl.ds(e * SUB, SUB), :], strip[pl.ds((eofs + e) * SUB, SUB), :]
    return jnp.where(inner < HALO, east, west)


def own_edge(lane):
    return (lane < STEPS) | (lane >= LANES - STEPS)


def fill_strip(fields, eofs, tile, packed, strip, t, lane):
    inner = lane & (SLOT - 1)
    west = (inner >= STEPS) & (inner < HALO)
    east = (inner >= HALO) & (inner < HALO + STEPS)
    for e in range(eofs):
        edges = edge_columns(fields, lambda f: tile(f * eofs + e), lane)
        for side, mask in enumerate((west, east)):
            i = side * eofs + e
            shift = (HALO if side else STEPS) - (i % 4) * SUB
            beyond = turn(packed[pl.ds(i // 4 * SUB, SUB), :], shift)
            strip[t, pl.ds(i * SUB, SUB), :] = jnp.where(mask, beyond, edges)
    strip[t, pl.ds(2 * eofs * SUB, 4 * SUB), :] = jnp.zeros((4 * SUB, LANES), jnp.float32)


def forward_coefficients(wide, wide_strip, groups):
    def coeff(k, w):
        strip = [wide_strip[k, w, pl.ds(g * SUB, SUB), :] for g in range(3)]
        return strip + [wide[k, w]] * groups

    return coeff


def before_forward_kernel(
    fields, eofs, own, halo, coeff_main, coeff_strip, wide, wide_strip, strip, kept, kept_flux
):
    lane = lane_grid()
    main_coefficients(coeff_main, wide)
    strip_coefficients(coeff_strip, wide_strip, eofs)
    fill_strip(fields, eofs, lambda i: own[pl.ds(i * SUB, SUB), :], halo, strip, 0, lane)

    def read(w, g):
        at = pl.ds((g if g < 3 else g - 3) * SUB * SUB + w - STEPS, SUB, stride=SUB)
        return strip[0, at, :] if g < 3 else own[at, :]

    groups = own.shape[0] // (SUB * SUB)
    coeff = forward_coefficients(wide, wide_strip, groups)
    diffuse_early(read, coeff, groups + 3, kept, kept_flux)


def forward_kernel(
    fields, eofs, own, from_a, from_b, wide, wide_strip, strip_own, kept, kept_flux,
    result, out, north, south, strip, strip_out, first, second, sems,
):
    _, odd, _ = position()
    lane = lane_grid()
    sub = lax.broadcasted_iota(jnp.int32, (SUB, LANES), 0)
    total = fields * eofs
    for pair in range(north.shape[0] // (2 * SUB)):
        above, below = decode_rows(from_a, from_b, odd, sub, pair)
        at = pl.ds(pair * 2 * SUB, 2 * SUB)
        north[at, :] = jnp.concatenate(above, axis=0)
        south[at, :] = jnp.concatenate(below, axis=0)
    for t, ref in ((0, north), (2, south)):
        packed = ref.at[pl.ds(total * SUB, 2 * eofs // 4 * SUB)]
        fill_strip(
            fields, eofs, lambda i: ref[pl.ds(i * SUB, SUB), :], packed, strip, t, lane
        )
    strip[1] = strip_own[0]
    groups = total // SUB
    read_main, write_main = main_rows(own, north, south, out)
    read_strip, write_strip, _ = strip_rows(strip, strip_out, wide_strip)

    def read(w, g):
        return read_strip(w, g) if g < 3 else read_main(w, g - 3)

    def write(w, g, cells):
        if g < 3:
            write_strip(w, g, cells)
        else:
            write_main(w, g - 3, cells)

    coeff = forward_coefficients(wide, wide_strip, groups)
    early = (kept, kept_flux)
    diffuse(read, write, coeff, groups + 3, first, second, False, early)
    edges = [both_edges(eofs, strip_out, e, lane & (SLOT - 1)) for e in range(eofs)]
    copies = []
    for f in range(fields):
        for e in range(eofs):
            at = pl.ds((f * eofs + e) * SUB, SUB)
            out[at, :] = jnp.where(own_edge(lane), turn(edges[e], -f * SLOT - HALO), out[at, :])
        part = pl.ds(f * eofs * SUB, eofs * SUB)
        copies.append(pltpu.make_async_copy(out.at[part], result.at[part], sems.at[f]))
        copies[-1].start()
    for copy in copies:
        copy.wait()


def call(kernel, args, outs, scratch=(), flops=1_000_000, out_space=pltpu.VMEM):
    whole = pl.BlockSpec(memory_space=pltpu.VMEM)
    moved = sum(a.size * a.dtype.itemsize for a in list(args) + list(outs))
    return pl.pallas_call(
        kernel,
        in_specs=[whole] * len(args),
        out_specs=[pl.BlockSpec(memory_space=out_space)] * len(outs),
        out_shape=list(outs),
        scratch_shapes=[pltpu.VMEM(*s) if isinstance(s, tuple) else s for s in scratch],
        compiler_params=pltpu.CompilerParams(vmem_limit_bytes=24 * 2**20),
        cost_estimate=pl.CostEstimate(flops=flops, bytes_accessed=moved, transcendentals=0),
    )(*args)


def panel_edges_apart(edges, count, me):
    groups = lax.axis_size("gx")
    wests, easts = [], []
    for s in range(count):
        for side, into in ((1, wests), (0, easts)):
            pairs = []
            for group in range(groups):
                for held in range(count):
                    tile = (held - s) % count
                    if side == 1:
                        to = group + (tile == 0)
                    else:
                        to = group - (tile == count - 1)
                    pairs.append((group * count + held, to % groups * count + tile))
            ahead = (-s - 1) if side == 1 else (1 - s)
            into.append(lax.ppermute(edges[ahead % count, side], RING, pairs))
    return wests + easts


def per_device(panels, eof_basis, control, coefficients):
    members, fields, depth, row_count, _ = panels.shape
    _, eofs, _, col_count = control.shape
    count = lax.axis_size("gz")
    me = lax.axis_index("gz")
    total = fields * eofs
    rows = total * row_count
    f32 = lambda *shape: jax.ShapeDtypeStruct(shape, jnp.float32)
    bf16 = lambda *shape: jax.ShapeDtypeStruct(shape, jnp.bfloat16)

    all_rows = rows + 4 * row_count
    own = jnp.concatenate(
        [control.reshape(rows, col_count), coefficients.reshape(4 * row_count, col_count)]
    )
    sent_a, sent_b = call(start_kernel, [own], [bf16(all_rows, col_count)] * 2)
    from_a, from_b = swap_a(sent_a, "gy"), swap_b(sent_b, "gy", False)
    strip_sent = (eofs // 2 + 1) * row_count
    tiles = call(
        functools.partial(slice_kernel, members, fields),
        [panels],
        [bf16(*panels.shape[:-1], col_count)] * count,
    )
    west, east, edges, basis = call(
        functools.partial(own_strips_kernel, fields, eofs, members),
        [own, eof_basis, *tiles],
        [bf16(strip_sent, col_count)] * 2
        + [
            bf16(count, 2, depth * row_count, col_count),
            bf16(count, fields, eofs * row_count, depth * row_count),
        ],
    )
    arrived = [
        lax.ppermute(tiles[s], "gz", [(i, (i + s) % count) for i in range(count)])
        for s in range(1, count)
    ]

    if count == 2:
        groups = lax.axis_size("gx")
        pairs = [(2 * g, (g + 1) % groups * 2) for g in range(groups)]
        pairs += [(2 * g + 1, (g - 1) % groups * 2 + 1) for g in range(groups)]
        far = lax.ppermute(jnp.where(me == 1, edges[1, 0], edges[1, 1]), RING, pairs)
        panel_sent, panel_parts = [edges], [edges, far]
    else:
        panel_sent, panel_parts = [], panel_edges_apart(edges, count, me)

    sent_a, sent_b, north, south = call(
        functools.partial(pack_kernel, fields, eofs),
        [from_a, from_b, west, east, *panel_sent],
        [bf16(3 * strip_sent + (count == 2) * depth * row_count, col_count)] * 2
        + [f32(rows + 4 * row_count, col_count)] * 2,
    )
    got_b = swap_b(sent_b, RING, True)
    got_a = swap_a(sent_a, RING)

    strip_rows = (2 * eofs + 4) * row_count
    main_scratch = [((WINDOW, total, LANES), jnp.float32)] * 2
    strip_scratch = [((WINDOW, 3 * SUB, LANES), jnp.float32)] * 2
    adj, strip, coeff_main, coeff_strip = call(
        functools.partial(main_kernel, fields, eofs),
        [own, north, south],
        [
            f32(rows, col_count),
            f32(3, eofs * row_count, col_count),
            f32(4, 3 * row_count, col_count),
            f32(2, 4, 3 * row_count, col_count),
        ],
        [((4, WINDOW, SUB, LANES), jnp.float32)] + main_scratch,
        flops=20_000_000,
    )
    (proj,) = call(
        functools.partial(project_kernel, fields, eofs, members),
        [basis, tiles[0], *arrived],
        [f32(members, rows, col_count)],
        flops=20_000_000,
    )
    packed = 2 * eofs // 4
    sent_a, sent_b, combined, halo, coeff_strip = call(
        functools.partial(combine_kernel, fields, eofs, members),
        [got_b, got_a, *panel_parts, basis, adj, proj, strip, coeff_strip],
        [bf16((total + packed + 1) // 2 * 2 * row_count, col_count)] * 2
        + [
            f32(rows, col_count),
            f32(packed * row_count, col_count),
            f32(2, 4, 3 * row_count, col_count),
        ],
        [
            ((3, strip_rows, LANES), jnp.float32),
            ((4, WINDOW, 3 * SUB, LANES), jnp.float32),
            ((strip_rows, LANES), jnp.float32),
            ((count, depth * row_count, 2 * LANES), jnp.bfloat16),
            ((2 * eofs * row_count, LANES), jnp.float32),
        ]
        + strip_scratch,
    )
    from_a, from_b = swap_a(sent_a, "gy"), swap_b(sent_b, "gy", False)
    early_steps = (SUB - 1) // 2
    early_count = sum(len(early_rows(step)[0]) for step in range(early_steps))
    wide, wide_strip, strip, kept, kept_flux = call(
        functools.partial(before_forward_kernel, fields, eofs),
        [combined, halo, coeff_main, coeff_strip],
        [
            f32(4, WINDOW, SUB, LANES),
            f32(4, WINDOW, 3 * SUB, LANES),
            f32(1, strip_rows, LANES),
            f32(early_count, total + 3 * SUB, LANES),
            f32(early_steps, total + 3 * SUB, LANES),
        ],
        flops=20_000_000,
    )
    (result,) = call(
        functools.partial(forward_kernel, fields, eofs),
        [combined, from_a, from_b, wide, wide_strip, strip, kept, kept_flux],
        [f32(rows, col_count)],
        [((rows, LANES), jnp.float32)]
        + [((sent_a.shape[0], LANES), jnp.float32)] * 2
        + [((3, strip_rows, LANES), jnp.float32), ((strip_rows, LANES), jnp.float32)]
        + [((WINDOW, total + 3 * SUB, LANES), jnp.float32)] * 2
        + [pltpu.SemaphoreType.DMA((fields,))],
        out_space=pltpu.HBM,
    )
    return result.reshape(control.shape)


def solution(mesh):
    in_specs = (
        P(None, None, "gz", "gy", "gx"),
        P(),
        P(None, None, "gy", ("gx", "gz")),
        P(None, "gy", ("gx", "gz")),
    )
    out_specs = P(None, None, "gy", ("gx", "gz"))
    return jax.shard_map(
        per_device, mesh=mesh, in_specs=in_specs, out_specs=out_specs, check_vma=False
    )
```

```python
import functools

import jax
import jax.numpy as jnp
from jax import lax
from jax.experimental import pallas as pl
from jax.experimental.pallas import tpu as pltpu
from jax.sharding import PartitionSpec as P

STEPS = 6
LANES = 128
SUB = 8
RING = ("gx", "gz")

time_step = 0.09

WINDOW = SUB + 2 * STEPS
HALO = 2 * STEPS
SLOT = 32


def turn(cells, shift):
    return pltpu.roll(cells, shift % LANES, 1)


def swap_a(values, axes):
    count = lax.axis_size(axes)
    return lax.ppermute(values, axes, [(i, i ^ 1) for i in range(count)])


def swap_b(values, axes, closed):
    count = lax.axis_size(axes)
    pairs = [(i, i + 1) for i in range(1, count - 1, 2)]
    if closed:
        pairs.append((count - 1, 0))
    return lax.ppermute(values, axes, pairs + [(j, i) for i, j in pairs])


def place(w):
    return (w + 2) // SUB, (w + 2) % SUB


def position():
    me = lax.axis_index("gz")
    ring = lax.axis_index("gx") * lax.axis_size("gz") + me
    return lax.rem(ring, 2) == 1, lax.rem(lax.axis_index("gy"), 2) == 1, me


def lane_grid():
    return lax.broadcasted_iota(jnp.int32, (SUB, LANES), 1)


def early_rows(step):
    rows = range(STEPS + 1 + step, STEPS + SUB - 1 - step)
    return rows, sum(len(early_rows(s)[0]) for s in range(step))


def diffuse_early(read, coeff, groups, kept, kept_flux):
    step = 0
    while len(early_rows(step)[0]):
        rows, base = early_rows(step)
        last_rows, last_base = early_rows(step - 1)

        def fetch(w):
            if step == 0:
                return [read(w, g) for g in range(groups)]
            at = last_base + w - last_rows[0]
            return [kept[at, pl.ds(g * SUB, SUB), :] for g in range(groups)]

        here, south = fetch(rows[0] - 1), None
        for w in range(rows[0] - 1, rows[-1] + 1):
            k = [coeff(i, w) for i in range(4)]
            north = fetch(w + 1)
            flux = []
            for g in range(groups):
                east_diff = turn(here[g], -1) - here[g]
                north_diff = north[g] - here[g]
                flux.append(k[1][g] * east_diff + k[2][g] * north_diff)
                if w in rows:
                    flux_east = k[0][g] * east_diff + k[1][g] * north_diff
                    div = (flux[g] - south[g]) + flux_east - turn(flux_east, 1)
                    kept[base + w - rows[0], pl.ds(g * SUB, SUB), :] = here[g] + k[3][g] * div
                if w == rows[-1]:
                    kept_flux[step, pl.ds(g * SUB, SUB), :] = flux[g]
            here, south = north, flux
        step += 1


def diffuse(read, write, coeff, groups, first, second, adjoint, early=None):
    state, spare = None, first
    made = range(0)
    for step in range(STEPS):
        low, high = step, WINDOW - 1 - step
        last, made = made, early_rows(step)[0] if early else range(0)

        def fetch(w):
            if state is None:
                return [read(w, g) for g in range(groups)]
            if w in last:
                at = early_rows(step - 1)[1] + w - last[0]
                return [early[0][at, pl.ds(g * SUB, SUB), :] for g in range(groups)]
            return [state[w, pl.ds(g * SUB, SUB), :] for g in range(groups)]

        here, seen, south = fetch(low), None, None
        for w in range(low, high):
            if w in made:
                if w == made[-1]:
                    here = fetch(w + 1)
                    south = [early[1][step, pl.ds(g * SUB, SUB), :] for g in range(groups)]
                continue
            k = [coeff(i, w) for i in range(4)]
            north = fetch(w + 1)
            if adjoint:
                if seen is None:
                    seen = [k[3][g] * here[g] for g in range(groups)]
                area = coeff(3, w + 1)
                seen_north = [area[g] * north[g] for g in range(groups)]
            else:
                seen, seen_north = here, north
            flux = []
            for g in range(groups):
                east_diff = turn(seen[g], -1) - seen[g]
                north_diff = seen_north[g] - seen[g]
                flux.append(k[1][g] * east_diff + k[2][g] * north_diff)
                if w > low:
                    flux_east = k[0][g] * east_diff + k[1][g] * north_diff
                    div = (flux[g] - south[g]) + flux_east - turn(flux_east, 1)
                    moved = here[g] + (div if adjoint else k[3][g] * div)
                    if step == STEPS - 1:
                        write(w, g, moved)
                    else:
                        spare[w, pl.ds(g * SUB, SUB), :] = moved
            here, seen, south = north, seen_north, flux
        state, spare = spare, (second if spare is first else first)


def read_pair(ref, pair):
    cells = ref[pl.ds(pair * 2 * SUB, 2 * SUB), :].astype(jnp.float32)
    return cells[:SUB], cells[SUB:]


def write_pair(ref, pair, first, second):
    cells = jnp.concatenate([first, second], axis=0).astype(jnp.bfloat16)
    ref[pl.ds(pair * 2 * SUB, 2 * SUB), :] = cells


def split(cells):
    high = cells.astype(jnp.bfloat16).astype(jnp.float32)
    return high, cells - high


def encode_rows(cells, sub):
    high, low = split(cells)
    edge = SUB - STEPS
    to_north = jnp.where(sub < STEPS, high, pltpu.roll(low, STEPS, 0))
    to_south = jnp.where(sub >= edge, high, pltpu.roll(low, edge, 0))
    return to_north, to_south


def decode_rows(from_a, from_b, odd, sub, pair):
    edge = SUB - STEPS
    north, south = [], []
    for a, b in zip(read_pair(from_a, pair), read_pair(from_b, pair)):
        above, below = jnp.where(odd, a, b), jnp.where(odd, b, a)
        north.append(above + jnp.where(sub >= STEPS, pltpu.roll(above, STEPS, 0), 0.0))
        south.append(below + jnp.where(sub < edge, pltpu.roll(below, edge, 0), 0.0))
    return north, south


def start_kernel(own, out_a, out_b):
    _, odd, _ = position()
    sub = lax.broadcasted_iota(jnp.int32, (SUB, LANES), 0)
    tiles = [own[pl.ds(i * SUB, SUB), :] for i in range(own.shape[0] // SUB)]
    put_rows(out_a, out_b, tiles, odd, sub)


def put_rows(out_a, out_b, tiles, odd, sub):
    for pair in range(len(tiles) // 2):
        north, south = zip(*[encode_rows(t, sub) for t in tiles[2 * pair : 2 * pair + 2]])
        write_pair(out_a, pair, *[jnp.where(odd, n, s) for n, s in zip(north, south)])
        write_pair(out_b, pair, *[jnp.where(odd, s, n) for n, s in zip(north, south)])


def edge_columns(fields, tile, lane):
    edges = turn(tile(0), HALO)
    for f in range(1, fields):
        edges = jnp.where(lane // SLOT == f, turn(tile(f), f * SLOT + HALO), edges)
    return edges


def strip_tiles(fields, eofs, tile, lane):
    pair = eofs // 2
    west_out, east_out = [], []
    inner = lane & (SLOT - 1)
    at = lane & (SLOT // 2 - 1)
    for j in range(pair):
        first = edge_columns(fields, lambda f: tile(f * eofs + j), lane)
        second = edge_columns(fields, lambda f: tile(f * eofs + pair + j), lane)
        second = turn(second, SLOT // 2)
        west = jnp.where((inner >= HALO - 4) & (inner < 2 * HALO), first, second)
        high, low = split(west)
        west_out.append(jnp.where((at >= HALO - 4) & (at < HALO), turn(low, -4), high))
        east = jnp.where(inner < SLOT // 2, first, second)
        high, low = split(east)
        east_out.append(jnp.where(at < HALO, high, turn(low, 4)))
    edges = edge_columns(4, lambda k: tile(fields * eofs + k), lane)
    west = jnp.where((inner >= HALO) & (inner < 2 * HALO), edges, 0.0)
    east = jnp.where(inner < HALO, edges, 0.0)
    for cells, out in ((west, west_out), (east, east_out)):
        high, low = split(cells)
        out.append(high + turn(low, SLOT // 2))
    return west_out, east_out


def slice_kernel(members, fields, panels, *tiles):
    _, _, me = position()
    for s, block in enumerate(tiles):
        start = pl.multiple_of(lax.rem(me + s, len(tiles)) * LANES, LANES)
        for m in range(members):
            for f in range(fields):
                block[m, f] = panels[m, f, :, :, pl.ds(start, LANES)]


def own_strips_kernel(fields, eofs, members, own, eof_basis, *rest):
    tiles, (west, east, edges, basis) = rest[:-4], rest[-4:]
    lane = lane_grid()

    def tile(i):
        return own[pl.ds(i * SUB, SUB), :]

    for ref, packed in zip((west, east), strip_tiles(fields, eofs, tile, lane)):
        for pair in range(len(packed) // 2):
            write_pair(ref, pair, *packed[2 * pair : 2 * pair + 2])

    count = len(tiles)
    depth = tiles[0].shape[2] * SUB
    column = lax.broadcasted_iota(jnp.int32, (LANES, 2 * LANES), 0)
    target = lax.broadcasted_iota(jnp.int32, (LANES, 2 * LANES), 1)
    west_ok = (target < LANES) & (column < STEPS)
    east_ok = (target >= LANES) & (column >= LANES - STEPS)
    offset = jnp.where(
        west_ok,
        target - column,
        jnp.where(east_ok, target - LANES - column + LANES - STEPS, -1),
    )
    for s, block in enumerate(tiles):
        total = jnp.zeros((depth, 2 * LANES), jnp.float32)
        for m in range(members):
            for f in range(fields):
                pick = (offset == f * SLOT + m * SUB).astype(jnp.bfloat16)
                total += jnp.dot(
                    block[m, f].reshape(depth, LANES), pick, preferred_element_type=jnp.float32
                )
        total = total.astype(jnp.bfloat16)
        edges[s, 0] = total[:, :LANES]
        edges[s, 1] = total[:, LANES:]

    levels = eof_basis.shape[1]

    def grid(shape, dim):
        return lax.broadcasted_iota(jnp.int32, shape, dim)

    shape = (eofs * SUB, eofs)
    widen = (grid(shape, 0) // SUB == grid(shape, 1)).astype(jnp.bfloat16)
    shape = (levels, levels * SUB)
    spread = (grid(shape, 1) // SUB == grid(shape, 0)).astype(jnp.bfloat16)
    shape = (eofs * SUB, levels * SUB)
    same_row = grid(shape, 0) % SUB == grid(shape, 1) % SUB
    for f in range(fields):
        wide = lax.dot_general(
            widen, eof_basis[f], (((1,), (1,)), ((), ())), preferred_element_type=jnp.float32
        ).astype(jnp.bfloat16)
        wide = jnp.dot(wide, spread, preferred_element_type=jnp.float32)
        wide = jnp.where(same_row, wide, 0.0).astype(jnp.bfloat16)
        for h in range(count):
            basis[h, f] = wide[:, h * depth : (h + 1) * depth]


def pack_kernel(fields, eofs, from_a, from_b, west, east, *rest):
    panel_edges, (out_a, out_b, north, south) = rest[:-4], rest[-4:]
    ring_odd, odd, _ = position()
    lane = lane_grid()
    sub = lax.broadcasted_iota(jnp.int32, (SUB, LANES), 0)
    for pair in range((fields * eofs + 4) // 2):
        above, below = decode_rows(from_a, from_b, odd, sub, pair)
        at = pl.ds(pair * 2 * SUB, 2 * SUB)
        north[at, :] = jnp.concatenate(above, axis=0)
        south[at, :] = jnp.concatenate(below, axis=0)

    def put(pair, mine_west, mine_east):
        write_pair(out_a, pair, *[jnp.where(ring_odd, w, e) for w, e in zip(mine_west, mine_east)])
        write_pair(out_b, pair, *[jnp.where(ring_odd, e, w) for w, e in zip(mine_west, mine_east)])

    pairs = (eofs // 2 + 1) // 2
    for t, ref in ((0, north), (2, south)):
        tiles = strip_tiles(fields, eofs, lambda i: ref[pl.ds(i * SUB, SUB), :], lane)
        for j in range(pairs):
            put(t * pairs + j, tiles[0][2 * j : 2 * j + 2], tiles[1][2 * j : 2 * j + 2])
    for j in range(pairs):
        put(pairs + j, read_pair(west, j), read_pair(east, j))
    for edges in panel_edges[:1]:
        for j in range(edges.shape[2] // (2 * SUB)):
            put(3 * pairs + j, read_pair(edges.at[0, 0], j), read_pair(edges.at[0, 1], j))


def main_kernel(
    fields, eofs, own, north, south,
    adj, strip, coeff_main, coeff_strip, wide, first, second,
):
    lane = lane_grid()
    inner = lane & (SLOT - 1)
    total = fields * eofs

    def tile(t, i):
        return (north, own, south)[t][pl.ds(i * SUB, SUB), :]

    for k in range(4):
        for t in range(3):
            cells = tile(t, total + k)
            if k < 3:
                cells = time_step * cells
            at = pl.ds(t * SUB, SUB)
            coeff_main[k, at, :] = cells
            edges = edge_columns(fields, lambda f: cells, lane)
            west = (inner >= HALO) & (inner < 2 * HALO)
            coeff_strip[0, k, at, :] = jnp.where(west, edges, 0.0)
            coeff_strip[1, k, at, :] = jnp.where(inner < HALO, edges, 0.0)
    main_coefficients(coeff_main, wide)
    groups = total // SUB
    read, write = main_rows(own, north, south, adj)
    diffuse(read, write, lambda k, w: [wide[k, w]] * groups, groups, first, second, True)
    for t in range(3):
        for e in range(eofs):
            strip[t, pl.ds(e * SUB, SUB), :] = edge_columns(
                fields, lambda f: tile(t, f * eofs + e), lane
            )


def project_kernel(fields, eofs, members, basis, panel, *rest):
    arrived, proj = rest[:-1], rest[-1]
    _, _, me = position()
    blocks = (panel,) + arrived
    count = len(blocks)
    depth = panel.shape[2] * SUB
    for f in range(fields):
        total = None
        for s, block in enumerate(blocks):
            cells = jnp.concatenate(
                [block[m, f].reshape(depth, LANES) for m in range(members)], axis=1
            )
            part = jnp.dot(
                basis[lax.rem(me - s + count, count), f], cells, preferred_element_type=jnp.float32
            )
            total = part if total is None else total + part
        for m in range(members):
            proj[m, pl.ds(f * eofs * SUB, eofs * SUB), :] = total[:, m * LANES : (m + 1) * LANES]


def main_coefficients(coeff_main, wide):
    for k in range(4):
        for w in range(WINDOW):
            wide[k, w] = jnp.broadcast_to(coeff_main[k, pl.ds(w + 2, 1), :], (SUB, LANES))


def strip_coefficients(coeff_strip, wide_strip, eofs):
    sub = lax.broadcasted_iota(jnp.int32, (SUB, LANES), 0)
    for k in range(4):
        for w in range(WINDOW):
            west = jnp.broadcast_to(coeff_strip[0, k, pl.ds(w + 2, 1), :], (SUB, LANES))
            east = jnp.broadcast_to(coeff_strip[1, k, pl.ds(w + 2, 1), :], (SUB, LANES))
            wide_strip[k, w, pl.ds(0, SUB), :] = west
            wide_strip[k, w, pl.ds(SUB, SUB), :] = jnp.where(sub < eofs - SUB, west, east)
            wide_strip[k, w, pl.ds(2 * SUB, SUB), :] = east


def main_rows(own, north, south, out):
    def read(w, g):
        t, y = place(w)
        return (north, own, south)[t][pl.ds(g * SUB * SUB + y, SUB, stride=SUB), :]

    def write(w, g, cells):
        out[pl.ds(g * SUB * SUB + w - STEPS, SUB, stride=SUB), :] = cells

    return read, write


def strip_rows(strip, out, wide_strip):
    def read(w, g):
        t, y = place(w)
        return strip[t, pl.ds(g * SUB * SUB + y, SUB, stride=SUB), :]

    def write(w, g, cells):
        out[pl.ds(g * SUB * SUB + w - STEPS, SUB, stride=SUB), :] = cells

    def coeff(k, w):
        return [wide_strip[k, w, pl.ds(g * SUB, SUB), :] for g in range(3)]

    return read, write, coeff


def combine_kernel(fields, eofs, members, got_b, got_a, *rest):
    (
        basis, adj, proj, strip_own, coeff_own,
        out_a, out_b, combined, halo_out, coeff_strip,
        strip, wide_strip, adj_strip, panel_in, proj_strip, first, second,
    ) = rest[-17:]
    panel_parts = rest[:-17]
    ring_odd, odd, me = position()
    lane = lane_grid()
    sub = lax.broadcasted_iota(jnp.int32, (SUB, LANES), 0)
    inner = lane & (SLOT - 1)
    pair = eofs // 2

    def got(j):
        found = zip(read_pair(got_a, j), read_pair(got_b, j))
        sides = [(jnp.where(ring_odd, a, b), jnp.where(ring_odd, b, a)) for a, b in found]
        return zip(*sides)

    west_mask = inner < HALO
    east_mask = (inner >= HALO) & (inner < 2 * HALO)
    at16 = lane & (SLOT // 2 - 1)
    pairs = (pair + 1) // 2
    for t in range(3):
        west_tiles, east_tiles = [], []
        for j in range(pairs):
            west, east = got(t * pairs + j)
            west_tiles += west
            east_tiles += east
        for j in range(pair):
            west, east = west_tiles[j], east_tiles[j]
            west = west + jnp.where((at16 >= HALO - 4) & (at16 < HALO), turn(west, -4), 0.0)
            east = east + jnp.where(at16 >= HALO, turn(east, 4), 0.0)
            for half in range(2):
                e = half * pair + j
                mine = strip_own[t, pl.ds(e * SUB, SUB), :]
                if half:
                    west, east = turn(west, -(SLOT // 2)), turn(east, -(SLOT // 2))
                strip[t, pl.ds(e * SUB, SUB), :] = jnp.where(west_mask, west, mine)
                strip[t, pl.ds((eofs + e) * SUB, SUB), :] = jnp.where(east_mask, east, mine)
        strip[t, pl.ds(2 * eofs * SUB, 4 * SUB), :] = jnp.zeros((4 * SUB, LANES), jnp.float32)
        at = pl.ds(t * SUB, SUB)
        for side, (cells, mask) in enumerate(
            ((west_tiles[pair], west_mask), (east_tiles[pair], east_mask))
        ):
            cells = cells + turn(cells, -(SLOT // 2))
            turned = [cells] + [turn(cells, i * SLOT) for i in range(1, 4)]
            for k in range(4):
                mine = turned[-k % 4]
                for f in range(1, 4):
                    mine = jnp.where(lane // SLOT == f, turned[(f - k) % 4], mine)
                if k < 3:
                    mine = time_step * mine
                coeff_strip[side, k, at, :] = jnp.where(mask, mine, coeff_own[side, k, at, :])
    count, depth = basis.shape[0], basis.shape[3]
    if len(panel_parts) == 2:
        edges, far = panel_parts
        near_west, near_east, far = edges[1, 0], edges[1, 1], far[...]
        at = pl.ds(3 * pairs * 2 * SUB, depth)
        a, b = got_a[at, :], got_b[at, :]
        wests = [jnp.where(ring_odd, near_east, far), jnp.where(ring_odd, a, b)]
        easts = [jnp.where(ring_odd, far, near_west), jnp.where(ring_odd, b, a)]
    else:
        wests = [ref[...] for ref in panel_parts[:count]]
        easts = [ref[...] for ref in panel_parts[count:]]
    for s in range(count):
        panel_in[s] = jnp.concatenate([wests[s], easts[s]], axis=1)
    wide_lane = lax.broadcasted_iota(jnp.int32, (eofs * SUB, 2 * LANES), 1) & (LANES - 1)
    halo = jnp.zeros((eofs * SUB, 2 * LANES), jnp.float32)
    for f in range(fields):
        total = None
        for s in range(count):
            part = jnp.dot(
                basis[lax.rem(me + s, count), f], panel_in[s], preferred_element_type=jnp.float32
            )
            total = part if total is None else total + part
        halo = jnp.where(wide_lane // SLOT == f, total, halo)
    proj_strip[pl.ds(0, eofs * SUB), :] = halo[:, :LANES]
    proj_strip[pl.ds(eofs * SUB, eofs * SUB), :] = halo[:, LANES:]

    strip_coefficients(coeff_strip, wide_strip, eofs)
    read, write, coeff = strip_rows(strip, adj_strip, wide_strip)
    diffuse(read, write, coeff, 3, first, second, True)

    scores = [jnp.zeros((SUB, LANES), jnp.float32) for _ in range(members)]
    for e in range(eofs):
        edges = both_edges(eofs, adj_strip, e, inner)
        for f in range(fields):
            at = pl.ds((f * eofs + e) * SUB, SUB)
            cells = jnp.where(own_edge(lane), turn(edges, -f * SLOT - HALO), adj[at, :])
            for m in range(members):
                scores[m] = scores[m] + proj[m, at, :] * cells
    scores = [s / (members - 1) for s in scores]
    tiles = []
    for i in range(fields * eofs):
        at = pl.ds(i * SUB, SUB)
        total = proj[0, at, :] * scores[0]
        for m in range(1, members):
            total = total + proj[m, at, :] * scores[m]
        combined[at, :] = total
        tiles.append(total)

    slot = inner // SUB
    packed = [jnp.zeros((SUB, LANES), jnp.float32) for _ in range(2 * eofs // 4)]
    for side in range(2):
        total = jnp.zeros((SUB, LANES), jnp.float32)
        for e in range(eofs):
            at = pl.ds((side * eofs + e) * SUB, SUB)
            cells = adj_strip[at, :]
            start = HALO if side else STEPS
            spread = turn(cells, -start)
            for m in range(1, members):
                spread = jnp.where(slot == m, turn(cells, m * SUB - start), spread)
            total = total + proj_strip[at, :] * spread
        total = total + turn(total, SLOT)
        total = (total + turn(total, 2 * SLOT)) / (members - 1)
        for e in range(eofs):
            i = side * eofs + e
            cells = proj_strip[pl.ds(i * SUB, SUB), :] * total
            cells = cells + turn(cells, -2 * SUB)
            cells = cells + turn(cells, -SUB)
            packed[i // 4] = jnp.where(slot == i % 4, turn(cells, (i % 4) * SUB), packed[i // 4])
    for j, cells in enumerate(packed):
        halo_out[pl.ds(j * SUB, SUB), :] = cells
    tiles += packed
    if len(tiles) % 2:
        tiles.append(jnp.zeros((SUB, LANES), jnp.float32))
    put_rows(out_a, out_b, tiles, odd, sub)


def both_edges(eofs, strip, e, inner):
    west, east = strip[pl.ds(e * SUB, SUB), :], strip[pl.ds((eofs + e) * SUB, SUB), :]
    return jnp.where(inner < HALO, east, west)


def own_edge(lane):
    return (lane < STEPS) | (lane >= LANES - STEPS)


def fill_strip(fields, eofs, tile, packed, strip, t, lane):
    inner = lane & (SLOT - 1)
    west = (inner >= STEPS) & (inner < HALO)
    east = (inner >= HALO) & (inner < HALO + STEPS)
    for e in range(eofs):
        edges = edge_columns(fields, lambda f: tile(f * eofs + e), lane)
        for side, mask in enumerate((west, east)):
            i = side * eofs + e
            shift = (HALO if side else STEPS) - (i % 4) * SUB
            beyond = turn(packed[pl.ds(i // 4 * SUB, SUB), :], shift)
            strip[t, pl.ds(i * SUB, SUB), :] = jnp.where(mask, beyond, edges)
    strip[t, pl.ds(2 * eofs * SUB, 4 * SUB), :] = jnp.zeros((4 * SUB, LANES), jnp.float32)


def forward_coefficients(wide, wide_strip, groups):
    def coeff(k, w):
        strip = [wide_strip[k, w, pl.ds(g * SUB, SUB), :] for g in range(3)]
        return strip + [wide[k, w]] * groups

    return coeff


def before_forward_kernel(
    fields, eofs, own, halo, coeff_main, coeff_strip, wide, wide_strip, strip, kept, kept_flux
):
    lane = lane_grid()
    main_coefficients(coeff_main, wide)
    strip_coefficients(coeff_strip, wide_strip, eofs)
    fill_strip(fields, eofs, lambda i: own[pl.ds(i * SUB, SUB), :], halo, strip, 0, lane)

    def read(w, g):
        at = pl.ds((g if g < 3 else g - 3) * SUB * SUB + w - STEPS, SUB, stride=SUB)
        return strip[0, at, :] if g < 3 else own[at, :]

    groups = own.shape[0] // (SUB * SUB)
    coeff = forward_coefficients(wide, wide_strip, groups)
    diffuse_early(read, coeff, groups + 3, kept, kept_flux)


def forward_kernel(
    fields, eofs, own, from_a, from_b, wide, wide_strip, strip_own, kept, kept_flux,
    result, out, north, south, strip, strip_out, first, second, sems,
):
    _, odd, _ = position()
    lane = lane_grid()
    sub = lax.broadcasted_iota(jnp.int32, (SUB, LANES), 0)
    total = fields * eofs
    for pair in range(north.shape[0] // (2 * SUB)):
        above, below = decode_rows(from_a, from_b, odd, sub, pair)
        at = pl.ds(pair * 2 * SUB, 2 * SUB)
        north[at, :] = jnp.concatenate(above, axis=0)
        south[at, :] = jnp.concatenate(below, axis=0)
    for t, ref in ((0, north), (2, south)):
        packed = ref.at[pl.ds(total * SUB, 2 * eofs // 4 * SUB)]
        fill_strip(
            fields, eofs, lambda i: ref[pl.ds(i * SUB, SUB), :], packed, strip, t, lane
        )
    strip[1] = strip_own[0]
    groups = total // SUB
    read_main, write_main = main_rows(own, north, south, out)
    read_strip, write_strip, _ = strip_rows(strip, strip_out, wide_strip)

    def read(w, g):
        return read_strip(w, g) if g < 3 else read_main(w, g - 3)

    def write(w, g, cells):
        if g < 3:
            write_strip(w, g, cells)
        else:
            write_main(w, g - 3, cells)

    coeff = forward_coefficients(wide, wide_strip, groups)
    early = (kept, kept_flux)
    diffuse(read, write, coeff, groups + 3, first, second, False, early)
    edges = [both_edges(eofs, strip_out, e, lane & (SLOT - 1)) for e in range(eofs)]
    copies = []
    for f in range(fields):
        for e in range(eofs):
            at = pl.ds((f * eofs + e) * SUB, SUB)
            out[at, :] = jnp.where(own_edge(lane), turn(edges[e], -f * SLOT - HALO), out[at, :])
        part = pl.ds(f * eofs * SUB, eofs * SUB)
        copies.append(pltpu.make_async_copy(out.at[part], result.at[part], sems.at[f]))
        copies[-1].start()
    for copy in copies:
        copy.wait()


def call(kernel, args, outs, scratch=(), flops=1_000_000, out_space=pltpu.VMEM):
    whole = pl.BlockSpec(memory_space=pltpu.VMEM)
    moved = sum(a.size * a.dtype.itemsize for a in list(args) + list(outs))
    return pl.pallas_call(
        kernel,
        in_specs=[whole] * len(args),
        out_specs=[pl.BlockSpec(memory_space=out_space)] * len(outs),
        out_shape=list(outs),
        scratch_shapes=[pltpu.VMEM(*s) if isinstance(s, tuple) else s for s in scratch],
        compiler_params=pltpu.CompilerParams(vmem_limit_bytes=24 * 2**20),
        cost_estimate=pl.CostEstimate(flops=flops, bytes_accessed=moved, transcendentals=0),
    )(*args)


def panel_edges_apart(edges, count, me):
    groups = lax.axis_size("gx")
    wests, easts = [], []
    for s in range(count):
        for side, into in ((1, wests), (0, easts)):
            pairs = []
            for group in range(groups):
                for held in range(count):
                    tile = (held - s) % count
                    if side == 1:
                        to = group + (tile == 0)
                    else:
                        to = group - (tile == count - 1)
                    pairs.append((group * count + held, to % groups * count + tile))
            ahead = (-s - 1) if side == 1 else (1 - s)
            into.append(lax.ppermute(edges[ahead % count, side], RING, pairs))
    return wests + easts


def per_device(panels, eof_basis, control, coefficients):
    members, fields, depth, row_count, _ = panels.shape
    _, eofs, _, col_count = control.shape
    count = lax.axis_size("gz")
    me = lax.axis_index("gz")
    total = fields * eofs
    rows = total * row_count
    f32 = lambda *shape: jax.ShapeDtypeStruct(shape, jnp.float32)
    bf16 = lambda *shape: jax.ShapeDtypeStruct(shape, jnp.bfloat16)

    all_rows = rows + 4 * row_count
    own = jnp.concatenate(
        [control.reshape(rows, col_count), coefficients.reshape(4 * row_count, col_count)]
    )
    sent_a, sent_b = call(start_kernel, [own], [bf16(all_rows, col_count)] * 2)
    from_a, from_b = swap_a(sent_a, "gy"), swap_b(sent_b, "gy", False)
    strip_sent = (eofs // 2 + 1) * row_count
    tiles = call(
        functools.partial(slice_kernel, members, fields),
        [panels],
        [bf16(*panels.shape[:-1], col_count)] * count,
    )
    west, east, edges, basis = call(
        functools.partial(own_strips_kernel, fields, eofs, members),
        [own, eof_basis, *tiles],
        [bf16(strip_sent, col_count)] * 2
        + [
            bf16(count, 2, depth * row_count, col_count),
            bf16(count, fields, eofs * row_count, depth * row_count),
        ],
    )
    arrived = [
        lax.ppermute(tiles[s], "gz", [(i, (i + s) % count) for i in range(count)])
        for s in range(1, count)
    ]

    if count == 2:
        groups = lax.axis_size("gx")
        pairs = [(2 * g, (g + 1) % groups * 2) for g in range(groups)]
        pairs += [(2 * g + 1, (g - 1) % groups * 2 + 1) for g in range(groups)]
        far = lax.ppermute(jnp.where(me == 1, edges[1, 0], edges[1, 1]), RING, pairs)
        panel_sent, panel_parts = [edges], [edges, far]
    else:
        panel_sent, panel_parts = [], panel_edges_apart(edges, count, me)

    sent_a, sent_b, north, south = call(
        functools.partial(pack_kernel, fields, eofs),
        [from_a, from_b, west, east, *panel_sent],
        [bf16(3 * strip_sent + (count == 2) * depth * row_count, col_count)] * 2
        + [f32(rows + 4 * row_count, col_count)] * 2,
    )
    got_b = swap_b(sent_b, RING, True)
    got_a = swap_a(sent_a, RING)

    strip_rows = (2 * eofs + 4) * row_count
    main_scratch = [((WINDOW, total, LANES), jnp.float32)] * 2
    strip_scratch = [((WINDOW, 3 * SUB, LANES), jnp.float32)] * 2
    adj, strip, coeff_main, coeff_strip = call(
        functools.partial(main_kernel, fields, eofs),
        [own, north, south],
        [
            f32(rows, col_count),
            f32(3, eofs * row_count, col_count),
            f32(4, 3 * row_count, col_count),
            f32(2, 4, 3 * row_count, col_count),
        ],
        [((4, WINDOW, SUB, LANES), jnp.float32)] + main_scratch,
        flops=20_000_000,
    )
    (proj,) = call(
        functools.partial(project_kernel, fields, eofs, members),
        [basis, tiles[0], *arrived],
        [f32(members, rows, col_count)],
        flops=20_000_000,
    )
    packed = 2 * eofs // 4
    sent_a, sent_b, combined, halo, coeff_strip = call(
        functools.partial(combine_kernel, fields, eofs, members),
        [got_b, got_a, *panel_parts, basis, adj, proj, strip, coeff_strip],
        [bf16((total + packed + 1) // 2 * 2 * row_count, col_count)] * 2
        + [
            f32(rows, col_count),
            f32(packed * row_count, col_count),
            f32(2, 4, 3 * row_count, col_count),
        ],
        [
            ((3, strip_rows, LANES), jnp.float32),
            ((4, WINDOW, 3 * SUB, LANES), jnp.float32),
            ((strip_rows, LANES), jnp.float32),
            ((count, depth * row_count, 2 * LANES), jnp.bfloat16),
            ((2 * eofs * row_count, LANES), jnp.float32),
        ]
        + strip_scratch,
    )
    from_a, from_b = swap_a(sent_a, "gy"), swap_b(sent_b, "gy", False)
    early_steps = (SUB - 1) // 2
    early_count = sum(len(early_rows(step)[0]) for step in range(early_steps))
    wide, wide_strip, strip, kept, kept_flux = call(
        functools.partial(before_forward_kernel, fields, eofs),
        [combined, halo, coeff_main, coeff_strip],
        [
            f32(4, WINDOW, SUB, LANES),
            f32(4, WINDOW, 3 * SUB, LANES),
            f32(1, strip_rows, LANES),
            f32(early_count, total + 3 * SUB, LANES),
            f32(early_steps, total + 3 * SUB, LANES),
        ],
        flops=20_000_000,
    )
    (result,) = call(
        functools.partial(forward_kernel, fields, eofs),
        [combined, from_a, from_b, wide, wide_strip, strip, kept, kept_flux],
        [f32(rows, col_count)],
        [((rows, LANES), jnp.float32)]
        + [((sent_a.shape[0], LANES), jnp.float32)] * 2
        + [((3, strip_rows, LANES), jnp.float32), ((strip_rows, LANES), jnp.float32)]
        + [((WINDOW, total + 3 * SUB, LANES), jnp.float32)] * 2
        + [pltpu.SemaphoreType.DMA((fields,))],
        out_space=pltpu.HBM,
    )
    return result.reshape(control.shape)


def solution(mesh):
    in_specs = (
        P(None, None, "gz", "gy", "gx"),
        P(),
        P(None, None, "gy", ("gx", "gz")),
        P(None, "gy", ("gx", "gz")),
    )
    out_specs = P(None, None, "gy", ("gx", "gz"))
    return jax.shard_map(
        per_device, mesh=mesh, in_specs=in_specs, out_specs=out_specs, check_vma=False
    )
```

```python
import functools

import jax
import jax.numpy as jnp
from jax import lax
from jax.experimental import pallas as pl
from jax.experimental.pallas import tpu as pltpu
from jax.sharding import PartitionSpec as P

STEPS = 6
LANES = 128
SUB = 8
RING = ("gx", "gz")

time_step = 0.09

WINDOW = SUB + 2 * STEPS
HALO = 2 * STEPS
SLOT = 32


def turn(cells, shift):
    return pltpu.roll(cells, shift % LANES, 1)


def swap_a(values, axes):
    count = lax.axis_size(axes)
    return lax.ppermute(values, axes, [(i, i ^ 1) for i in range(count)])


def swap_b(values, axes, closed):
    count = lax.axis_size(axes)
    pairs = [(i, i + 1) for i in range(1, count - 1, 2)]
    if closed:
        pairs.append((count - 1, 0))
    return lax.ppermute(values, axes, pairs + [(j, i) for i, j in pairs])


def place(w):
    return (w + 2) // SUB, (w + 2) % SUB


def position():
    me = lax.axis_index("gz")
    ring = lax.axis_index("gx") * lax.axis_size("gz") + me
    return lax.rem(ring, 2) == 1, lax.rem(lax.axis_index("gy"), 2) == 1, me


def lane_grid():
    return lax.broadcasted_iota(jnp.int32, (SUB, LANES), 1)


def early_rows(step):
    rows = range(STEPS + 1 + step, STEPS + SUB - 1 - step)
    return rows, sum(len(early_rows(s)[0]) for s in range(step))


def diffuse_early(read, coeff, groups, kept, kept_flux):
    step = 0
    while len(early_rows(step)[0]):
        rows, base = early_rows(step)
        last_rows, last_base = early_rows(step - 1)

        def fetch(w):
            if step == 0:
                return [read(w, g) for g in range(groups)]
            at = last_base + w - last_rows[0]
            return [kept[at, pl.ds(g * SUB, SUB), :] for g in range(groups)]

        here, south = fetch(rows[0] - 1), None
        for w in range(rows[0] - 1, rows[-1] + 1):
            k = [coeff(i, w) for i in range(4)]
            north = fetch(w + 1)
            flux = []
            for g in range(groups):
                east_diff = turn(here[g], -1) - here[g]
                north_diff = north[g] - here[g]
                flux.append(k[1][g] * east_diff + k[2][g] * north_diff)
                if w in rows:
                    flux_east = k[0][g] * east_diff + k[1][g] * north_diff
                    div = (flux[g] - south[g]) + flux_east - turn(flux_east, 1)
                    kept[base + w - rows[0], pl.ds(g * SUB, SUB), :] = here[g] + k[3][g] * div
                if w == rows[-1]:
                    kept_flux[step, pl.ds(g * SUB, SUB), :] = flux[g]
            here, south = north, flux
        step += 1


def diffuse(read, write, coeff, groups, first, second, adjoint, early=None):
    state, spare = None, first
    made = range(0)
    for step in range(STEPS):
        low, high = step, WINDOW - 1 - step
        last, made = made, early_rows(step)[0] if early else range(0)

        def fetch(w):
            if state is None:
                return [read(w, g) for g in range(groups)]
            if w in last:
                at = early_rows(step - 1)[1] + w - last[0]
                return [early[0][at, pl.ds(g * SUB, SUB), :] for g in range(groups)]
            return [state[w, pl.ds(g * SUB, SUB), :] for g in range(groups)]

        here, seen, south = fetch(low), None, None
        for w in range(low, high):
            if w in made:
                if w == made[-1]:
                    here = fetch(w + 1)
                    south = [early[1][step, pl.ds(g * SUB, SUB), :] for g in range(groups)]
                continue
            k = [coeff(i, w) for i in range(4)]
            north = fetch(w + 1)
            if adjoint:
                if seen is None:
                    seen = [k[3][g] * here[g] for g in range(groups)]
                area = coeff(3, w + 1)
                seen_north = [area[g] * north[g] for g in range(groups)]
            else:
                seen, seen_north = here, north
            flux = []
            for g in range(groups):
                east_diff = turn(seen[g], -1) - seen[g]
                north_diff = seen_north[g] - seen[g]
                flux.append(k[1][g] * east_diff + k[2][g] * north_diff)
                if w > low:
                    flux_east = k[0][g] * east_diff + k[1][g] * north_diff
                    div = (flux[g] - south[g]) + flux_east - turn(flux_east, 1)
                    moved = here[g] + (div if adjoint else k[3][g] * div)
                    if step == STEPS - 1:
                        write(w, g, moved)
                    else:
                        spare[w, pl.ds(g * SUB, SUB), :] = moved
            here, seen, south = north, seen_north, flux
        state, spare = spare, (second if spare is first else first)


def read_pair(ref, pair):
    cells = ref[pl.ds(pair * 2 * SUB, 2 * SUB), :].astype(jnp.float32)
    return cells[:SUB], cells[SUB:]


def write_pair(ref, pair, first, second):
    cells = jnp.concatenate([first, second], axis=0).astype(jnp.bfloat16)
    ref[pl.ds(pair * 2 * SUB, 2 * SUB), :] = cells


def split(cells):
    high = cells.astype(jnp.bfloat16).astype(jnp.float32)
    return high, cells - high


def encode_rows(cells, sub):
    high, low = split(cells)
    edge = SUB - STEPS
    to_north = jnp.where(sub < STEPS, high, pltpu.roll(low, STEPS, 0))
    to_south = jnp.where(sub >= edge, high, pltpu.roll(low, edge, 0))
    return to_north, to_south


def decode_rows(from_a, from_b, odd, sub, pair):
    edge = SUB - STEPS
    north, south = [], []
    for a, b in zip(read_pair(from_a, pair), read_pair(from_b, pair)):
        above, below = jnp.where(odd, a, b), jnp.where(odd, b, a)
        north.append(above + jnp.where(sub >= STEPS, pltpu.roll(above, STEPS, 0), 0.0))
        south.append(below + jnp.where(sub < edge, pltpu.roll(below, edge, 0), 0.0))
    return north, south


def start_kernel(own, out_a, out_b):
    _, odd, _ = position()
    sub = lax.broadcasted_iota(jnp.int32, (SUB, LANES), 0)
    tiles = [own[pl.ds(i * SUB, SUB), :] for i in range(own.shape[0] // SUB)]
    put_rows(out_a, out_b, tiles, odd, sub)


def put_rows(out_a, out_b, tiles, odd, sub):
    for pair in range(len(tiles) // 2):
        north, south = zip(*[encode_rows(t, sub) for t in tiles[2 * pair : 2 * pair + 2]])
        write_pair(out_a, pair, *[jnp.where(odd, n, s) for n, s in zip(north, south)])
        write_pair(out_b, pair, *[jnp.where(odd, s, n) for n, s in zip(north, south)])


def edge_columns(fields, tile, lane):
    edges = turn(tile(0), HALO)
    for f in range(1, fields):
        edges = jnp.where(lane // SLOT == f, turn(tile(f), f * SLOT + HALO), edges)
    return edges


def strip_tiles(fields, eofs, tile, lane):
    pair = eofs // 2
    west_out, east_out = [], []
    inner = lane & (SLOT - 1)
    at = lane & (SLOT // 2 - 1)
    for j in range(pair):
        first = edge_columns(fields, lambda f: tile(f * eofs + j), lane)
        second = edge_columns(fields, lambda f: tile(f * eofs + pair + j), lane)
        second = turn(second, SLOT // 2)
        west = jnp.where((inner >= HALO - 4) & (inner < 2 * HALO), first, second)
        high, low = split(west)
        west_out.append(jnp.where((at >= HALO - 4) & (at < HALO), turn(low, -4), high))
        east = jnp.where(inner < SLOT // 2, first, second)
        high, low = split(east)
        east_out.append(jnp.where(at < HALO, high, turn(low, 4)))
    edges = edge_columns(4, lambda k: tile(fields * eofs + k), lane)
    west = jnp.where((inner >= HALO) & (inner < 2 * HALO), edges, 0.0)
    east = jnp.where(inner < HALO, edges, 0.0)
    for cells, out in ((west, west_out), (east, east_out)):
        high, low = split(cells)
        out.append(high + turn(low, SLOT // 2))
    return west_out, east_out


def slice_kernel(members, fields, panels, *tiles):
    _, _, me = position()
    for s, block in enumerate(tiles):
        start = pl.multiple_of(lax.rem(me + s, len(tiles)) * LANES, LANES)
        for m in range(members):
            for f in range(fields):
                block[m, f] = panels[m, f, :, :, pl.ds(start, LANES)]


def own_strips_kernel(fields, eofs, members, own, eof_basis, *rest):
    tiles, (west, east, edges, basis) = rest[:-4], rest[-4:]
    lane = lane_grid()

    def tile(i):
        return own[pl.ds(i * SUB, SUB), :]

    for ref, packed in zip((west, east), strip_tiles(fields, eofs, tile, lane)):
        for pair in range(len(packed) // 2):
            write_pair(ref, pair, *packed[2 * pair : 2 * pair + 2])

    count = len(tiles)
    depth = tiles[0].shape[2] * SUB
    column = lax.broadcasted_iota(jnp.int32, (LANES, 2 * LANES), 0)
    target = lax.broadcasted_iota(jnp.int32, (LANES, 2 * LANES), 1)
    west_ok = (target < LANES) & (column < STEPS)
    east_ok = (target >= LANES) & (column >= LANES - STEPS)
    offset = jnp.where(
        west_ok,
        target - column,
        jnp.where(east_ok, target - LANES - column + LANES - STEPS, -1),
    )
    for s, block in enumerate(tiles):
        total = jnp.zeros((depth, 2 * LANES), jnp.float32)
        for m in range(members):
            for f in range(fields):
                pick = (offset == f * SLOT + m * SUB).astype(jnp.bfloat16)
                total += jnp.dot(
                    block[m, f].reshape(depth, LANES), pick, preferred_element_type=jnp.float32
                )
        total = total.astype(jnp.bfloat16)
        edges[s, 0] = total[:, :LANES]
        edges[s, 1] = total[:, LANES:]

    levels = eof_basis.shape[1]

    def grid(shape, dim):
        return lax.broadcasted_iota(jnp.int32, shape, dim)

    shape = (eofs * SUB, eofs)
    widen = (grid(shape, 0) // SUB == grid(shape, 1)).astype(jnp.bfloat16)
    shape = (levels, levels * SUB)
    spread = (grid(shape, 1) // SUB == grid(shape, 0)).astype(jnp.bfloat16)
    shape = (eofs * SUB, levels * SUB)
    same_row = grid(shape, 0) % SUB == grid(shape, 1) % SUB
    for f in range(fields):
        wide = lax.dot_general(
            widen, eof_basis[f], (((1,), (1,)), ((), ())), preferred_element_type=jnp.float32
        ).astype(jnp.bfloat16)
        wide = jnp.dot(wide, spread, preferred_element_type=jnp.float32)
        wide = jnp.where(same_row, wide, 0.0).astype(jnp.bfloat16)
        for h in range(count):
            basis[h, f] = wide[:, h * depth : (h + 1) * depth]


def pack_kernel(fields, eofs, from_a, from_b, west, east, *rest):
    panel_edges, (out_a, out_b, north, south) = rest[:-4], rest[-4:]
    ring_odd, odd, _ = position()
    lane = lane_grid()
    sub = lax.broadcasted_iota(jnp.int32, (SUB, LANES), 0)
    for pair in range((fields * eofs + 4) // 2):
        above, below = decode_rows(from_a, from_b, odd, sub, pair)
        at = pl.ds(pair * 2 * SUB, 2 * SUB)
        north[at, :] = jnp.concatenate(above, axis=0)
        south[at, :] = jnp.concatenate(below, axis=0)

    def put(pair, mine_west, mine_east):
        write_pair(out_a, pair, *[jnp.where(ring_odd, w, e) for w, e in zip(mine_west, mine_east)])
        write_pair(out_b, pair, *[jnp.where(ring_odd, e, w) for w, e in zip(mine_west, mine_east)])

    pairs = (eofs // 2 + 1) // 2
    for t, ref in ((0, north), (2, south)):
        tiles = strip_tiles(fields, eofs, lambda i: ref[pl.ds(i * SUB, SUB), :], lane)
        for j in range(pairs):
            put(t * pairs + j, tiles[0][2 * j : 2 * j + 2], tiles[1][2 * j : 2 * j + 2])
    for j in range(pairs):
        put(pairs + j, read_pair(west, j), read_pair(east, j))
    for edges in panel_edges[:1]:
        for j in range(edges.shape[2] // (2 * SUB)):
            put(3 * pairs + j, read_pair(edges.at[0, 0], j), read_pair(edges.at[0, 1], j))


def main_kernel(
    fields, eofs, own, north, south,
    adj, strip, coeff_main, coeff_strip, wide, first, second,
):
    lane = lane_grid()
    inner = lane & (SLOT - 1)
    total = fields * eofs

    def tile(t, i):
        return (north, own, south)[t][pl.ds(i * SUB, SUB), :]

    for k in range(4):
        for t in range(3):
            cells = tile(t, total + k)
            if k < 3:
                cells = time_step * cells
            at = pl.ds(t * SUB, SUB)
            coeff_main[k, at, :] = cells
            edges = edge_columns(fields, lambda f: cells, lane)
            west = (inner >= HALO) & (inner < 2 * HALO)
            coeff_strip[0, k, at, :] = jnp.where(west, edges, 0.0)
            coeff_strip[1, k, at, :] = jnp.where(inner < HALO, edges, 0.0)
    main_coefficients(coeff_main, wide)
    groups = total // SUB
    read, write = main_rows(own, north, south, adj)
    diffuse(read, write, lambda k, w: [wide[k, w]] * groups, groups, first, second, True)
    for t in range(3):
        for e in range(eofs):
            strip[t, pl.ds(e * SUB, SUB), :] = edge_columns(
                fields, lambda f: tile(t, f * eofs + e), lane
            )


def project_kernel(fields, eofs, members, basis, panel, *rest):
    arrived, proj = rest[:-1], rest[-1]
    _, _, me = position()
    blocks = (panel,) + arrived
    count = len(blocks)
    depth = panel.shape[2] * SUB
    for f in range(fields):
        total = None
        for s, block in enumerate(blocks):
            cells = jnp.concatenate(
                [block[m, f].reshape(depth, LANES) for m in range(members)], axis=1
            )
            part = jnp.dot(
                basis[lax.rem(me - s + count, count), f], cells, preferred_element_type=jnp.float32
            )
            total = part if total is None else total + part
        for m in range(members):
            proj[m, pl.ds(f * eofs * SUB, eofs * SUB), :] = total[:, m * LANES : (m + 1) * LANES]


def main_coefficients(coeff_main, wide):
    for k in range(4):
        for w in range(WINDOW):
            wide[k, w] = jnp.broadcast_to(coeff_main[k, pl.ds(w + 2, 1), :], (SUB, LANES))


def strip_coefficients(coeff_strip, wide_strip, eofs):
    sub = lax.broadcasted_iota(jnp.int32, (SUB, LANES), 0)
    for k in range(4):
        for w in range(WINDOW):
            west = jnp.broadcast_to(coeff_strip[0, k, pl.ds(w + 2, 1), :], (SUB, LANES))
            east = jnp.broadcast_to(coeff_strip[1, k, pl.ds(w + 2, 1), :], (SUB, LANES))
            wide_strip[k, w, pl.ds(0, SUB), :] = west
            wide_strip[k, w, pl.ds(SUB, SUB), :] = jnp.where(sub < eofs - SUB, west, east)
            wide_strip[k, w, pl.ds(2 * SUB, SUB), :] = east


def main_rows(own, north, south, out):
    def read(w, g):
        t, y = place(w)
        return (north, own, south)[t][pl.ds(g * SUB * SUB + y, SUB, stride=SUB), :]

    def write(w, g, cells):
        out[pl.ds(g * SUB * SUB + w - STEPS, SUB, stride=SUB), :] = cells

    return read, write


def strip_rows(strip, out, wide_strip):
    def read(w, g):
        t, y = place(w)
        return strip[t, pl.ds(g * SUB * SUB + y, SUB, stride=SUB), :]

    def write(w, g, cells):
        out[pl.ds(g * SUB * SUB + w - STEPS, SUB, stride=SUB), :] = cells

    def coeff(k, w):
        return [wide_strip[k, w, pl.ds(g * SUB, SUB), :] for g in range(3)]

    return read, write, coeff


def combine_kernel(fields, eofs, members, got_b, got_a, *rest):
    (
        basis, adj, proj, strip_own, coeff_own,
        out_a, out_b, combined, halo_out, coeff_strip,
        strip, wide_strip, adj_strip, panel_in, proj_strip, first, second,
    ) = rest[-17:]
    panel_parts = rest[:-17]
    ring_odd, odd, me = position()
    lane = lane_grid()
    sub = lax.broadcasted_iota(jnp.int32, (SUB, LANES), 0)
    inner = lane & (SLOT - 1)
    pair = eofs // 2

    def got(j):
        found = zip(read_pair(got_a, j), read_pair(got_b, j))
        sides = [(jnp.where(ring_odd, a, b), jnp.where(ring_odd, b, a)) for a, b in found]
        return zip(*sides)

    west_mask = inner < HALO
    east_mask = (inner >= HALO) & (inner < 2 * HALO)
    at16 = lane & (SLOT // 2 - 1)
    pairs = (pair + 1) // 2
    for t in range(3):
        west_tiles, east_tiles = [], []
        for j in range(pairs):
            west, east = got(t * pairs + j)
            west_tiles += west
            east_tiles += east
        for j in range(pair):
            west, east = west_tiles[j], east_tiles[j]
            west = west + jnp.where((at16 >= HALO - 4) & (at16 < HALO), turn(west, -4), 0.0)
            east = east + jnp.where(at16 >= HALO, turn(east, 4), 0.0)
            for half in range(2):
                e = half * pair + j
                mine = strip_own[t, pl.ds(e * SUB, SUB), :]
                if half:
                    west, east = turn(west, -(SLOT // 2)), turn(east, -(SLOT // 2))
                strip[t, pl.ds(e * SUB, SUB), :] = jnp.where(west_mask, west, mine)
                strip[t, pl.ds((eofs + e) * SUB, SUB), :] = jnp.where(east_mask, east, mine)
        strip[t, pl.ds(2 * eofs * SUB, 4 * SUB), :] = jnp.zeros((4 * SUB, LANES), jnp.float32)
        at = pl.ds(t * SUB, SUB)
        for side, (cells, mask) in enumerate(
            ((west_tiles[pair], west_mask), (east_tiles[pair], east_mask))
        ):
            cells = cells + turn(cells, -(SLOT // 2))
            turned = [cells] + [turn(cells, i * SLOT) for i in range(1, 4)]
            for k in range(4):
                mine = turned[-k % 4]
                for f in range(1, 4):
                    mine = jnp.where(lane // SLOT == f, turned[(f - k) % 4], mine)
                if k < 3:
                    mine = time_step * mine
                coeff_strip[side, k, at, :] = jnp.where(mask, mine, coeff_own[side, k, at, :])
    count, depth = basis.shape[0], basis.shape[3]
    if len(panel_parts) == 2:
        edges, far = panel_parts
        near_west, near_east, far = edges[1, 0], edges[1, 1], far[...]
        at = pl.ds(3 * pairs * 2 * SUB, depth)
        a, b = got_a[at, :], got_b[at, :]
        wests = [jnp.where(ring_odd, near_east, far), jnp.where(ring_odd, a, b)]
        easts = [jnp.where(ring_odd, far, near_west), jnp.where(ring_odd, b, a)]
    else:
        wests = [ref[...] for ref in panel_parts[:count]]
        easts = [ref[...] for ref in panel_parts[count:]]
    for s in range(count):
        panel_in[s] = jnp.concatenate([wests[s], easts[s]], axis=1)
    wide_lane = lax.broadcasted_iota(jnp.int32, (eofs * SUB, 2 * LANES), 1) & (LANES - 1)
    halo = jnp.zeros((eofs * SUB, 2 * LANES), jnp.float32)
    for f in range(fields):
        total = None
        for s in range(count):
            part = jnp.dot(
                basis[lax.rem(me + s, count), f], panel_in[s], preferred_element_type=jnp.float32
            )
            total = part if total is None else total + part
        halo = jnp.where(wide_lane // SLOT == f, total, halo)
    proj_strip[pl.ds(0, eofs * SUB), :] = halo[:, :LANES]
    proj_strip[pl.ds(eofs * SUB, eofs * SUB), :] = halo[:, LANES:]

    strip_coefficients(coeff_strip, wide_strip, eofs)
    read, write, coeff = strip_rows(strip, adj_strip, wide_strip)
    diffuse(read, write, coeff, 3, first, second, True)

    scores = [[jnp.zeros((SUB, LANES), jnp.float32)] * 2 for _ in range(members)]
    for e in range(eofs):
        edges = both_edges(eofs, adj_strip, e, inner)
        for f in range(fields):
            at = pl.ds((f * eofs + e) * SUB, SUB)
            cells = jnp.where(own_edge(lane), turn(edges, -f * SLOT - HALO), adj[at, :])
            for m in range(members):
                scores[m][f % 2] = scores[m][f % 2] + proj[m, at, :] * cells
    scores = [(even + odd_sum) / (members - 1) for even, odd_sum in scores]
    tiles = []
    for i in range(fields * eofs):
        at = pl.ds(i * SUB, SUB)
        total = proj[0, at, :] * scores[0]
        for m in range(1, members):
            total = total + proj[m, at, :] * scores[m]
        combined[at, :] = total
        tiles.append(total)

    slot = inner // SUB
    packed = [jnp.zeros((SUB, LANES), jnp.float32) for _ in range(2 * eofs // 4)]
    for side in range(2):
        total = jnp.zeros((SUB, LANES), jnp.float32)
        for e in range(eofs):
            at = pl.ds((side * eofs + e) * SUB, SUB)
            cells = adj_strip[at, :]
            start = HALO if side else STEPS
            spread = turn(cells, -start)
            for m in range(1, members):
                spread = jnp.where(slot == m, turn(cells, m * SUB - start), spread)
            total = total + proj_strip[at, :] * spread
        total = total + turn(total, SLOT)
        total = (total + turn(total, 2 * SLOT)) / (members - 1)
        for e in range(eofs):
            i = side * eofs + e
            cells = proj_strip[pl.ds(i * SUB, SUB), :] * total
            cells = cells + turn(cells, -2 * SUB)
            cells = cells + turn(cells, -SUB)
            packed[i // 4] = jnp.where(slot == i % 4, turn(cells, (i % 4) * SUB), packed[i // 4])
    for j, cells in enumerate(packed):
        halo_out[pl.ds(j * SUB, SUB), :] = cells
    tiles += packed
    if len(tiles) % 2:
        tiles.append(jnp.zeros((SUB, LANES), jnp.float32))
    put_rows(out_a, out_b, tiles, odd, sub)


def both_edges(eofs, strip, e, inner):
    west, east = strip[pl.ds(e * SUB, SUB), :], strip[pl.ds((eofs + e) * SUB, SUB), :]
    return jnp.where(inner < HALO, east, west)


def own_edge(lane):
    return (lane < STEPS) | (lane >= LANES - STEPS)


def fill_strip(fields, eofs, tile, packed, strip, t, lane):
    inner = lane & (SLOT - 1)
    west = (inner >= STEPS) & (inner < HALO)
    east = (inner >= HALO) & (inner < HALO + STEPS)
    for e in range(eofs):
        edges = edge_columns(fields, lambda f: tile(f * eofs + e), lane)
        for side, mask in enumerate((west, east)):
            i = side * eofs + e
            shift = (HALO if side else STEPS) - (i % 4) * SUB
            beyond = turn(packed[pl.ds(i // 4 * SUB, SUB), :], shift)
            strip[t, pl.ds(i * SUB, SUB), :] = jnp.where(mask, beyond, edges)
    strip[t, pl.ds(2 * eofs * SUB, 4 * SUB), :] = jnp.zeros((4 * SUB, LANES), jnp.float32)


def forward_coefficients(wide, wide_strip, groups):
    def coeff(k, w):
        strip = [wide_strip[k, w, pl.ds(g * SUB, SUB), :] for g in range(3)]
        return strip + [wide[k, w]] * groups

    return coeff


def before_forward_kernel(
    fields, eofs, own, halo, coeff_main, coeff_strip, wide, wide_strip, strip, kept, kept_flux
):
    lane = lane_grid()
    main_coefficients(coeff_main, wide)
    strip_coefficients(coeff_strip, wide_strip, eofs)
    fill_strip(fields, eofs, lambda i: own[pl.ds(i * SUB, SUB), :], halo, strip, 0, lane)

    def read(w, g):
        at = pl.ds((g if g < 3 else g - 3) * SUB * SUB + w - STEPS, SUB, stride=SUB)
        return strip[0, at, :] if g < 3 else own[at, :]

    groups = own.shape[0] // (SUB * SUB)
    coeff = forward_coefficients(wide, wide_strip, groups)
    diffuse_early(read, coeff, groups + 3, kept, kept_flux)


def forward_kernel(
    fields, eofs, own, from_a, from_b, wide, wide_strip, strip_own, kept, kept_flux,
    result, out, north, south, strip, strip_out, first, second, sems,
):
    _, odd, _ = position()
    lane = lane_grid()
    sub = lax.broadcasted_iota(jnp.int32, (SUB, LANES), 0)
    total = fields * eofs
    for pair in range(north.shape[0] // (2 * SUB)):
        above, below = decode_rows(from_a, from_b, odd, sub, pair)
        at = pl.ds(pair * 2 * SUB, 2 * SUB)
        north[at, :] = jnp.concatenate(above, axis=0)
        south[at, :] = jnp.concatenate(below, axis=0)
    for t, ref in ((0, north), (2, south)):
        packed = ref.at[pl.ds(total * SUB, 2 * eofs // 4 * SUB)]
        fill_strip(
            fields, eofs, lambda i: ref[pl.ds(i * SUB, SUB), :], packed, strip, t, lane
        )
    strip[1] = strip_own[0]
    groups = total // SUB
    read_main, write_main = main_rows(own, north, south, out)
    read_strip, write_strip, _ = strip_rows(strip, strip_out, wide_strip)

    def read(w, g):
        return read_strip(w, g) if g < 3 else read_main(w, g - 3)

    def write(w, g, cells):
        if g < 3:
            write_strip(w, g, cells)
        else:
            write_main(w, g - 3, cells)

    coeff = forward_coefficients(wide, wide_strip, groups)
    early = (kept, kept_flux)
    diffuse(read, write, coeff, groups + 3, first, second, False, early)
    edges = [both_edges(eofs, strip_out, e, lane & (SLOT - 1)) for e in range(eofs)]
    copies = []
    for f in range(fields):
        for e in range(eofs):
            at = pl.ds((f * eofs + e) * SUB, SUB)
            out[at, :] = jnp.where(own_edge(lane), turn(edges[e], -f * SLOT - HALO), out[at, :])
        part = pl.ds(f * eofs * SUB, eofs * SUB)
        copies.append(pltpu.make_async_copy(out.at[part], result.at[part], sems.at[f]))
        copies[-1].start()
    for copy in copies:
        copy.wait()


def call(kernel, args, outs, scratch=(), flops=1_000_000, out_space=pltpu.VMEM):
    whole = pl.BlockSpec(memory_space=pltpu.VMEM)
    moved = sum(a.size * a.dtype.itemsize for a in list(args) + list(outs))
    return pl.pallas_call(
        kernel,
        in_specs=[whole] * len(args),
        out_specs=[pl.BlockSpec(memory_space=out_space)] * len(outs),
        out_shape=list(outs),
        scratch_shapes=[pltpu.VMEM(*s) if isinstance(s, tuple) else s for s in scratch],
        compiler_params=pltpu.CompilerParams(vmem_limit_bytes=24 * 2**20),
        cost_estimate=pl.CostEstimate(flops=flops, bytes_accessed=moved, transcendentals=0),
    )(*args)


def panel_edges_apart(edges, count, me):
    groups = lax.axis_size("gx")
    wests, easts = [], []
    for s in range(count):
        for side, into in ((1, wests), (0, easts)):
            pairs = []
            for group in range(groups):
                for held in range(count):
                    tile = (held - s) % count
                    if side == 1:
                        to = group + (tile == 0)
                    else:
                        to = group - (tile == count - 1)
                    pairs.append((group * count + held, to % groups * count + tile))
            ahead = (-s - 1) if side == 1 else (1 - s)
            into.append(lax.ppermute(edges[ahead % count, side], RING, pairs))
    return wests + easts


def per_device(panels, eof_basis, control, coefficients):
    members, fields, depth, row_count, _ = panels.shape
    _, eofs, _, col_count = control.shape
    count = lax.axis_size("gz")
    me = lax.axis_index("gz")
    total = fields * eofs
    rows = total * row_count
    f32 = lambda *shape: jax.ShapeDtypeStruct(shape, jnp.float32)
    bf16 = lambda *shape: jax.ShapeDtypeStruct(shape, jnp.bfloat16)

    all_rows = rows + 4 * row_count
    own = jnp.concatenate(
        [control.reshape(rows, col_count), coefficients.reshape(4 * row_count, col_count)]
    )
    sent_a, sent_b = call(start_kernel, [own], [bf16(all_rows, col_count)] * 2)
    from_a, from_b = swap_a(sent_a, "gy"), swap_b(sent_b, "gy", False)
    strip_sent = (eofs // 2 + 1) * row_count
    tiles = call(
        functools.partial(slice_kernel, members, fields),
        [panels],
        [bf16(*panels.shape[:-1], col_count)] * count,
    )
    west, east, edges, basis = call(
        functools.partial(own_strips_kernel, fields, eofs, members),
        [own, eof_basis, *tiles],
        [bf16(strip_sent, col_count)] * 2
        + [
            bf16(count, 2, depth * row_count, col_count),
            bf16(count, fields, eofs * row_count, depth * row_count),
        ],
    )
    arrived = [
        lax.ppermute(tiles[s], "gz", [(i, (i + s) % count) for i in range(count)])
        for s in range(1, count)
    ]

    if count == 2:
        groups = lax.axis_size("gx")
        pairs = [(2 * g, (g + 1) % groups * 2) for g in range(groups)]
        pairs += [(2 * g + 1, (g - 1) % groups * 2 + 1) for g in range(groups)]
        far = lax.ppermute(jnp.where(me == 1, edges[1, 0], edges[1, 1]), RING, pairs)
        panel_sent, panel_parts = [edges], [edges, far]
    else:
        panel_sent, panel_parts = [], panel_edges_apart(edges, count, me)

    sent_a, sent_b, north, south = call(
        functools.partial(pack_kernel, fields, eofs),
        [from_a, from_b, west, east, *panel_sent],
        [bf16(3 * strip_sent + (count == 2) * depth * row_count, col_count)] * 2
        + [f32(rows + 4 * row_count, col_count)] * 2,
    )
    got_b = swap_b(sent_b, RING, True)
    got_a = swap_a(sent_a, RING)

    strip_rows = (2 * eofs + 4) * row_count
    main_scratch = [((WINDOW, total, LANES), jnp.float32)] * 2
    strip_scratch = [((WINDOW, 3 * SUB, LANES), jnp.float32)] * 2
    adj, strip, coeff_main, coeff_strip = call(
        functools.partial(main_kernel, fields, eofs),
        [own, north, south],
        [
            f32(rows, col_count),
            f32(3, eofs * row_count, col_count),
            f32(4, 3 * row_count, col_count),
            f32(2, 4, 3 * row_count, col_count),
        ],
        [((4, WINDOW, SUB, LANES), jnp.float32)] + main_scratch,
        flops=20_000_000,
    )
    (proj,) = call(
        functools.partial(project_kernel, fields, eofs, members),
        [basis, tiles[0], *arrived],
        [f32(members, rows, col_count)],
        flops=20_000_000,
    )
    packed = 2 * eofs // 4
    sent_a, sent_b, combined, halo, coeff_strip = call(
        functools.partial(combine_kernel, fields, eofs, members),
        [got_b, got_a, *panel_parts, basis, adj, proj, strip, coeff_strip],
        [bf16((total + packed + 1) // 2 * 2 * row_count, col_count)] * 2
        + [
            f32(rows, col_count),
            f32(packed * row_count, col_count),
            f32(2, 4, 3 * row_count, col_count),
        ],
        [
            ((3, strip_rows, LANES), jnp.float32),
            ((4, WINDOW, 3 * SUB, LANES), jnp.float32),
            ((strip_rows, LANES), jnp.float32),
            ((count, depth * row_count, 2 * LANES), jnp.bfloat16),
            ((2 * eofs * row_count, LANES), jnp.float32),
        ]
        + strip_scratch,
    )
    from_a, from_b = swap_a(sent_a, "gy"), swap_b(sent_b, "gy", False)
    early_steps = (SUB - 1) // 2
    early_count = sum(len(early_rows(step)[0]) for step in range(early_steps))
    wide, wide_strip, strip, kept, kept_flux = call(
        functools.partial(before_forward_kernel, fields, eofs),
        [combined, halo, coeff_main, coeff_strip],
        [
            f32(4, WINDOW, SUB, LANES),
            f32(4, WINDOW, 3 * SUB, LANES),
            f32(1, strip_rows, LANES),
            f32(early_count, total + 3 * SUB, LANES),
            f32(early_steps, total + 3 * SUB, LANES),
        ],
        flops=20_000_000,
    )
    (result,) = call(
        functools.partial(forward_kernel, fields, eofs),
        [combined, from_a, from_b, wide, wide_strip, strip, kept, kept_flux],
        [f32(rows, col_count)],
        [((rows, LANES), jnp.float32)]
        + [((sent_a.shape[0], LANES), jnp.float32)] * 2
        + [((3, strip_rows, LANES), jnp.float32), ((strip_rows, LANES), jnp.float32)]
        + [((WINDOW, total + 3 * SUB, LANES), jnp.float32)] * 2
        + [pltpu.SemaphoreType.DMA((fields,))],
        out_space=pltpu.HBM,
    )
    return result.reshape(control.shape)


def solution(mesh):
    in_specs = (
        P(None, None, "gz", "gy", "gx"),
        P(),
        P(None, None, "gy", ("gx", "gz")),
        P(None, "gy", ("gx", "gz")),
    )
    out_specs = P(None, None, "gy", ("gx", "gz"))
    return jax.shard_map(
        per_device, mesh=mesh, in_specs=in_specs, out_specs=out_specs, check_vma=False
    )
```
